512 devices in a mesh: expert: 16 (over y_hi, z), tensor: 32 (over y_lo, x, core).
Axes of the slice: x: 4, y: 8 (y_hi: 2, y_lo: 4; y = y_hi * 4 + y_lo), z: 8, core: 2. Of those that a mesh axis runs over, the one named last changes fastest.
Arguments:
- residual: bfloat16 [2048, 2048], P('expert', 'tensor'), may hold values from -6 to 6
- heads_out: bfloat16 [2048, 2048], P('expert', 'tensor'), may hold values from -6 to 6
- out_weight: bfloat16 [2048, 2048], P(None, 'tensor'), may hold values from -0.125 to 0.125
- norm_gain: float32 [2048], P('tensor'), may hold values from 0.5 to 1.5
- up_weight: bfloat16 [32, 2048, 8192], P('expert', None, 'tensor'), may hold values from -0.125 to 0.125
- down_weight: bfloat16 [32, 8192, 2048], P('expert', 'tensor'), may hold values from -0.0625 to 0.0625
- routes: int32 [2048, 2], P('expert'), may hold values from 0 to 31, all different within a row; in each aligned block of 128 rows (0 to 127, 128 to 255, ...) at most 9 rows name the same one
- gate_values: float32 [2048, 2], P('expert'), may hold values from 0.2 to 1
- cotangent: bfloat16 [2048, 2048], P('expert', 'tensor'), may hold values from -6 to 6
Outputs:
- result: bfloat16 [2048, 2048], P('expert', 'tensor')
- grad_residual: bfloat16 [2048, 2048], P('expert', 'tensor')
- grad_heads: bfloat16 [2048, 2048], P('expert', 'tensor')
- grad_out_weight: bfloat16 [2048, 2048], P(None, 'tensor')
The draws below stay inside these ranges and needn't reach their ends.
Inputs may be any that keep to these rules, and one draw needn't show every extreme that they name: `routes`: each row names two different experts. Among the 128 rows of one index of expert (aligned blocks), no expert is named by more than 9 rows, a bound that some block reaches.
All inputs are finite; a program needn't handle non-finite values.
Results may differ from the reference program's by a relative error of at most 0.019.
Values may be sent and summed in bfloat16 or wider, within the bound.
No kernel may reach another device: no remote copies, remote signals or barrier semaphores. Data moves between devices by JAX's collectives and lax.ppermute only.
A program may use at most 128 MiB of HBM per device.

```python
import math
import jax
import jax.numpy as jnp
import numpy as np
from jax import lax

MODEL_WIDTH = 2048
FF = 8192
TOK_DEV = 128
EXPERTS = 32
CAP = 9
PATCH_TOKENS = 2048
N_EXPERT = 16
N_TENSOR = 32


def level_of(rng, shape, pieces, smallest, high):
    gain = 1.0
    for axis_at, shards_of in pieces:
        steps = jax.random.uniform(jax.random.fold_in(jax.random.fold_in(rng, 6), axis_at), (shards_of,), jnp.float32, smallest / len(pieces), high / len(pieces))
        gain = gain * jnp.repeat(jnp.exp(steps), shape[axis_at] // shards_of).reshape((-1,) + (1,) * (len(shape) - 1 - axis_at))
    return gain


def routed_block(key, own, number, rows, amount, top, bound, lean):
    order = jax.random.permutation(key, amount)
    crowded, common = portions_of(amount, rows * top, bound, lean, True), portions_of(amount, rows * top, bound, lean, False)
    places = jnp.arange(amount)

    def named(lengths, turn):
        used = int((lengths > 0).sum())
        fixed = max(1, used // 4)
        passed = fixed + (places - fixed + turn * (used - fixed)) % max(1, amount - fixed)
        return jnp.zeros((amount,), jnp.int32).at[order[jnp.where(places < fixed, places, passed)]].set(jnp.asarray(lengths, jnp.int32))

    lengths = jnp.where(number % 4 == 0, named(crowded, number // 4), named(common, number - number // 4 - 1))
    mixed = jax.random.permutation(jax.random.fold_in(own, 3), amount)
    giver, taker = mixed[0:amount // 2 * 2:2], mixed[1:amount // 2 * 2:2]
    slack = jnp.minimum(lengths[giver] - 1, bound - lengths[taker]) // 2
    slack = jnp.where((giver == order[0]) | (taker == order[0]) | (lengths[taker] == 0), 0, jnp.maximum(slack, 0))
    passed = jax.random.randint(jax.random.fold_in(own, 4), (amount // 2,), 0, 1 << 20) % (slack + 1)
    lengths = lengths.at[giver].add(-passed).at[taker].add(passed)
    labels = jnp.searchsorted(jnp.cumsum(lengths), jnp.arange(rows * top), side="right").astype(jnp.int32)
    grid = labels.reshape(top, rows).T
    grid = grid[jax.random.permutation(jax.random.fold_in(own, 1), rows)]
    turn = jax.random.randint(jax.random.fold_in(own, 2), (rows, 1), 0, top)
    return jnp.take_along_axis(grid, (jnp.arange(top)[None, :] + turn) % top, axis=1)


def portions_of(amount, total, most, skew, full):
    portions = [(1 << 20) // math.isqrt(grade ** skew) + 1 for grade in range(1, amount + 1)]
    largest = most if full else min(most, max(-(-total // amount), total * portions[0] // sum(portions)))
    least = 1 if total - largest >= amount - 1 else 0
    given, surplus = [largest] + [least] * (amount - 1), total - largest - least * (amount - 1)
    while surplus > 0:
        movable = [i for i in range(1, amount) if given[i] < largest] or [i for i in range(1, amount) if given[i] < most]
        pool, remaining = sum([portions[i] for i in movable]), surplus
        for i in movable:
            extra = min(most - given[i], max(1, remaining * portions[i] // pool), surplus)
            given[i] = given[i] + extra
            surplus = surplus - extra
    return np.array(given)


def gaussian(stream_key, dims, width, bound, cuts=(), kind=jnp.bfloat16):
    values = jax.random.normal(stream_key, dims, jnp.float32) * width
    if len(cuts) > 0:
        values = level_of(stream_key, dims, cuts, -0.22, 0.18) * values
    return jnp.clip(values, min=-bound, max=bound).astype(kind)


def setup_inputs(seed: int = 0) -> dict:
    arg_keys = jax.random.split(jax.random.key(seed), 10)
    residual = gaussian(arg_keys[0], (PATCH_TOKENS, MODEL_WIDTH), 1.0, 6.0, ((0, 16), (1, 32)))
    heads_out = gaussian(arg_keys[1], (PATCH_TOKENS, MODEL_WIDTH), 1.0, 6.0, ((0, 16), (1, 32)))
    out_weight = gaussian(arg_keys[2], (MODEL_WIDTH, MODEL_WIDTH), MODEL_WIDTH ** -0.5, 0.125, ((1, 32),))
    norm_gain = jnp.clip(1.0 + 0.1 * jax.random.normal(arg_keys[3], (MODEL_WIDTH,), jnp.float32), 0.5, 1.5)
    up_weight = gaussian(arg_keys[4], (EXPERTS, MODEL_WIDTH, FF), MODEL_WIDTH ** -0.5, 0.125, ((0, 16), (2, 32)))
    down_weight = gaussian(arg_keys[5], (EXPERTS, FF, MODEL_WIDTH), FF ** -0.5, 0.0625, ((0, 16), (1, 32)))
    routes_keys = jax.random.split(jax.random.fold_in(arg_keys[6], 1), PATCH_TOKENS // TOK_DEV)
    routes_turns = jax.random.permutation(jax.random.fold_in(arg_keys[6], 3), PATCH_TOKENS // TOK_DEV)
    routes = jax.vmap(lambda own, number: routed_block(jax.random.fold_in(arg_keys[6], 2), own, number, TOK_DEV, EXPERTS, 2, CAP, 3))(routes_keys, routes_turns).reshape((PATCH_TOKENS, 2))
    gate_values = jnp.clip(0.2 + 0.8 * jax.random.uniform(arg_keys[7], (PATCH_TOKENS, 2), jnp.float32) ** level_of(arg_keys[7], (PATCH_TOKENS, 2), ((0, 16),), -0.2, 0.2), 0.2, 1.0)
    cotangent = gaussian(arg_keys[8], (PATCH_TOKENS, MODEL_WIDTH), 1.0, 6.0, ((0, 16), (1, 32)))
    return {"residual": residual, "heads_out": heads_out, "out_weight": out_weight, "norm_gain": norm_gain, "up_weight": up_weight, "down_weight": down_weight, "routes": routes, "gate_values": gate_values, "cotangent": cotangent}


def activate(value):
    return jax.nn.gelu(value, approximate=True)

def route_tables(routes, gate_values, experts, capacity):
    rows_here = routes.shape[0]
    flat_ids = routes.reshape(-1)
    onehot = (flat_ids[:, None] == jnp.arange(experts, dtype=jnp.int32)[None, :]).astype(jnp.int32)
    earlier = jnp.cumsum(onehot, axis=0) - onehot
    places = lax.optimization_barrier(jnp.sum(earlier * onehot, axis=1))
    target = (flat_ids * capacity + places).reshape(rows_here, 2)
    slot_ids = jnp.arange(experts * capacity, dtype=jnp.int32)
    matches = (slot_ids[:, None, None] == target[None, :, :]).astype(jnp.float32)
    slot_placement = lax.optimization_barrier(jnp.sum(matches, axis=2))
    gate_weighted = lax.optimization_barrier(jnp.sum(matches * gate_values[None, :, :].astype(jnp.float32), axis=2))
    return (slot_placement, gate_weighted)

def reference(residual, heads_out, out_weight, norm_gain, up_weight, down_weight, routes, gate_values, cotangent):
    highest_precision = lax.Precision.HIGHEST
    stream = residual.astype(jnp.float32) + jnp.dot(heads_out, out_weight, preferred_element_type=jnp.float32)
    center = lax.optimization_barrier(jnp.mean(stream, axis=1))
    inv_scale = lax.rsqrt(lax.optimization_barrier(jnp.mean(stream * stream, axis=1)) - center * center + 1e-05)
    normal = (stream - center[:, None]) * inv_scale[:, None]
    normed = (normal * norm_gain[None, :]).astype(jnp.bfloat16)
    blocks = N_EXPERT
    slot_placement, gate_weighted = jax.vmap(lambda route_rows, gate_rows: route_tables(route_rows, gate_rows, EXPERTS, CAP))(routes.reshape(blocks, TOK_DEV, 2), gate_values.reshape(blocks, TOK_DEV, 2))
    normalized_blocks = normed.reshape(blocks, TOK_DEV, MODEL_WIDTH).astype(jnp.float32)
    slot_input = jnp.einsum('ksm,kmh->ksh', slot_placement, normalized_blocks, precision=highest_precision).astype(jnp.bfloat16)
    cotangent_blocks = cotangent.reshape(blocks, TOK_DEV, MODEL_WIDTH).astype(jnp.float32)
    slot_gradient = jnp.einsum('ksm,kmh->ksh', gate_weighted, cotangent_blocks, precision=highest_precision).astype(jnp.bfloat16)

    def by_expert(values):
        return values.reshape(blocks, EXPERTS, CAP, MODEL_WIDTH).transpose(1, 0, 2, 3).reshape(EXPERTS, blocks * CAP, MODEL_WIDTH)
    per_dev = FF // N_TENSOR

    def one_expert(inputs):
        rows, grad_rows, up_mat, down_mat = inputs
        pre_act = jnp.dot(rows, up_mat, preferred_element_type=jnp.float32)
        hidden_f, pullback = jax.vjp(activate, pre_act)
        hidden = hidden_f.astype(jnp.bfloat16)

        def add_out(running, block_idx):
            shard_part = lax.dynamic_slice_in_dim(hidden, block_idx * per_dev, per_dev, 1)
            matrix = lax.dynamic_slice_in_dim(down_mat, block_idx * per_dev, per_dev, 0)
            partial_value = lax.optimization_barrier(jnp.dot(shard_part, matrix, preferred_element_type=jnp.float32).astype(jnp.bfloat16))
            return (running + partial_value.astype(jnp.float32), None)
        expert_output, _ = lax.scan(add_out, jnp.zeros((rows.shape[0], MODEL_WIDTH), jnp.float32), jnp.arange(N_TENSOR, dtype=jnp.int32))
        grad_hidden = lax.dot_general(grad_rows, down_mat, (((1,), (1,)), ((), ())), preferred_element_type=jnp.float32)
        grad_act = pullback(grad_hidden)[0].astype(jnp.bfloat16)

        def add_in(running, block_idx):
            shard_part = lax.dynamic_slice_in_dim(grad_act, block_idx * per_dev, per_dev, 1)
            matrix = lax.dynamic_slice_in_dim(up_mat, block_idx * per_dev, per_dev, 1)
            partial_value = lax.optimization_barrier(lax.dot_general(shard_part, matrix, (((1,), (1,)), ((), ())), preferred_element_type=jnp.float32).astype(jnp.bfloat16))
            return (running + partial_value.astype(jnp.float32), None)
        input_gradient, _ = lax.scan(add_in, jnp.zeros((rows.shape[0], MODEL_WIDTH), jnp.float32), jnp.arange(N_TENSOR, dtype=jnp.int32))
        return (expert_output.astype(jnp.bfloat16), input_gradient.astype(jnp.bfloat16))
    expert_output, input_gradient = lax.map(one_expert, (by_expert(slot_input), by_expert(slot_gradient), up_weight, down_weight))

    def per_block_rows(values):
        return values.reshape(EXPERTS, blocks, CAP, MODEL_WIDTH).transpose(1, 0, 2, 3).reshape(blocks, EXPERTS * CAP, MODEL_WIDTH).astype(jnp.float32)
    expert_mixture = jnp.einsum('hxv,hxn->hvn', gate_weighted, per_block_rows(expert_output), precision=highest_precision).reshape(PATCH_TOKENS, MODEL_WIDTH)
    result = (stream + expert_mixture).astype(jnp.bfloat16)
    normed_gradient = jnp.einsum('hxv,hxn->hvn', slot_placement, per_block_rows(input_gradient), precision=highest_precision).reshape(PATCH_TOKENS, MODEL_WIDTH)
    grad_scaled = normed_gradient * norm_gain[None, :]
    sum_first = lax.optimization_barrier(jnp.sum(grad_scaled, axis=1)) / MODEL_WIDTH
    sum_second = lax.optimization_barrier(jnp.sum(grad_scaled * normal, axis=1)) / MODEL_WIDTH
    grad_stream = cotangent.astype(jnp.float32) + inv_scale[:, None] * (grad_scaled - sum_first[:, None] - normal * sum_second[:, None])
    grad_residual = grad_stream.astype(jnp.bfloat16)
    grad_heads = lax.dot_general(grad_residual, out_weight, (((1,), (1,)), ((), ())), preferred_element_type=jnp.float32)
    grad_out_weight = lax.dot_general(heads_out, grad_residual, (((0,), (0,)), ((), ())), preferred_element_type=jnp.float32).astype(jnp.bfloat16)
    return (result, grad_residual, grad_heads.astype(jnp.bfloat16), grad_out_weight)
```

```python
import jax
import jax.numpy as jnp
from jax import lax
from jax.experimental import pallas as pl
from jax.experimental.pallas import tpu as pltpu
from jax.sharding import Mesh, PartitionSpec as P

AXES = ("yh", "z", "yl", "x", "c")
EXPERT = ("yh", "z")
TENSOR = ("yl", "x", "c")
SPLIT = (2, 8, 4, 4, 2)
BLOCKS = 16
CAP = 9
MSG = 24
PACK = 320
SLOTS = BLOCKS * CAP
ROWS = BLOCKS * MSG
WIDTH = 2048
HID = 256
F32 = jnp.float32
BF16 = jnp.bfloat16
HIGHEST = lax.Precision.HIGHEST
ROOT = 0.7978845608028654
CUBIC = 0.044715


def iota(shape, axis):
    return lax.broadcasted_iota(jnp.int32, shape, axis)


def div(value, by):
    scale = -(-(1 << 14) // by)
    return lax.shift_right_logical(value * scale, 14)


def dot_nn(a, b, **kw):
    return lax.dot_general(a, b, (((1,), (0,)), ((), ())), preferred_element_type=F32, **kw)


def dot_nt(a, b, **kw):
    return lax.dot_general(a, b, (((1,), (1,)), ((), ())), preferred_element_type=F32, **kw)


def dot_tn(a, b, **kw):
    return lax.dot_general(a, b, (((0,), (0,)), ((), ())), preferred_element_type=F32, **kw)


def eye(n):
    return (iota((n, n), 0) == iota((n, n), 1)).astype(F32).astype(BF16)


def call(kernel, outs, name, n_smem=0, n_in=0):
    return pl.pallas_call(
        kernel,
        out_shape=outs,
        in_specs=[pl.BlockSpec(memory_space=pltpu.SMEM)] * n_smem
        + [pl.BlockSpec(memory_space=pltpu.VMEM)] * n_in,
        name=name,
        compiler_params=pltpu.CompilerParams(vmem_limit_bytes=48 * 1024 * 1024),
    )


def shape(dims, dtype):
    return jax.ShapeDtypeStruct(dims, dtype)


def split_two(value):
    high = value.astype(BF16)
    low = (value - high.astype(F32)).astype(BF16)
    return high, low


def prepare(core_ref, heads_ref, routes_ref, gates_ref, heads_t_ref, place_ref, gate_ref):
    turned = dot_nt(eye(64), heads_ref[...]).astype(BF16)
    for i in range(16):
        heads_t_ref[i] = turned
    core = core_ref[0]
    row = iota((ROWS, 128), 0)
    group = div(row, MSG)
    local = row - group * MSG
    slot = jnp.where(local < CAP, local, local - CAP)
    used = local < 2 * CAP
    expert = 2 * group + core
    first = (routes_ref[0:1, :] == expert) & used
    second = (routes_ref[1:2, :] == expert) & used
    named = jnp.where(first | second, 1.0, 0.0)
    before = (iota((128, 128), 0) < iota((128, 128), 1)).astype(F32).astype(BF16)
    earlier = dot_nn(named.astype(BF16), before)
    taken = (earlier == slot.astype(F32)) & (named > 0.5)
    place_ref[...] = jnp.where(taken, 1.0, 0.0).astype(BF16)
    gate = jnp.where(first, gates_ref[0:1, :], gates_ref[1:2, :])
    gate_ref[...] = jnp.where(taken, gate, 0.0)


def project(core_ref, heads_ref, weight_ref, residual_ref, cotangent_ref, gain_ref, out_ref):
    parts = []
    for chip in range(16):
        parts.append(heads_ref[0, chip])
        parts.append(heads_ref[1, chip])
    heads_t = jnp.concatenate(parts, axis=0)
    mixed = dot_tn(weight_ref[...], heads_t)
    out_ref[0:64] = dot_nt(eye(64), residual_ref[...]) + mixed
    out_ref[64:128] = dot_nt(eye(64), cotangent_ref[...])
    mine = div(iota((8, 128), 1), 64) == core_ref[0]
    out_ref[128:136] = jnp.where(mine, jnp.broadcast_to(gain_ref[...], (8, 128)), 0.0)


def dispatch(both_ref, place_ref, gate_ref, out_ref):
    stream = jnp.concatenate([both_ref[0, 0:64], both_ref[1, 0:64]], axis=0)
    cot = jnp.concatenate([both_ref[0, 64:128], both_ref[1, 64:128]], axis=0)
    gain = both_ref[0, 128:129] + both_ref[1, 128:129]
    shift = jnp.mean(stream, axis=0, keepdims=True)
    centered = (stream - shift).astype(BF16)
    place = place_ref[...]
    placed = place.astype(F32)
    rows_x = dot_nt(place, centered)
    rows_c = dot_nt(place, cot.astype(BF16))
    gate_col = jnp.sum(gate_ref[...], axis=1, keepdims=True)
    shift_col = jnp.sum(placed * shift, axis=1, keepdims=True)
    row = iota((ROWS, 128), 0)
    lane = iota((ROWS, 128), 1)
    local = row - div(row, MSG) * MSG
    high, low = split_two(shift_col)
    spread = jnp.where(lane == local, high.astype(F32), 0.0)
    spread = spread + jnp.where(lane == local + 16, low.astype(F32), 0.0)
    spread = jnp.where(local < CAP, spread, 0.0).astype(BF16)
    to = iota((ROWS, ROWS), 0)
    come = iota((ROWS, ROWS), 1)
    to_group = div(to, MSG)
    gather = (to - to_group * MSG == 18) & (to_group == div(come, MSG))
    stats = dot_nn(jnp.where(gather, 1.0, 0.0).astype(BF16), spread)
    gain_high, gain_low = split_two(gain)
    rest = gain - gain_high.astype(F32) - gain_low.astype(F32)
    value = jnp.where(local < CAP, rows_x, jnp.where(local < 2 * CAP, rows_c * gate_col, stats))
    value = jnp.where(local == 19, gain_high.astype(F32), value)
    value = jnp.where(local == 20, gain_low.astype(F32), value)
    value = jnp.where(local == 21, rest, value)
    value = value.astype(BF16)
    for e in range(BLOCKS):
        piece = value[e * MSG : (e + 1) * MSG]
        for y in range(4):
            out_ref[e, y] = piece


def repack(in_ref, out_ref):
    to = iota((PACK, ROWS), 0)
    come = iota((PACK, ROWS), 1)
    group = div(come, MSG)
    local = come - group * MSG
    pick = (local < CAP) & (to == group * CAP + local)
    pick |= (local >= CAP) & (local < 2 * CAP) & (to == SLOTS + group * CAP + local - CAP)
    pick |= (local == 18) & (to == 2 * SLOTS + group)
    pick |= (group == 0) & (local >= 19) & (local < 22) & (to == 304 + local - 19)
    pick = jnp.where(pick, 1.0, 0.0).astype(BF16)
    for y in range(4):
        rows = in_ref[:, y].astype(F32).reshape(ROWS, 128).astype(BF16)
        packed = dot_nn(pick, rows).astype(BF16)
        for x in range(4):
            out_ref[x, y] = packed


def experts(which_ref, in_ref, up_ref, down_ref, out_ref):
    slot = iota((SLOTS, 128), 0)
    lane = iota((SLOTS, 128), 1)
    block = div(slot, CAP)
    local = slot - block * CAP
    expand = (div(iota((SLOTS, 16), 0), CAP) == iota((SLOTS, 16), 1)).astype(F32).astype(BF16)
    shift_lane = (lane == local) | (lane == local + 16)
    chunks = [None] * 16
    cots = [None] * 16
    gains = [None] * 16
    total = jnp.zeros((SLOTS, 128), F32)
    for x in range(4):
        for y in range(4):
            shift = dot_nn(expand, in_ref[x, y, 288:304])
            shift = jnp.sum(jnp.where(shift_lane, shift, 0.0), axis=1, keepdims=True)
            chunk = in_ref[x, y, 0:144].astype(F32) + shift
            total = total + chunk
            chunks[y * 4 + x] = chunk
            cots[y * 4 + x] = in_ref[x, y, 144:288]
            gains[y * 4 + x] = in_ref[x, y, 304:320]
    center = jnp.sum(total, axis=1, keepdims=True) / WIDTH
    squares = jnp.zeros((SLOTS, 128), F32)
    for i in range(16):
        chunks[i] = chunks[i] - center
        squares = squares + chunks[i] * chunks[i]
    inv_scale = lax.rsqrt(jnp.sum(squares, axis=1, keepdims=True) / WIDTH + 1e-05)
    rows = []
    for i in range(16):
        parts = gains[i].astype(F32)
        gain = parts[0:1] + parts[1:2] + parts[2:3]
        rows.append((chunks[i] * inv_scale * gain).astype(BF16))
    rows = jnp.concatenate(
        [jnp.concatenate(rows, axis=1), jnp.concatenate(gains, axis=1)], axis=0
    )
    up = up_ref[0]
    down = down_ref[0]
    product = dot_nn(rows, up)
    pre = product[0:SLOTS]
    weigh = product[SLOTS : SLOTS + 1] + product[SLOTS + 1 : SLOTS + 2]
    weigh = weigh + product[SLOTS + 2 : SLOTS + 3]
    grad_hidden = dot_nt(jnp.concatenate(cots, axis=1), down)
    bend = jnp.tanh(ROOT * (pre + CUBIC * pre * pre * pre))
    hidden = (0.5 * pre * (1.0 + bend)).astype(BF16)
    slope = 0.5 * (1.0 + bend) + 0.5 * pre * (1.0 - bend * bend) * (
        ROOT * (1.0 + 3.0 * CUBIC * pre * pre)
    )
    grad_act = (grad_hidden * slope).astype(BF16)
    value = dot_nn(hidden, down).astype(BF16)
    grad_in = dot_nt(grad_act, up).astype(BF16)
    wide = grad_act.astype(F32)
    sum_first = jnp.sum(wide * weigh, axis=1, keepdims=True)
    sum_second = jnp.sum(wide * pre, axis=1, keepdims=True)
    spread = jnp.where(lane == local, sum_first, 0.0)
    spread = spread + jnp.where(lane == local + 16, sum_second, 0.0)
    spread = spread + jnp.where(lane == local + 32, center * (1.0 / 32), 0.0)
    spread = spread + jnp.where(lane == local + 48, inv_scale * (1.0 / 32), 0.0)
    high, low = split_two(spread)
    collect = (iota((16, SLOTS), 0) == div(iota((16, SLOTS), 1), CAP)).astype(F32).astype(BF16)
    high = dot_nn(collect, high).astype(BF16)
    low = dot_nn(collect, low).astype(BF16)
    for x in range(4):
        for y in range(4):
            at = (y * 4 + x) * 128
            out_ref[x, y, 0:144] = value[:, at : at + 128]
            out_ref[x, y, 144:288] = grad_in[:, at : at + 128]
            out_ref[x, y, 288:304] = high
            out_ref[x, y, 304:320] = low


def run_experts(which, rows, up, down):
    return pl.pallas_call(
        experts,
        out_shape=shape((4, 4, PACK, 128), BF16),
        grid_spec=pltpu.PrefetchScalarGridSpec(
            num_scalar_prefetch=1,
            grid=(1,),
            in_specs=[
                pl.BlockSpec((4, 4, PACK, 128), lambda i, j: (0, 0, 0, 0)),
                pl.BlockSpec((1, WIDTH, HID), lambda i, j: (j[0], 0, 0)),
                pl.BlockSpec((1, HID, WIDTH), lambda i, j: (j[0], 0, 0)),
            ],
            out_specs=pl.BlockSpec((4, 4, PACK, 128), lambda i, j: (0, 0, 0, 0)),
        ),
        name="experts",
        compiler_params=pltpu.CompilerParams(vmem_limit_bytes=48 * 1024 * 1024),
    )(which, rows, up, down)


def add_pair(a_ref, b_ref, out_ref):
    for x in range(4):
        for y in range(4):
            value = a_ref[x, y].astype(F32) + b_ref[x, y].astype(F32)
            out_ref[x, y, 0:288] = value[0:288].astype(BF16)
            high, low = split_two(value[288:304] + value[304:320])
            out_ref[x, y, 288:304] = high
            out_ref[x, y, 304:320] = low


def add_four(in_ref, out_ref):
    to = iota((ROWS, PACK), 0)
    come = iota((ROWS, PACK), 1)
    group = div(to, MSG)
    local = to - group * MSG
    pick = (local < CAP) & (come == group * CAP + local)
    pick |= (local >= CAP) & (local < 2 * CAP) & (come == SLOTS + group * CAP + local - CAP)
    pick |= (local == 18) & (come == 288 + group)
    pick |= (local == 19) & (come == 304 + group)
    pick = jnp.where(pick, 1.0, 0.0).astype(BF16)
    for y in range(4):
        value = in_ref[0, y].astype(F32)
        for x in range(1, 4):
            value = value + in_ref[x, y].astype(F32)
        high, low = split_two(value[288:304] + value[304:320])
        rows = jnp.concatenate([value[0:288].astype(BF16), high, low], axis=0)
        message = dot_nn(pick, rows).astype(BF16)
        for e in range(BLOCKS):
            out_ref[e, y] = message[e * MSG : (e + 1) * MSG]


def combine(in_ref, place_ref, gate_ref, out_ref):
    value = in_ref[:, 0].astype(F32)
    for y in range(1, 4):
        value = value + in_ref[:, y].astype(F32)
    stats = value[:, 18:19] + value[:, 19:20]
    stats = jnp.broadcast_to(stats, (BLOCKS, MSG, 128)).reshape(ROWS, 128)
    value = value.reshape(ROWS, 128).astype(BF16)
    row = iota((ROWS, 128), 0)
    lane = iota((ROWS, 128), 1)
    local = row - div(row, MSG) * MSG
    forward = local < CAP
    place = place_ref[...].astype(F32)
    ahead = jnp.where(forward, place, 0.0)
    behind = jnp.where(forward, 0.0, place).astype(BF16)
    gate = jnp.where(forward, gate_ref[...], 0.0)
    mixture = dot_tn(value.astype(F32), gate, precision=HIGHEST)
    grad = dot_tn(value, behind)
    out_ref[0, 0:64] = mixture[0:64]
    out_ref[1, 0:64] = mixture[64:128]
    out_ref[0, 64:128] = grad[0:64]
    out_ref[1, 64:128] = grad[64:128]
    for q in range(4):
        column = jnp.sum(jnp.where(lane == local + 16 * q, stats, 0.0), axis=1, keepdims=True)
        token = jnp.sum(ahead * column, axis=0, keepdims=True)
        out_ref[0, 128 + q : 129 + q] = token
        out_ref[1, 128 + q : 129 + q] = token
    out_ref[0, 132:136] = jnp.zeros((4, 128), F32)
    out_ref[1, 132:136] = jnp.zeros((4, 128), F32)


def finish(in_ref, own_ref, gain_ref, weight_ref, heads_ref, result_ref, grad_ref, gh_ref, gw_ref):
    got = in_ref[0] + in_ref[1]
    stream = own_ref[0:64]
    cot = own_ref[64:128]
    mixture = got[0:64]
    scaled = got[64:128] * gain_ref[...]
    first = got[128:129] / WIDTH
    second = got[129:130] / WIDTH
    center = got[130:131] * 0.5
    inv_scale = got[131:132] * 0.5
    normal = (stream - center) * inv_scale
    grad = (cot + inv_scale * (scaled - first - normal * second)).astype(BF16)
    result = (stream + mixture).astype(BF16)
    turn = eye(128)
    result_ref[...] = dot_nt(turn, result).astype(BF16)
    grad_ref[...] = dot_nt(turn, grad).astype(BF16)
    heads_grad = dot_nn(weight_ref[...], grad).astype(BF16)
    for chip in range(16):
        for core in range(2):
            at = (chip * 2 + core) * 64
            gh_ref[core, chip] = heads_grad[at : at + 64]
            heads = jnp.concatenate([heads_ref[0, chip], heads_ref[1, chip]], axis=0)
        gw_ref[chip] = dot_nt(grad, heads).astype(BF16)


def a2a(value, axes):
    return lax.all_to_all(value, axes, split_axis=0, concat_axis=0, tiled=True)


def total(value):
    return jnp.sum(value.astype(F32), axis=0)


def local(
    residual, heads_out, out_weight, norm_gain, up_weight, down_weight, routes, gates, cotangent
):
    core = lax.axis_index("c").astype(jnp.int32).reshape(1)
    swap = [(0, 1), (1, 0)]
    heads_t, place, gate = call(
        prepare,
        (shape((16, 64, 128), BF16), shape((ROWS, 128), BF16), shape((ROWS, 128), F32)),
        "prepare",
        1,
        3,
    )(core, heads_out, routes.T, gates.T)
    heads_t = a2a(heads_t, ("yl", "x"))
    heads_t = lax.all_gather(heads_t, "c", axis=0)
    gain_row = jnp.concatenate([norm_gain, norm_gain]).reshape(1, 128)
    own = call(project, shape((136, 128), F32), "project", 1, 5)(
        core, heads_t, out_weight, residual, cotangent, gain_row
    )
    both = lax.all_gather(own, "c", axis=0)
    message = call(dispatch, shape((BLOCKS, 4, MSG, 128), BF16), "dispatch", 0, 3)(
        both, place, gate
    )
    message = a2a(message.reshape(64, MSG, 128), ("yh", "z", "yl"))
    packed = call(repack, shape((4, 4, PACK, 128), BF16), "repack", 0, 1)(
        message.reshape(BLOCKS, 4, MSG, 128)
    )
    mine = a2a(packed, "x")
    other = lax.ppermute(mine, "c", swap)
    other_part = run_experts(1 - core, other, up_weight, down_weight)
    mine_part = run_experts(core, mine, up_weight, down_weight)
    came = lax.ppermute(other_part, "c", swap)
    part = call(add_pair, shape((4, 4, PACK, 128), BF16), "add_pair", 0, 2)(mine_part, came)
    part = a2a(part, "x")
    message = call(add_four, shape((BLOCKS, 4, MSG, 128), BF16), "add_four", 0, 1)(part)
    message = a2a(message.reshape(64, MSG, 128), ("yh", "z", "yl"))
    halves = call(combine, shape((2, 136, 128), F32), "combine", 0, 3)(
        message.reshape(BLOCKS, 4, MSG, 128), place, gate
    )
    halves = a2a(halves, "c")
    result, grad_residual, grad_heads, grad_weight = call(
        finish,
        (
            shape((128, 64), BF16),
            shape((128, 64), BF16),
            shape((2, 16, 64, 128), BF16),
            shape((16, 64, 128), BF16),
        ),
        "finish",
        0,
        5,
    )(halves, own, norm_gain.reshape(64, 1), out_weight, heads_t)
    grad_weight = total(a2a(grad_weight, EXPERT)).astype(BF16)
    grad_weight = a2a(jnp.broadcast_to(grad_weight, (16, 64, 128)), EXPERT)
    grad_weight = grad_weight.transpose(0, 2, 1).reshape(WIDTH, 64)
    grad_heads = total(a2a(grad_heads, "c")).astype(BF16)
    grad_heads = total(a2a(grad_heads, ("yl", "x"))).astype(BF16).T
    return (result, grad_residual, grad_heads, grad_weight)


def solution(mesh):
    view = Mesh(mesh.devices.reshape(SPLIT), AXES)
    return jax.shard_map(
        local,
        mesh=view,
        in_specs=(
            P(EXPERT, TENSOR),
            P(EXPERT, TENSOR),
            P(None, TENSOR),
            P(TENSOR),
            P(EXPERT, None, TENSOR),
            P(EXPERT, TENSOR, None),
            P(EXPERT, None),
            P(EXPERT, None),
            P(EXPERT, TENSOR),
        ),
        out_specs=(
            P(EXPERT, TENSOR),
            P(EXPERT, TENSOR),
            P(EXPERT, TENSOR),
            P(None, TENSOR),
        ),
        check_vma=False,
    )
```

```python
import jax
import jax.numpy as jnp
from jax import lax
from jax.experimental import pallas as pl
from jax.experimental.pallas import tpu as pltpu
from jax.sharding import Mesh, PartitionSpec as P

AXES = ("yh", "z", "yl", "x", "c")
EXPERT = ("yh", "z")
TENSOR = ("yl", "x", "c")
SPLIT = (2, 8, 4, 4, 2)
BLOCKS = 16
CAP = 9
MSG = 24
PACK = 304
SLOTS = BLOCKS * CAP
SIDE = 2432
ROWS = BLOCKS * MSG
WIDTH = 2048
HID = 256
F32 = jnp.float32
BF16 = jnp.bfloat16
HIGHEST = lax.Precision.HIGHEST
ROOT = 0.7978845608028654
CUBIC = 0.044715


def iota(shape, axis):
    return lax.broadcasted_iota(jnp.int32, shape, axis)


def div(value, by):
    scale = -(-(1 << 14) // by)
    return lax.shift_right_logical(value * scale, 14)


def dot_nn(a, b, **kw):
    return lax.dot_general(a, b, (((1,), (0,)), ((), ())), preferred_element_type=F32, **kw)


def dot_nt(a, b, **kw):
    return lax.dot_general(a, b, (((1,), (1,)), ((), ())), preferred_element_type=F32, **kw)


def dot_tn(a, b, **kw):
    return lax.dot_general(a, b, (((0,), (0,)), ((), ())), preferred_element_type=F32, **kw)


def eye(n):
    return (iota((n, n), 0) == iota((n, n), 1)).astype(F32).astype(BF16)


def call(kernel, outs, name, n_smem, n_in):
    return pl.pallas_call(
        kernel,
        out_shape=outs,
        in_specs=[pl.BlockSpec(memory_space=pltpu.SMEM)] * n_smem
        + [pl.BlockSpec(memory_space=pltpu.VMEM)] * n_in,
        name=name,
        compiler_params=pltpu.CompilerParams(vmem_limit_bytes=48 * 1024 * 1024),
    )


def shape(dims, dtype):
    return jax.ShapeDtypeStruct(dims, dtype)


def split_three(value):
    high = value.astype(BF16)
    rest = value - high.astype(F32)
    middle = rest.astype(BF16)
    return high, middle, (rest - middle.astype(F32)).astype(BF16)


def split_two(value):
    high = value.astype(BF16)
    low = (value - high.astype(F32)).astype(BF16)
    return high, low


def join(block):
    return block + jnp.concatenate([block[:, 64:], block[:, :64]], axis=1)


def part(value):
    high, low = split_two(value)
    lane = iota(value.shape, 1)
    return jnp.where(lane < 64, high.astype(F32), low.astype(F32)).astype(BF16)


def pack(weight_ref, residual_ref, cotangent_ref, gain_ref, out_ref):
    out_ref[:, 0:2048] = weight_ref[...]
    out_ref[:, 2048:2176] = residual_ref[...]
    out_ref[:, 2176:2304] = cotangent_ref[...]
    high, middle, low = split_three(jnp.broadcast_to(gain_ref[...], (64, 128)))
    lane = iota((64, 128), 1)
    value = jnp.where(lane == 0, high.astype(F32), middle.astype(F32))
    out_ref[:, 2304:2432] = jnp.where(lane == 2, low.astype(F32), value).astype(BF16)


def prepare(core_ref, routes_ref, gates_ref, place_ref, gate_ref):
    core = core_ref[0]
    row = iota((ROWS, 128), 0)
    group = div(row, MSG)
    local = row - group * MSG
    slot = jnp.where(local < CAP, local, local - CAP)
    used = local < 2 * CAP
    expert = 2 * group + core
    first = (routes_ref[0:1, :] == expert) & used
    second = (routes_ref[1:2, :] == expert) & used
    named = jnp.where(first | second, 1.0, 0.0)
    before = (iota((128, 128), 0) < iota((128, 128), 1)).astype(F32).astype(BF16)
    earlier = dot_nn(named.astype(BF16), before)
    taken = (earlier == slot.astype(F32)) & (named > 0.5)
    place_ref[...] = jnp.where(taken, 1.0, 0.0).astype(BF16)
    gate = jnp.where(first, gates_ref[0:1, :], gates_ref[1:2, :])
    gate_ref[...] = jnp.where(taken, gate, 0.0)


def turn_weight(core_ref, side_ref, out_ref):
    mirror = eye(128)
    for chip in range(16):
        turned = dot_nt(mirror, side_ref[:, chip * 128 : chip * 128 + 128])
        out_ref[chip] = jnp.where(core_ref[0] == 0, turned[0:64], turned[64:128]).astype(BF16)


def dispatch(block_ref, heads_ref, side_ref, place_ref, gate_ref, stream_ref, out_ref):
    pieces = []
    for chip in range(16):
        pieces.append(heads_ref[0, chip])
        pieces.append(heads_ref[1, chip])
    mixed = dot_nn(side_ref[:, 0:2048], jnp.concatenate(pieces, axis=0))
    stream = side_ref[:, 2048:2176].astype(F32) + mixed
    stream_ref[...] = stream
    shift = jnp.mean(stream, axis=0, keepdims=True)
    centered = (stream - shift).astype(BF16)
    place = place_ref[...]
    placed = place.astype(F32)
    rows_x = dot_nt(place, centered)
    rows_c = dot_nt(place, side_ref[:, 2176:2304])
    gate_col = jnp.sum(gate_ref[...], axis=1, keepdims=True)
    shift_col = jnp.sum(placed * shift, axis=1, keepdims=True)
    row = iota((ROWS, 128), 0)
    lane = iota((ROWS, 128), 1)
    local = row - div(row, MSG) * MSG
    high, low = split_two(shift_col)
    spread = jnp.where(lane == local, high.astype(F32), 0.0)
    spread = spread + jnp.where(lane == local + 16, low.astype(F32), 0.0)
    spread = jnp.where(local < CAP, spread, 0.0).astype(BF16)
    to = iota((ROWS, ROWS), 0)
    come = iota((ROWS, ROWS), 1)
    to_group = div(to, MSG)
    gather = (to - to_group * MSG == 18) & (to_group == div(come, MSG))
    stats = dot_nn(jnp.where(gather, 1.0, 0.0).astype(BF16), spread)
    feature = iota((128, 128), 0)
    at = iota((128, 128), 1) - 32
    which = lax.shift_right_logical(jnp.maximum(at, 0), 3)
    mine = (at >= 0) & (at < 24) & (feature == 8 * block_ref[0] + (at & 7))
    gains = side_ref[:, 2304:2432].astype(F32)
    gain = jnp.where(which == 0, gains[:, 0:1], jnp.where(which == 1, gains[:, 1:2], gains[:, 2:3]))
    gain = jnp.sum(jnp.where(mine, gain, 0.0), axis=0, keepdims=True)
    value = jnp.where(local < CAP, rows_x, jnp.where(local < 2 * CAP, rows_c * gate_col, stats))
    value = jnp.where(local == 18, value + gain, value).astype(BF16)
    for e in range(BLOCKS):
        piece = value[e * MSG : (e + 1) * MSG]
        for y in range(4):
            out_ref[e, y] = piece


def selection(to, come):
    group = div(come, MSG)
    local = come - group * MSG
    pick = (local < CAP) & (to == group * CAP + local)
    pick |= (local >= CAP) & (local < 2 * CAP) & (to == SLOTS + group * CAP + local - CAP)
    pick |= (local == 18) & (to == 2 * SLOTS + group)
    return jnp.where(pick, 1.0, 0.0).astype(BF16)


def repack(in_ref, out_ref):
    pick = selection(iota((PACK, ROWS), 0), iota((PACK, ROWS), 1))
    for y in range(4):
        rows = in_ref[:, y].astype(F32).reshape(ROWS, 128).astype(BF16)
        packed = dot_nn(pick, rows).astype(BF16)
        for x in range(4):
            out_ref[x, y] = packed


def slot_tables():
    slot = iota((SLOTS, 128), 0)
    return slot - div(slot, CAP) * CAP, iota((SLOTS, 128), 1)


def read_rows(in_ref):
    local, lane = slot_tables()
    expand = (div(iota((SLOTS, 16), 0), CAP) == iota((SLOTS, 16), 1)).astype(F32).astype(BF16)
    shift_lane = (lane == local) | (lane == local + 16)
    at = iota((128, 128), 0) - 32
    collect = (at >= 0) & (at < 24) & ((at & 7) == (iota((128, 128), 1) & 7))
    collect = jnp.where(collect, 1.0, 0.0).astype(BF16)
    own = lax.shift_right_logical(iota((16, 128), 1), 3) == iota((16, 128), 0)
    chunks = [None] * 16
    gains = [None] * 16
    total = jnp.zeros((SLOTS, 128), F32)
    for x in range(4):
        for y in range(4):
            block = in_ref[x, y, 288:304]
            shift = dot_nn(expand, block)
            shift = jnp.sum(jnp.where(shift_lane, shift, 0.0), axis=1, keepdims=True)
            chunk = in_ref[x, y, 0:144].astype(F32) + shift
            total = total + chunk
            chunks[y * 4 + x] = chunk
            gain = jnp.where(own, dot_nn(block, collect), 0.0)
            gains[y * 4 + x] = jnp.sum(gain, axis=0, keepdims=True)
    center = jnp.sum(total, axis=1, keepdims=True) / WIDTH
    squares = jnp.zeros((SLOTS, 128), F32)
    for i in range(16):
        chunks[i] = chunks[i] - center
        squares = squares + chunks[i] * chunks[i]
    inv_scale = lax.rsqrt(jnp.sum(squares, axis=1, keepdims=True) / WIDTH + 1e-05)
    rows = []
    for i in range(16):
        rows.append((chunks[i] * inv_scale * gains[i]).astype(BF16))
    return jnp.concatenate(rows, axis=1), jnp.concatenate(gains, axis=1), center, inv_scale


def ahead(in_ref, up, down):
    rows, gain, center, inv_scale = read_rows(in_ref)
    high, middle, low = split_three(jnp.broadcast_to(gain, (16, WIDTH)))
    row = iota((16, WIDTH), 0)
    gain = jnp.where(row == 0, high.astype(F32), middle.astype(F32))
    gain = jnp.where(row == 2, low.astype(F32), gain).astype(BF16)
    product = dot_nn(jnp.concatenate([rows, gain], axis=0), up)
    pre = product[0:SLOTS]
    weigh = product[SLOTS : SLOTS + 1] + product[SLOTS + 1 : SLOTS + 2]
    weigh = weigh + product[SLOTS + 2 : SLOTS + 3]
    bend = jnp.tanh(ROOT * (pre + CUBIC * pre * pre * pre))
    hidden = (0.5 * pre * (1.0 + bend)).astype(BF16)
    return pre, weigh, center, inv_scale, dot_nn(hidden, down).astype(BF16)


def behind(in_ref, up, down, pre, weigh, center, inv_scale):
    cots = [None] * 16
    for x in range(4):
        for y in range(4):
            cots[y * 4 + x] = in_ref[x, y, 144:288]
    grad_hidden = dot_nt(jnp.concatenate(cots, axis=1), down)
    bend = jnp.tanh(ROOT * (pre + CUBIC * pre * pre * pre))
    slope = 0.5 * (1.0 + bend) + 0.5 * pre * (1.0 - bend * bend) * (
        ROOT * (1.0 + 3.0 * CUBIC * pre * pre)
    )
    grad_act = (grad_hidden * slope).astype(BF16)
    wide = grad_act.astype(F32)
    sum_first = jnp.sum(wide * weigh, axis=1, keepdims=True)
    sum_second = jnp.sum(wide * pre, axis=1, keepdims=True)
    local, lane = slot_tables()
    spread = jnp.where(lane == local, sum_first, 0.0)
    spread = spread + jnp.where(lane == local + 16, sum_second, 0.0)
    spread = spread + jnp.where(lane == local + 32, center * (1.0 / 32), 0.0)
    spread = spread + jnp.where(lane == local + 48, inv_scale * (1.0 / 32), 0.0)
    high, low = split_two(spread)
    collect = (iota((16, SLOTS), 0) == div(iota((16, SLOTS), 1), CAP)).astype(F32).astype(BF16)
    high = dot_nn(collect, high)
    low = dot_nn(collect, low)
    stats = high + jnp.concatenate([low[:, 64:], low[:, :64]], axis=1)
    return dot_nt(grad_act, up).astype(BF16), stats.astype(BF16)


def both_ways(which_ref, in_ref, up_ref, down_ref, out_ref):
    up, down = up_ref[which_ref[0]], down_ref[which_ref[0]]
    pre, weigh, center, inv_scale, value = ahead(in_ref, up, down)
    grad_in, stats = behind(in_ref, up, down, pre, weigh, center, inv_scale)
    for x in range(4):
        for y in range(4):
            at = (y * 4 + x) * 128
            out_ref[x, y, 0:144] = value[:, at : at + 128]
            out_ref[x, y, 144:288] = grad_in[:, at : at + 128]
            out_ref[x, y, 288:304] = stats


def only_ahead(which_ref, in_ref, up_ref, down_ref, out_ref, pre_ref, weigh_ref, scalar_ref):
    up, down = up_ref[which_ref[0]], down_ref[which_ref[0]]
    pre, weigh, center, inv_scale, value = ahead(in_ref, up, down)
    pre_ref[...] = pre
    weigh_ref[...] = jnp.broadcast_to(weigh, (8, HID))
    lane = iota((SLOTS, 128), 1)
    scalar_ref[...] = jnp.where(lane == 0, center, inv_scale)
    for x in range(4):
        for y in range(4):
            at = (y * 4 + x) * 128
            out_ref[x, y] = value[:, at : at + 128]


def only_behind(
    which_ref, in_ref, up_ref, down_ref, pre_ref, weigh_ref, scalar_ref, out_ref
):
    up, down = up_ref[which_ref[0]], down_ref[which_ref[0]]
    center, inv_scale = scalar_ref[:, 0:1], scalar_ref[:, 1:2]
    grad_in, stats = behind(
        in_ref, up, down, pre_ref[...], weigh_ref[0:1], center, inv_scale
    )
    for x in range(4):
        for y in range(4):
            at = (y * 4 + x) * 128
            out_ref[x, y, 0:144] = grad_in[:, at : at + 128]
            out_ref[x, y, 144:160] = stats


def add_pair(value_ref, grad_ref, came_ref, out_ref):
    for x in range(4):
        for y in range(4):
            came = came_ref[x, y].astype(F32)
            out_ref[x, y, 0:144] = (value_ref[x, y].astype(F32) + came[0:144]).astype(BF16)
            grad = grad_ref[x, y].astype(F32)
            out_ref[x, y, 144:288] = (grad[0:144] + came[144:288]).astype(BF16)
            out_ref[x, y, 288:304] = part(join(grad[144:160] + came[288:304]))


def add_four(in_ref, out_ref):
    pick = selection(iota((ROWS, PACK), 1), iota((ROWS, PACK), 0))
    for y in range(4):
        value = in_ref[0, y].astype(F32)
        for x in range(1, 4):
            value = value + in_ref[x, y].astype(F32)
        rows = jnp.concatenate([value[0:288].astype(BF16), part(join(value[288:304]))], axis=0)
        message = dot_nn(pick, rows).astype(BF16)
        for e in range(BLOCKS):
            out_ref[e, y] = message[e * MSG : (e + 1) * MSG]


def combine(in_ref, place_ref, gate_ref, out_ref):
    value = in_ref[:, 0].astype(F32)
    for y in range(1, 4):
        value = value + in_ref[:, y].astype(F32)
    stats = value[:, 18]
    stats = join(stats).reshape(BLOCKS, 1, 128)
    stats = jnp.broadcast_to(stats, (BLOCKS, MSG, 128)).reshape(ROWS, 128)
    value = value.reshape(ROWS, 128).astype(BF16)
    row = iota((ROWS, 128), 0)
    lane = iota((ROWS, 128), 1)
    local = row - div(row, MSG) * MSG
    forward = local < CAP
    place = place_ref[...].astype(F32)
    ahead_place = jnp.where(forward, place, 0.0)
    behind_place = jnp.where(forward, 0.0, place).astype(BF16)
    gate = jnp.where(forward, gate_ref[...], 0.0)
    out_ref[0:128] = dot_tn(value.astype(F32), gate, precision=HIGHEST)
    out_ref[128:256] = dot_tn(value, behind_place)
    for q in range(4):
        column = jnp.sum(jnp.where(lane == local + 16 * q, stats, 0.0), axis=1, keepdims=True)
        out_ref[256 + q : 257 + q] = jnp.sum(ahead_place * column, axis=0, keepdims=True)
    out_ref[260:264] = jnp.zeros((4, 128), F32)


def finish(
    core_ref, in_ref, stream_ref, side_ref, weight_ref, heads_ref, result_ref, grad_ref, gh_ref, gw_ref
):
    got = in_ref[0] + in_ref[1]
    stream = stream_ref[...]
    cot = side_ref[:, 2176:2304].astype(F32)
    gains = side_ref[:, 2304:2432].astype(F32)
    scaled = got[128:256] * (gains[:, 0:1] + gains[:, 1:2] + gains[:, 2:3])
    first = got[256:257] / WIDTH
    second = got[257:258] / WIDTH
    center = got[258:259] * 0.5
    inv_scale = got[259:260] * 0.5
    normal = (stream - center) * inv_scale
    grad = cot + inv_scale * (scaled - first - normal * second)
    result = stream + got[0:128]
    low = core_ref[0] == 0
    result_ref[...] = jnp.where(low, result[0:64], result[64:128]).astype(BF16)
    own = jnp.where(low, grad[0:64], grad[64:128]).astype(BF16)
    grad_ref[...] = own
    grad = grad.astype(BF16)
    for chip in range(16):
        gh_ref[chip] = dot_nn(weight_ref[chip], grad).astype(BF16)
        heads = jnp.concatenate([heads_ref[0, chip], heads_ref[1, chip]], axis=0)
        gw_ref[chip] = dot_nt(own, heads).astype(BF16)


def a2a(value, axes):
    return lax.all_to_all(value, axes, split_axis=0, concat_axis=0, tiled=True)


def total(value):
    return jnp.sum(value.astype(F32), axis=0)


def local(
    residual, heads_out, out_weight, norm_gain, up_weight, down_weight, routes, gates, cotangent
):
    core = lax.axis_index("c").astype(jnp.int32).reshape(1)
    block = lax.axis_index(EXPERT).astype(jnp.int32).reshape(1)
    swap = [(0, 1), (1, 0)]
    heads_t = a2a(jnp.broadcast_to(heads_out.T, (16, 64, 128)), ("yl", "x"))
    side = call(pack, shape((64, SIDE), BF16), "pack", 0, 4)(
        out_weight.T, residual.T, cotangent.T, norm_gain.reshape(64, 1)
    )
    side = lax.all_gather(side, "c", axis=0, tiled=True)
    place, gate = call(
        prepare, (shape((ROWS, 128), BF16), shape((ROWS, 128), F32)), "prepare", 1, 2
    )(core, routes.T, gates.T)
    turned = call(turn_weight, shape((16, 64, 128), BF16), "turn_weight", 1, 1)(core, side)
    heads_t = lax.all_gather(heads_t, "c", axis=0)
    stream, message = call(
        dispatch, (shape((128, 128), F32), shape((BLOCKS, 4, MSG, 128), BF16)), "dispatch", 1, 4
    )(block, heads_t, side, place, gate)
    message = a2a(message.reshape(64, MSG, 128), ("yh", "z", "yl"))
    packed = call(repack, shape((4, 4, PACK, 128), BF16), "repack", 0, 1)(
        message.reshape(BLOCKS, 4, MSG, 128)
    )
    mine = a2a(packed, "x")
    other = lax.ppermute(mine, "c", swap)
    value, pre, weigh, scalars = call(
        only_ahead,
        (
            shape((4, 4, SLOTS, 128), BF16),
            shape((SLOTS, HID), F32),
            shape((8, HID), F32),
            shape((SLOTS, 128), F32),
        ),
        "only_ahead",
        1,
        3,
    )(core, mine, up_weight, down_weight)
    sent = call(both_ways, shape((4, 4, PACK, 128), BF16), "both_ways", 1, 3)(
        1 - core, other, up_weight, down_weight
    )
    sent, pre = lax.optimization_barrier((sent, pre))
    came = lax.ppermute(sent, "c", swap)
    grad = call(only_behind, shape((4, 4, SLOTS + 16, 128), BF16), "only_behind", 1, 6)(
        core, mine, up_weight, down_weight, pre, weigh, scalars
    )
    summed = call(add_pair, shape((4, 4, PACK, 128), BF16), "add_pair", 0, 3)(value, grad, came)
    summed = a2a(summed, "x")
    message = call(add_four, shape((BLOCKS, 4, MSG, 128), BF16), "add_four", 0, 1)(summed)
    message = a2a(message.reshape(64, MSG, 128), ("yh", "z", "yl"))
    both = call(combine, shape((264, 128), F32), "combine", 0, 3)(
        message.reshape(BLOCKS, 4, MSG, 128), place, gate
    )
    both = lax.all_gather(both, "c", axis=0)
    result, grad_residual, grad_heads, grad_weight = call(
        finish,
        (
            shape((64, 128), BF16),
            shape((64, 128), BF16),
            shape((16, 64, 128), BF16),
            shape((16, 64, 128), BF16),
        ),
        "finish",
        1,
        5,
    )(core, both, stream, side, turned, heads_t)
    grad_weight = total(a2a(grad_weight.reshape(8, 2, 64, 128), "z"))
    grad_weight, grad_heads = lax.optimization_barrier((grad_weight, grad_heads))
    grad_weight = grad_weight + lax.ppermute(grad_weight, "yh", swap)
    grad_heads = total(a2a(grad_heads, ("yl", "x"))).astype(BF16).T
    grad_weight = jnp.broadcast_to(grad_weight.astype(BF16), (8, 2, 64, 128))
    grad_weight = a2a(grad_weight, "z")
    grad_weight = grad_weight.transpose(2, 0, 1, 3).reshape(64, WIDTH).T
    return (result.T, grad_residual.T, grad_heads, grad_weight)


def solution(mesh):
    view = Mesh(mesh.devices.reshape(SPLIT), AXES)
    return jax.shard_map(
        local,
        mesh=view,
        in_specs=(
            P(EXPERT, TENSOR),
            P(EXPERT, TENSOR),
            P(None, TENSOR),
            P(TENSOR),
            P(EXPERT, None, TENSOR),
            P(EXPERT, TENSOR, None),
            P(EXPERT, None),
            P(EXPERT, None),
            P(EXPERT, TENSOR),
        ),
        out_specs=(
            P(EXPERT, TENSOR),
            P(EXPERT, TENSOR),
            P(EXPERT, TENSOR),
            P(None, TENSOR),
        ),
        check_vma=False,
    )
```

```python
import jax
import jax.numpy as jnp
from jax import lax
from jax.experimental import pallas as pl
from jax.experimental.pallas import tpu as pltpu
from jax.sharding import Mesh, PartitionSpec as P

AXES = ("yh", "z", "yl", "x", "c")
EXPERT = ("yh", "z")
TENSOR = ("yl", "x", "c")
SPLIT = (2, 8, 4, 4, 2)
BLOCKS = 16
CAP = 9
MSG = 24
ORDER = (0, 2, 1, 3)
PACK = 304
SLOTS = BLOCKS * CAP
SIDE = 2432
ROWS = BLOCKS * MSG
WIDTH = 2048
HID = 256
F32 = jnp.float32
BF16 = jnp.bfloat16
HIGHEST = lax.Precision.HIGHEST
ROOT = 0.7978845608028654
CUBIC = 0.044715


def iota(shape, axis):
    return lax.broadcasted_iota(jnp.int32, shape, axis)


def div(value, by):
    scale = -(-(1 << 14) // by)
    return lax.shift_right_logical(value * scale, 14)


def dot_nn(a, b, **kw):
    return lax.dot_general(a, b, (((1,), (0,)), ((), ())), preferred_element_type=F32, **kw)


def dot_nt(a, b, **kw):
    return lax.dot_general(a, b, (((1,), (1,)), ((), ())), preferred_element_type=F32, **kw)


def dot_tn(a, b, **kw):
    return lax.dot_general(a, b, (((0,), (0,)), ((), ())), preferred_element_type=F32, **kw)


def eye(n):
    return (iota((n, n), 0) == iota((n, n), 1)).astype(F32).astype(BF16)


def call(kernel, outs, name, n_smem, n_in):
    return pl.pallas_call(
        kernel,
        out_shape=outs,
        in_specs=[pl.BlockSpec(memory_space=pltpu.SMEM)] * n_smem
        + [pl.BlockSpec(memory_space=pltpu.VMEM)] * n_in,
        out_specs=jax.tree.map(lambda _: pl.BlockSpec(memory_space=pltpu.VMEM), outs),
        name=name,
        compiler_params=pltpu.CompilerParams(vmem_limit_bytes=16 * 1024 * 1024),
    )


def shape(dims, dtype):
    return jax.ShapeDtypeStruct(dims, dtype)


def split_three(value):
    high = value.astype(BF16)
    rest = value - high.astype(F32)
    middle = rest.astype(BF16)
    return high, middle, (rest - middle.astype(F32)).astype(BF16)


def split_two(value):
    high = value.astype(BF16)
    low = (value - high.astype(F32)).astype(BF16)
    return high, low


def join(block):
    return block + jnp.concatenate([block[:, 64:], block[:, :64]], axis=1)


def part(value):
    high, low = split_two(value)
    lane = iota(value.shape, 1)
    return jnp.where(lane < 64, high.astype(F32), low.astype(F32)).astype(BF16)


def pack(weight_ref, residual_ref, cotangent_ref, gain_ref, out_ref):
    out_ref[:, 0:2048] = weight_ref[...]
    out_ref[:, 2048:2176] = residual_ref[...]
    out_ref[:, 2176:2304] = cotangent_ref[...]
    high, middle, low = split_three(jnp.broadcast_to(gain_ref[...], (64, 128)))
    lane = iota((64, 128), 1)
    value = jnp.where(lane == 0, high.astype(F32), middle.astype(F32))
    out_ref[:, 2304:2432] = jnp.where(lane == 2, low.astype(F32), value).astype(BF16)


def prepare(core_ref, routes_ref, gates_ref, place_ref, gate_ref, pick_ref, drop_ref):
    core = core_ref[0]
    row = iota((ROWS, 128), 0)
    group = div(row, MSG)
    local = row - group * MSG
    slot = jnp.where(local < CAP, local, local - CAP)
    used = local < 2 * CAP
    expert = 2 * group + core
    first = (routes_ref[0:1, :] == expert) & used
    second = (routes_ref[1:2, :] == expert) & used
    named = jnp.where(first | second, 1.0, 0.0)
    before = (iota((128, 128), 0) < iota((128, 128), 1)).astype(F32).astype(BF16)
    earlier = dot_nn(named.astype(BF16), before)
    taken = (earlier == slot.astype(F32)) & (named > 0.5)
    place_ref[...] = jnp.where(taken, 1.0, 0.0).astype(BF16)
    gate = jnp.where(first, gates_ref[0:1, :], gates_ref[1:2, :])
    gate_ref[...] = jnp.where(taken, gate, 0.0)
    pick_ref[...] = selection(iota((PACK, ROWS), 0), iota((PACK, ROWS), 1))
    drop_ref[...] = selection(iota((ROWS, PACK), 1), iota((ROWS, PACK), 0))


def turn_weight(core_ref, side_ref, out_ref):
    mirror = eye(128)
    for chip in range(16):
        turned = dot_nt(mirror, side_ref[:, chip * 128 : chip * 128 + 128])
        out_ref[chip] = jnp.where(core_ref[0] == 0, turned[0:64], turned[64:128]).astype(BF16)


def dispatch(block_ref, heads_ref, side_ref, place_ref, gate_ref, stream_ref, out_ref):
    pieces = []
    for chip in range(16):
        pieces.append(heads_ref[0, chip])
        pieces.append(heads_ref[1, chip])
    mixed = dot_nn(side_ref[:, 0:2048], jnp.concatenate(pieces, axis=0))
    stream = side_ref[:, 2048:2176].astype(F32) + mixed
    stream_ref[...] = stream
    shift = jnp.mean(stream, axis=0, keepdims=True)
    centered = (stream - shift).astype(BF16)
    place = place_ref[...]
    placed = place.astype(F32)
    rows_x = dot_nt(place, centered)
    rows_c = dot_nt(place, side_ref[:, 2176:2304])
    gate_col = jnp.sum(gate_ref[...], axis=1, keepdims=True)
    shift_col = jnp.sum(placed * shift, axis=1, keepdims=True)
    row = iota((ROWS, 128), 0)
    lane = iota((ROWS, 128), 1)
    local = row - div(row, MSG) * MSG
    high, low = split_two(shift_col)
    spread = jnp.where(lane == local, high.astype(F32), 0.0)
    spread = spread + jnp.where(lane == local + 16, low.astype(F32), 0.0)
    spread = jnp.where(local < CAP, spread, 0.0).astype(BF16)
    to = iota((ROWS, ROWS), 0)
    come = iota((ROWS, ROWS), 1)
    to_group = div(to, MSG)
    gather = (to - to_group * MSG == 18) & (to_group == div(come, MSG))
    stats = dot_nn(jnp.where(gather, 1.0, 0.0).astype(BF16), spread)
    feature = iota((128, 128), 0)
    at = iota((128, 128), 1) - 32
    which = lax.shift_right_logical(jnp.maximum(at, 0), 3)
    mine = (at >= 0) & (at < 24) & (feature == 8 * block_ref[0] + (at & 7))
    gains = side_ref[:, 2304:2432].astype(F32)
    gain = jnp.where(which == 0, gains[:, 0:1], jnp.where(which == 1, gains[:, 1:2], gains[:, 2:3]))
    gain = jnp.sum(jnp.where(mine, gain, 0.0), axis=0, keepdims=True)
    value = jnp.where(local < CAP, rows_x, jnp.where(local < 2 * CAP, rows_c * gate_col, stats))
    value = jnp.where(local == 18, value + gain, value)
    for e in range(BLOCKS):
        piece = value[e * MSG : (e + 1) * MSG].astype(BF16)
        for y in range(4):
            out_ref[e, y] = piece


def selection(to, come):
    group = div(come, MSG)
    local = come - group * MSG
    pick = (local < CAP) & (to == group * CAP + local)
    pick |= (local >= CAP) & (local < 2 * CAP) & (to == SLOTS + group * CAP + local - CAP)
    pick |= (local == 18) & (to == 2 * SLOTS + group)
    return jnp.where(pick, 1.0, 0.0).astype(BF16)


def repack(in_ref, pick_ref, out_ref):
    pick = pick_ref[...]
    for y in range(4):
        rows = in_ref[:, y].astype(F32).reshape(ROWS, 128).astype(BF16)
        packed = dot_nn(pick, rows).astype(BF16)
        for x in range(4):
            out_ref[x, y] = packed


def slot_tables():
    slot = iota((SLOTS, 128), 0)
    return slot - div(slot, CAP) * CAP, iota((SLOTS, 128), 1)


def read_rows(in_ref):
    local, lane = slot_tables()
    expand = (div(iota((SLOTS, 16), 0), CAP) == iota((SLOTS, 16), 1)).astype(F32).astype(BF16)
    shift_lane = (lane == local) | (lane == local + 16)
    at = iota((128, 128), 0) - 32
    collect = (at >= 0) & (at < 24) & ((at & 7) == (iota((128, 128), 1) & 7))
    collect = jnp.where(collect, 1.0, 0.0).astype(BF16)
    ones = jnp.ones((128, 128), BF16)
    own = lax.shift_right_logical(iota((16, 128), 1), 3) == iota((16, 128), 0)
    blocks = [in_ref[i % 4, i // 4, 288:304] for i in range(16)]
    shifts = dot_nn(expand, jnp.concatenate(blocks, axis=1))
    gain_rows = dot_nn(jnp.concatenate(blocks, axis=0), collect)
    chunks = []
    gains = []
    total = jnp.zeros((SLOTS, 128), F32)
    for i in range(16):
        shift = jnp.where(shift_lane, shifts[:, i * 128 : i * 128 + 128], 0.0).astype(BF16)
        chunk = in_ref[i % 4, i // 4, 0:144].astype(F32) + dot_nn(shift, ones)
        total = total + chunk
        chunks.append(chunk)
        gain = jnp.where(own, gain_rows[i * 16 : i * 16 + 16], 0.0)
        gains.append(jnp.sum(gain, axis=0, keepdims=True))
    center = jnp.sum(total, axis=1, keepdims=True) / WIDTH
    squares = jnp.zeros((SLOTS, 128), F32)
    for i in range(16):
        chunks[i] = chunks[i] - center
        squares = squares + chunks[i] * chunks[i]
    inv_scale = lax.rsqrt(jnp.sum(squares, axis=1, keepdims=True) / WIDTH + 1e-05)
    rows = []
    for i in range(16):
        rows.append((chunks[i] * inv_scale * gains[i]).astype(BF16))
    return jnp.concatenate(rows, axis=1), jnp.concatenate(gains, axis=1), center, inv_scale


def ahead(in_ref, up, down):
    rows, gain, center, inv_scale = read_rows(in_ref)
    high, middle, low = split_three(jnp.broadcast_to(gain, (16, WIDTH)))
    row = iota((16, WIDTH), 0)
    gain = jnp.where(row == 0, high.astype(F32), middle.astype(F32))
    gain = jnp.where(row == 2, low.astype(F32), gain).astype(BF16)
    product = dot_nn(jnp.concatenate([rows, gain], axis=0), up)
    pre = product[0:SLOTS]
    weigh = product[SLOTS : SLOTS + 1] + product[SLOTS + 1 : SLOTS + 2]
    weigh = weigh + product[SLOTS + 2 : SLOTS + 3]
    bend = jnp.tanh(ROOT * (pre + CUBIC * pre * pre * pre))
    hidden = (0.5 * pre * (1.0 + bend)).astype(BF16)
    return pre, weigh, center, inv_scale, dot_nn(hidden, down).astype(BF16)


def behind(in_ref, up, down, pre, weigh, center, inv_scale):
    cots = [None] * 16
    for x in range(4):
        for y in range(4):
            cots[y * 4 + x] = in_ref[x, y, 144:288]
    grad_hidden = dot_nt(jnp.concatenate(cots, axis=1), down)
    bend = jnp.tanh(ROOT * (pre + CUBIC * pre * pre * pre))
    slope = 0.5 * (1.0 + bend) + 0.5 * pre * (1.0 - bend * bend) * (
        ROOT * (1.0 + 3.0 * CUBIC * pre * pre)
    )
    grad_act = (grad_hidden * slope).astype(BF16)
    wide = grad_act.astype(F32)
    sum_first = jnp.sum(wide * weigh, axis=1, keepdims=True)
    sum_second = jnp.sum(wide * pre, axis=1, keepdims=True)
    local, lane = slot_tables()
    spread = jnp.where(lane == local, sum_first, 0.0)
    spread = spread + jnp.where(lane == local + 16, sum_second, 0.0)
    spread = spread + jnp.where(lane == local + 32, center * (1.0 / 32), 0.0)
    spread = spread + jnp.where(lane == local + 48, inv_scale * (1.0 / 32), 0.0)
    high, low = split_two(spread)
    collect = (iota((16, SLOTS), 0) == div(iota((16, SLOTS), 1), CAP)).astype(F32).astype(BF16)
    high = dot_nn(collect, high)
    low = dot_nn(collect, low)
    stats = high + jnp.concatenate([low[:, 64:], low[:, :64]], axis=1)
    return dot_nt(grad_act, up).astype(BF16), stats.astype(BF16)


def both_ways(which_ref, in_ref, up_ref, down_ref, out_ref):
    up, down = up_ref[which_ref[0]], down_ref[which_ref[0]]
    pre, weigh, center, inv_scale, value = ahead(in_ref, up, down)
    grad_in, stats = behind(in_ref, up, down, pre, weigh, center, inv_scale)
    for x in range(4):
        for y in range(4):
            at = (y * 4 + x) * 128
            out_ref[x, y, 0:144] = value[:, at : at + 128]
            out_ref[x, y, 144:288] = grad_in[:, at : at + 128]
            out_ref[x, y, 288:304] = stats


def only_ahead(which_ref, in_ref, up_ref, down_ref, out_ref, pre_ref, weigh_ref, scalar_ref):
    up, down = up_ref[which_ref[0]], down_ref[which_ref[0]]
    pre, weigh, center, inv_scale, value = ahead(in_ref, up, down)
    pre_ref[...] = pre
    weigh_ref[...] = jnp.broadcast_to(weigh, (8, HID))
    lane = iota((SLOTS, 128), 1)
    scalar_ref[...] = jnp.where(lane == 0, center, inv_scale)
    for x in range(4):
        for y in range(4):
            at = (y * 4 + x) * 128
            out_ref[x, y] = value[:, at : at + 128]


def only_behind(
    which_ref, in_ref, up_ref, down_ref, pre_ref, weigh_ref, scalar_ref, out_ref
):
    up, down = up_ref[which_ref[0]], down_ref[which_ref[0]]
    center, inv_scale = scalar_ref[:, 0:1], scalar_ref[:, 1:2]
    grad_in, stats = behind(
        in_ref, up, down, pre_ref[...], weigh_ref[0:1], center, inv_scale
    )
    for x in range(4):
        for y in range(4):
            at = (y * 4 + x) * 128
            out_ref[x, y, 0:144] = grad_in[:, at : at + 128]
            out_ref[x, y, 144:160] = stats


def add_pair(value_ref, grad_ref, came_ref, out_ref):
    for x in range(4):
        for y in range(4):
            came = came_ref[x, y].astype(F32)
            out_ref[x, y, 0:144] = (value_ref[x, y].astype(F32) + came[0:144]).astype(BF16)
            grad = grad_ref[x, y].astype(F32)
            out_ref[x, y, 144:288] = (grad[0:144] + came[144:288]).astype(BF16)
            out_ref[x, y, 288:304] = part(join(grad[144:160] + came[288:304]))


def add_four(in_ref, drop_ref, out_ref):
    drop = drop_ref[...]
    for y in range(4):
        value = in_ref[0, y].astype(F32)
        for x in range(1, 4):
            value = value + in_ref[x, y].astype(F32)
        rows = jnp.concatenate([value[0:288].astype(BF16), part(join(value[288:304]))], axis=0)
        message = dot_nn(drop, rows)
        for e in range(BLOCKS):
            out_ref[e, y] = message[e * MSG : (e + 1) * MSG].astype(BF16)


def combine(in_ref, place_ref, gate_ref, out_ref):
    value = in_ref[:, 0].astype(F32)
    for y in range(1, 4):
        value = value + in_ref[:, y].astype(F32)
    stats = value[:, 18]
    stats = join(stats).reshape(BLOCKS, 1, 128)
    stats = jnp.broadcast_to(stats, (BLOCKS, MSG, 128)).reshape(ROWS, 128)
    value = value.reshape(ROWS, 128).astype(BF16)
    row = iota((ROWS, 128), 0)
    lane = iota((ROWS, 128), 1)
    local = row - div(row, MSG) * MSG
    forward = local < CAP
    place = place_ref[...].astype(F32)
    ahead_place = jnp.where(forward, place, 0.0)
    behind_place = jnp.where(forward, 0.0, place).astype(BF16)
    gate = jnp.where(forward, gate_ref[...], 0.0)
    out_ref[0:128] = dot_tn(value.astype(F32), gate, precision=HIGHEST)
    out_ref[128:256] = dot_tn(value, behind_place)
    for q in range(4):
        column = jnp.sum(jnp.where(lane == local + 16 * q, stats, 0.0), axis=1, keepdims=True)
        out_ref[256 + q : 257 + q] = jnp.sum(ahead_place * column, axis=0, keepdims=True)
    out_ref[260:264] = jnp.zeros((4, 128), F32)


def finish(
    core_ref, in_ref, stream_ref, side_ref, heads_ref, result_ref, grad_ref, pair_ref, gw_ref
):
    got = in_ref[0] + in_ref[1]
    stream = stream_ref[...]
    cot = side_ref[:, 2176:2304].astype(F32)
    gains = side_ref[:, 2304:2432].astype(F32)
    scaled = got[128:256] * (gains[:, 0:1] + gains[:, 1:2] + gains[:, 2:3])
    first = got[256:257] / WIDTH
    second = got[257:258] / WIDTH
    center = got[258:259] * 0.5
    inv_scale = got[259:260] * 0.5
    normal = (stream - center) * inv_scale
    grad = cot + inv_scale * (scaled - first - normal * second)
    result = stream + got[0:128]
    low = core_ref[0] == 0
    result_ref[...] = jnp.where(low, result[0:64], result[64:128]).astype(BF16)
    own = jnp.where(low, grad[0:64], grad[64:128]).astype(BF16)
    grad_ref[...] = own
    pair_ref[...] = grad.astype(BF16)
    for chip in range(16):
        heads = jnp.concatenate([heads_ref[0, chip], heads_ref[1, chip]], axis=0)
        gw_ref[chip] = dot_nt(own, heads).astype(BF16)


def heads_back(at_ref, pair_ref, weight_ref, keep_ref, send_ref):
    for k in range(4):
        for j in range(4):
            chip = (at_ref[1] ^ ORDER[j]) * 4 + (at_ref[0] ^ ORDER[k])
            out_ref = keep_ref if k < 2 else send_ref
            out_ref[k % 2, j] = dot_nn(weight_ref[chip], pair_ref[...]).astype(BF16)


def lay(in_ref, out_ref):
    for chip in range(16):
        out_ref[:, chip * 128 : chip * 128 + 128] = in_ref[chip]


def a2a(value, axes):
    return lax.all_to_all(value, axes, split_axis=0, concat_axis=0, tiled=True)


def halve(keep, send, axis):
    came = lax.ppermute(send, axis, [(i, i ^ 1) for i in range(4)])
    half = keep.astype(F32) + came.astype(F32)
    came = lax.ppermute(half[1].astype(BF16), axis, [(i, i ^ 2) for i in range(4)])
    return half[0], came


def total(value):
    return jnp.sum(value.astype(F32), axis=0)


def local(
    residual, heads_out, out_weight, norm_gain, up_weight, down_weight, routes, gates, cotangent
):
    core = lax.axis_index("c").astype(jnp.int32).reshape(1)
    block = lax.axis_index(EXPERT).astype(jnp.int32).reshape(1)
    swap = [(0, 1), (1, 0)]
    heads_t = a2a(jnp.broadcast_to(heads_out.T, (16, 64, 128)), ("yl", "x"))
    side = call(pack, shape((64, SIDE), BF16), "pack", 0, 4)(
        out_weight.T, residual.T, cotangent.T, norm_gain.reshape(64, 1)
    )
    side = lax.all_gather(side, "c", axis=0, tiled=True)
    place, gate, pick, drop = call(
        prepare,
        (
            shape((ROWS, 128), BF16),
            shape((ROWS, 128), F32),
            shape((PACK, ROWS), BF16),
            shape((ROWS, PACK), BF16),
        ),
        "prepare",
        1,
        2,
    )(core, routes.T, gates.T)
    turned = call(turn_weight, shape((16, 64, 128), BF16), "turn_weight", 1, 1)(core, side)
    heads_t, turned = lax.optimization_barrier((heads_t, turned))
    heads_t = lax.all_gather(heads_t, "c", axis=0)
    stream, message = call(
        dispatch, (shape((128, 128), F32), shape((BLOCKS, 4, MSG, 128), BF16)), "dispatch", 1, 4
    )(block, heads_t, side, place, gate)
    message = a2a(message.reshape(64, MSG, 128), ("yh", "z", "yl"))
    packed = call(repack, shape((4, 4, PACK, 128), BF16), "repack", 0, 2)(
        message.reshape(BLOCKS, 4, MSG, 128), pick
    )
    mine = a2a(packed, "x")
    other = lax.ppermute(mine, "c", swap)
    value, pre, weigh, scalars = call(
        only_ahead,
        (
            shape((4, 4, SLOTS, 128), BF16),
            shape((SLOTS, HID), F32),
            shape((8, HID), F32),
            shape((SLOTS, 128), F32),
        ),
        "only_ahead",
        1,
        3,
    )(core, mine, up_weight, down_weight)
    sent = call(both_ways, shape((4, 4, PACK, 128), BF16), "both_ways", 1, 3)(
        1 - core, other, up_weight, down_weight
    )
    sent, pre = lax.optimization_barrier((sent, pre))
    came = lax.ppermute(sent, "c", swap)
    grad = call(only_behind, shape((4, 4, SLOTS + 16, 128), BF16), "only_behind", 1, 6)(
        core, mine, up_weight, down_weight, pre, weigh, scalars
    )
    summed = call(add_pair, shape((4, 4, PACK, 128), BF16), "add_pair", 0, 3)(value, grad, came)
    summed = a2a(summed, "x")
    message = call(add_four, shape((BLOCKS, 4, MSG, 128), BF16), "add_four", 0, 2)(
        summed, drop
    )
    message = a2a(message.reshape(64, MSG, 128), ("yh", "z", "yl"))
    both = call(combine, shape((264, 128), F32), "combine", 0, 3)(
        message.reshape(BLOCKS, 4, MSG, 128), place, gate
    )
    both = lax.all_gather(both, "c", axis=0)
    result, grad_residual, grad_pair, grad_weight = call(
        finish,
        (
            shape((64, 128), BF16),
            shape((64, 128), BF16),
            shape((128, 128), BF16),
            shape((16, 64, 128), BF16),
        ),
        "finish",
        1,
        4,
    )(core, both, stream, side, heads_t)
    grad_weight = total(a2a(grad_weight, EXPERT)).astype(BF16)
    at = jnp.stack([lax.axis_index("x"), lax.axis_index("yl")]).astype(jnp.int32)
    keep, send = call(heads_back, (shape((2, 4, 64, 128), BF16),) * 2, "heads_back", 1, 2)(
        at, grad_pair, turned
    )
    pieces = halve(keep, send, "x")
    grad_weight = jnp.broadcast_to(grad_weight, (16, 64, 128))
    grad_weight, pieces = lax.optimization_barrier((grad_weight, pieces))
    grad_weight = a2a(grad_weight, EXPERT)
    grad_weight = call(lay, shape((64, WIDTH), BF16), "lay", 0, 1)(grad_weight)
    heads_sum = (pieces[0] + pieces[1].astype(F32)).astype(BF16)
    pieces = halve(heads_sum[0:2], heads_sum[2:4], "yl")
    grad_heads = (pieces[0] + pieces[1].astype(F32)).astype(BF16).T
    return (result.T, grad_residual.T, grad_heads, grad_weight.T)


def solution(mesh):
    view = Mesh(mesh.devices.reshape(SPLIT), AXES)
    return jax.shard_map(
        local,
        mesh=view,
        in_specs=(
            P(EXPERT, TENSOR),
            P(EXPERT, TENSOR),
            P(None, TENSOR),
            P(TENSOR),
            P(EXPERT, None, TENSOR),
            P(EXPERT, TENSOR, None),
            P(EXPERT, None),
            P(EXPERT, None),
            P(EXPERT, TENSOR),
        ),
        out_specs=(
            P(EXPERT, TENSOR),
            P(EXPERT, TENSOR),
            P(EXPERT, TENSOR),
            P(None, TENSOR),
        ),
        check_vma=False,
    )
```

```python
import jax
import jax.numpy as jnp
from jax import lax
from jax.experimental import pallas as pl
from jax.experimental.pallas import tpu as pltpu
from jax.sharding import Mesh, PartitionSpec as P

AXES = ("yh", "z", "yl", "x", "c")
EXPERT = ("yh", "z")
TENSOR = ("yl", "x", "c")
SPLIT = (2, 8, 4, 4, 2)
BLOCKS = 16
CAP = 9
MSG = 24
ORDER = (0, 2, 1, 3)
PACK = 304
SLOTS = BLOCKS * CAP
SIDE = 2432
ROWS = BLOCKS * MSG
WIDTH = 2048
HID = 256
F32 = jnp.float32
BF16 = jnp.bfloat16
HIGHEST = lax.Precision.HIGHEST
ROOT = 0.7978845608028654
CUBIC = 0.044715


def iota(shape, axis):
    return lax.broadcasted_iota(jnp.int32, shape, axis)


def div(value, by):
    scale = -(-(1 << 14) // by)
    return lax.shift_right_logical(value * scale, 14)


def dot_nn(a, b, **kw):
    return lax.dot_general(a, b, (((1,), (0,)), ((), ())), preferred_element_type=F32, **kw)


def dot_nt(a, b, **kw):
    return lax.dot_general(a, b, (((1,), (1,)), ((), ())), preferred_element_type=F32, **kw)


def dot_tn(a, b, **kw):
    return lax.dot_general(a, b, (((0,), (0,)), ((), ())), preferred_element_type=F32, **kw)


def eye(n):
    return (iota((n, n), 0) == iota((n, n), 1)).astype(F32).astype(BF16)


def call(kernel, outs, name, n_smem, n_in):
    return pl.pallas_call(
        kernel,
        out_shape=outs,
        in_specs=[pl.BlockSpec(memory_space=pltpu.SMEM)] * n_smem
        + [pl.BlockSpec(memory_space=pltpu.VMEM)] * n_in,
        out_specs=jax.tree.map(lambda _: pl.BlockSpec(memory_space=pltpu.VMEM), outs),
        name=name,
        compiler_params=pltpu.CompilerParams(vmem_limit_bytes=16 * 1024 * 1024),
    )


def shape(dims, dtype):
    return jax.ShapeDtypeStruct(dims, dtype)


def split_three(value):
    high = value.astype(BF16)
    rest = value - high.astype(F32)
    middle = rest.astype(BF16)
    return high, middle, (rest - middle.astype(F32)).astype(BF16)


def split_two(value):
    high = value.astype(BF16)
    low = (value - high.astype(F32)).astype(BF16)
    return high, low


def join(block):
    return block + jnp.concatenate([block[:, 64:], block[:, :64]], axis=1)


def part(value):
    high, low = split_two(value)
    lane = iota(value.shape, 1)
    return jnp.where(lane < 64, high.astype(F32), low.astype(F32)).astype(BF16)


def prepare(
    core_ref, wide_ref, small_ref, side_ref, place_ref, gate_ref, pick_ref, drop_ref
):
    side_ref[:, 0:2304] = wide_ref[...]
    pick = iota((PACK, ROWS), 0) == packed_row(iota((8, ROWS), 1))[0:1]
    pick_ref[...] = jnp.where(pick, 1.0, 0.0).astype(BF16)
    drop = iota((ROWS, PACK), 1) == packed_row(iota((ROWS, 128), 0))[:, 0:1]
    drop_ref[...] = jnp.where(drop, 1.0, 0.0).astype(BF16)
    routes = small_ref[0:2].astype(jnp.int32)
    gates = small_ref[2:4]
    core = core_ref[0]
    row = iota((ROWS, 128), 0)
    group = div(row, MSG)
    local = row - group * MSG
    slot = jnp.where(local < CAP, local, local - CAP)
    used = local < 2 * CAP
    expert = 2 * group + core
    first = (routes[0:1, :] == expert) & used
    second = (routes[1:2, :] == expert) & used
    named = jnp.where(first | second, 1.0, 0.0)
    before = (iota((128, 128), 0) < iota((128, 128), 1)).astype(F32).astype(BF16)
    earlier = dot_nn(named.astype(BF16), before)
    taken = (earlier == slot.astype(F32)) & (named > 0.5)
    place_ref[...] = jnp.where(taken, 1.0, 0.0).astype(BF16)
    gate = jnp.where(first, gates[0:1, :], gates[1:2, :])
    gate_ref[...] = jnp.where(taken, gate, 0.0)
    own = iota((64, 64), 0) == iota((64, 64), 1)
    gain = jnp.sum(jnp.where(own, small_ref[4:5, 0:64], 0.0), axis=1, keepdims=True)
    high, middle, low = split_three(jnp.broadcast_to(gain, (64, 128)))
    lane = iota((64, 128), 1)
    value = jnp.where(lane == 0, high.astype(F32), middle.astype(F32))
    side_ref[:, 2304:2432] = jnp.where(lane == 2, low.astype(F32), value).astype(BF16)


def turn_weight(core_ref, side_ref, out_ref):
    mirror = eye(128)
    for chip in range(16):
        turned = dot_nt(mirror, side_ref[:, chip * 128 : chip * 128 + 128])
        out_ref[chip] = jnp.where(core_ref[0] == 0, turned[0:64], turned[64:128]).astype(BF16)


def dispatch(block_ref, heads_ref, side_ref, place_ref, gate_ref, stream_ref, out_ref):
    pieces = []
    for chip in range(16):
        pieces.append(heads_ref[0, chip])
        pieces.append(heads_ref[1, chip])
    mixed = dot_nn(side_ref[:, 0:2048], jnp.concatenate(pieces, axis=0))
    stream = side_ref[:, 2048:2176].astype(F32) + mixed
    stream_ref[...] = stream
    shift = jnp.mean(stream, axis=0, keepdims=True)
    centered = (stream - shift).astype(BF16)
    place = place_ref[...]
    placed = place.astype(F32)
    rows_x = dot_nt(place, centered)
    rows_c = dot_nt(place, side_ref[:, 2176:2304])
    gate_col = jnp.sum(gate_ref[...], axis=1, keepdims=True)
    shift_col = jnp.sum(placed * shift, axis=1, keepdims=True)
    row = iota((ROWS, 128), 0)
    lane = iota((ROWS, 128), 1)
    local = row - div(row, MSG) * MSG
    high, low = split_two(shift_col)
    spread = jnp.where(lane == local, high.astype(F32), 0.0)
    spread = spread + jnp.where(lane == local + 16, low.astype(F32), 0.0)
    spread = jnp.where(local < CAP, spread, 0.0).astype(BF16)
    to = iota((ROWS, ROWS), 0)
    come = iota((ROWS, ROWS), 1)
    to_group = div(to, MSG)
    gather = (to - to_group * MSG == 18) & (to_group == div(come, MSG))
    stats = dot_nn(jnp.where(gather, 1.0, 0.0).astype(BF16), spread)
    feature = iota((128, 128), 0)
    at = iota((128, 128), 1) - 32
    which = lax.shift_right_logical(jnp.maximum(at, 0), 3)
    mine = (at >= 0) & (at < 24) & (feature == 8 * block_ref[0] + (at & 7))
    gains = side_ref[:, 2304:2432].astype(F32)
    gain = jnp.where(which == 0, gains[:, 0:1], jnp.where(which == 1, gains[:, 1:2], gains[:, 2:3]))
    gain = jnp.sum(jnp.where(mine, gain, 0.0), axis=0, keepdims=True)
    value = jnp.where(local < CAP, rows_x, jnp.where(local < 2 * CAP, rows_c * gate_col, stats))
    value = jnp.where(local == 18, value + gain, value)
    for e in range(BLOCKS):
        piece = value[e * MSG : (e + 1) * MSG].astype(BF16)
        for y in range(4):
            out_ref[e, y] = piece


def packed_row(come):
    group = div(come, MSG)
    local = come - group * MSG
    to = jnp.where(local < CAP, group * CAP + local, SLOTS + group * CAP + local - CAP)
    return jnp.where(local < 2 * CAP, to, jnp.where(local == 18, 2 * SLOTS + group, -1))


def repack(in_ref, pick_ref, out_ref):
    pick = pick_ref[...]
    for y in range(4):
        rows = in_ref[:, y].astype(F32).reshape(ROWS, 128).astype(BF16)
        packed = dot_nn(pick, rows).astype(BF16)
        for x in range(4):
            out_ref[x, y] = packed


def slot_tables():
    slot = iota((SLOTS, 128), 0)
    return slot - div(slot, CAP) * CAP, iota((SLOTS, 128), 1)


def read_rows(in_ref):
    local, lane = slot_tables()
    expand = (div(iota((SLOTS, 16), 0), CAP) == iota((SLOTS, 16), 1)).astype(F32).astype(BF16)
    shift_lane = (lane == local) | (lane == local + 16)
    at = iota((128, 128), 0) - 32
    collect = (at >= 0) & (at < 24) & ((at & 7) == (iota((128, 128), 1) & 7))
    collect = jnp.where(collect, 1.0, 0.0).astype(BF16)
    ones = jnp.ones((128, 128), BF16)
    own = lax.shift_right_logical(iota((16, 128), 1), 3) == iota((16, 128), 0)
    blocks = [in_ref[i % 4, i // 4, 288:304] for i in range(16)]
    shifts = dot_nn(expand, jnp.concatenate(blocks, axis=1))
    gain_rows = dot_nn(jnp.concatenate(blocks, axis=0), collect)
    chunks = []
    gains = []
    total = jnp.zeros((SLOTS, 128), F32)
    squares = jnp.zeros((SLOTS, 128), F32)
    for i in range(16):
        shift = jnp.where(shift_lane, shifts[:, i * 128 : i * 128 + 128], 0.0).astype(BF16)
        chunk = in_ref[i % 4, i // 4, 0:144].astype(F32) + dot_nn(shift, ones)
        total = total + chunk
        squares = squares + chunk * chunk
        chunks.append(chunk)
        gain = jnp.where(own, gain_rows[i * 16 : i * 16 + 16], 0.0)
        gains.append(jnp.sum(gain, axis=0, keepdims=True))
    center = jnp.sum(total, axis=1, keepdims=True) / WIDTH
    variance = jnp.sum(squares, axis=1, keepdims=True) / WIDTH - center * center
    inv_scale = lax.rsqrt(variance + 1e-05)
    rows = []
    for i in range(16):
        rows.append(((chunks[i] - center) * inv_scale * gains[i]).astype(BF16))
    return jnp.concatenate(rows, axis=1), jnp.concatenate(gains, axis=1), center, inv_scale


def ahead(in_ref, up, down):
    rows, gain, center, inv_scale = read_rows(in_ref)
    high, middle, low = split_three(jnp.broadcast_to(gain, (16, WIDTH)))
    row = iota((16, WIDTH), 0)
    gain = jnp.where(row == 0, high.astype(F32), middle.astype(F32))
    gain = jnp.where(row == 2, low.astype(F32), gain).astype(BF16)
    product = dot_nn(jnp.concatenate([rows, gain], axis=0), up)
    pre = product[0:SLOTS]
    weigh = product[SLOTS : SLOTS + 1] + product[SLOTS + 1 : SLOTS + 2]
    weigh = weigh + product[SLOTS + 2 : SLOTS + 3]
    bend = jnp.tanh(ROOT * (pre + CUBIC * pre * pre * pre))
    hidden = (0.5 * pre * (1.0 + bend)).astype(BF16)
    return pre, weigh, center, inv_scale, dot_nn(hidden, down).astype(BF16)


def behind(in_ref, up, down, pre, weigh, center, inv_scale):
    cots = [None] * 16
    for x in range(4):
        for y in range(4):
            cots[y * 4 + x] = in_ref[x, y, 144:288]
    grad_hidden = dot_nt(jnp.concatenate(cots, axis=1), down)
    bend = jnp.tanh(ROOT * (pre + CUBIC * pre * pre * pre))
    slope = 0.5 * (1.0 + bend) + 0.5 * pre * (1.0 - bend * bend) * (
        ROOT * (1.0 + 3.0 * CUBIC * pre * pre)
    )
    grad_act = (grad_hidden * slope).astype(BF16)
    wide = grad_act.astype(F32)
    sum_first = jnp.sum(wide * weigh, axis=1, keepdims=True)
    sum_second = jnp.sum(wide * pre, axis=1, keepdims=True)
    local, lane = slot_tables()
    spread = jnp.where(lane == local, sum_first, 0.0)
    spread = spread + jnp.where(lane == local + 16, sum_second, 0.0)
    spread = spread + jnp.where(lane == local + 32, center * (1.0 / 32), 0.0)
    spread = spread + jnp.where(lane == local + 48, inv_scale * (1.0 / 32), 0.0)
    high, low = split_two(spread)
    collect = (iota((16, SLOTS), 0) == div(iota((16, SLOTS), 1), CAP)).astype(F32).astype(BF16)
    high = dot_nn(collect, high)
    low = dot_nn(collect, low)
    stats = high + jnp.concatenate([low[:, 64:], low[:, :64]], axis=1)
    return dot_nt(grad_act, up).astype(BF16), stats.astype(BF16)


def both_ways(which_ref, in_ref, up_ref, down_ref, out_ref):
    up, down = up_ref[which_ref[0]], down_ref[which_ref[0]]
    pre, weigh, center, inv_scale, value = ahead(in_ref, up, down)
    grad_in, stats = behind(in_ref, up, down, pre, weigh, center, inv_scale)
    for x in range(4):
        for y in range(4):
            at = (y * 4 + x) * 128
            out_ref[x, y, 0:144] = value[:, at : at + 128]
            out_ref[x, y, 144:288] = grad_in[:, at : at + 128]
            out_ref[x, y, 288:304] = stats


def only_ahead(which_ref, in_ref, up_ref, down_ref, out_ref, pre_ref, weigh_ref, scalar_ref):
    up, down = up_ref[which_ref[0]], down_ref[which_ref[0]]
    pre, weigh, center, inv_scale, value = ahead(in_ref, up, down)
    pre_ref[...] = pre
    weigh_ref[...] = jnp.broadcast_to(weigh, (8, HID))
    lane = iota((SLOTS, 128), 1)
    scalar_ref[...] = jnp.where(lane == 0, center, inv_scale)
    for x in range(4):
        for y in range(4):
            at = (y * 4 + x) * 128
            out_ref[x, y] = value[:, at : at + 128]


def only_behind(
    which_ref, in_ref, up_ref, down_ref, pre_ref, weigh_ref, scalar_ref, out_ref
):
    up, down = up_ref[which_ref[0]], down_ref[which_ref[0]]
    center, inv_scale = scalar_ref[:, 0:1], scalar_ref[:, 1:2]
    grad_in, stats = behind(
        in_ref, up, down, pre_ref[...], weigh_ref[0:1], center, inv_scale
    )
    for x in range(4):
        for y in range(4):
            at = (y * 4 + x) * 128
            out_ref[x, y, 0:144] = grad_in[:, at : at + 128]
            out_ref[x, y, 144:160] = stats


def add_pair(value_ref, grad_ref, came_ref, out_ref):
    for x in range(4):
        for y in range(4):
            came = came_ref[x, y].astype(F32)
            out_ref[x, y, 0:144] = (value_ref[x, y].astype(F32) + came[0:144]).astype(BF16)
            grad = grad_ref[x, y].astype(F32)
            out_ref[x, y, 144:288] = (grad[0:144] + came[144:288]).astype(BF16)
            out_ref[x, y, 288:304] = part(join(grad[144:160] + came[288:304]))


def add_four(in_ref, drop_ref, out_ref):
    drop = drop_ref[...]
    for y in range(4):
        value = in_ref[0, y].astype(F32)
        for x in range(1, 4):
            value = value + in_ref[x, y].astype(F32)
        rows = jnp.concatenate([value[0:288].astype(BF16), part(join(value[288:304]))], axis=0)
        message = dot_nn(drop, rows)
        for e in range(BLOCKS):
            out_ref[e, y] = message[e * MSG : (e + 1) * MSG].astype(BF16)


def combine(in_ref, place_ref, gate_ref, out_ref):
    value = in_ref[:, 0].astype(F32)
    for y in range(1, 4):
        value = value + in_ref[:, y].astype(F32)
    stats = value[:, 18]
    stats = join(stats).reshape(BLOCKS, 1, 128)
    stats = jnp.broadcast_to(stats, (BLOCKS, MSG, 128)).reshape(ROWS, 128)
    value = value.reshape(ROWS, 128).astype(BF16)
    row = iota((ROWS, 128), 0)
    lane = iota((ROWS, 128), 1)
    local = row - div(row, MSG) * MSG
    forward = local < CAP
    place = place_ref[...].astype(F32)
    ahead_place = jnp.where(forward, place, 0.0)
    behind_place = jnp.where(forward, 0.0, place).astype(BF16)
    gate = jnp.where(forward, gate_ref[...], 0.0)
    out_ref[0:128] = dot_tn(value.astype(F32), gate, precision=HIGHEST)
    out_ref[128:256] = dot_tn(value, behind_place)
    for q in range(4):
        column = jnp.sum(jnp.where(lane == local + 16 * q, stats, 0.0), axis=1, keepdims=True)
        out_ref[256 + q : 257 + q] = jnp.sum(ahead_place * column, axis=0, keepdims=True)
    out_ref[260:264] = jnp.zeros((4, 128), F32)


def finish(
    core_ref, in_ref, stream_ref, side_ref, heads_ref, result_ref, grad_ref, pair_ref, gw_ref
):
    got = in_ref[0] + in_ref[1]
    stream = stream_ref[...]
    cot = side_ref[:, 2176:2304].astype(F32)
    gains = side_ref[:, 2304:2432].astype(F32)
    scaled = got[128:256] * (gains[:, 0:1] + gains[:, 1:2] + gains[:, 2:3])
    first = got[256:257] / WIDTH
    second = got[257:258] / WIDTH
    center = got[258:259] * 0.5
    inv_scale = got[259:260] * 0.5
    normal = (stream - center) * inv_scale
    grad = cot + inv_scale * (scaled - first - normal * second)
    result = stream + got[0:128]
    low = core_ref[0] == 0
    result_ref[...] = jnp.where(low, result[0:64], result[64:128]).astype(BF16)
    own = jnp.where(low, grad[0:64], grad[64:128]).astype(BF16)
    grad_ref[...] = own
    pair_ref[...] = grad.astype(BF16)
    for chip in range(16):
        heads = jnp.concatenate([heads_ref[0, chip], heads_ref[1, chip]], axis=0)
        gw_ref[chip] = dot_nt(own, heads).astype(BF16)


def heads_back(at_ref, pair_ref, weight_ref, keep_ref, send_ref):
    for k in range(4):
        for j in range(4):
            chip = (at_ref[1] ^ ORDER[j]) * 4 + (at_ref[0] ^ ORDER[k])
            out_ref = keep_ref if k < 2 else send_ref
            out_ref[k % 2, j] = dot_nn(weight_ref[chip], pair_ref[...]).astype(BF16)


def lay(in_ref, out_ref):
    for chip in range(16):
        out_ref[:, chip * 128 : chip * 128 + 128] = in_ref[chip]


def a2a(value, axes):
    return lax.all_to_all(value, axes, split_axis=0, concat_axis=0, tiled=True)


def halve(keep, send, axis):
    came = lax.ppermute(send, axis, [(i, i ^ 1) for i in range(4)])
    half = keep.astype(F32) + came.astype(F32)
    came = lax.ppermute(half[1].astype(BF16), axis, [(i, i ^ 2) for i in range(4)])
    return half[0], came


def total(value):
    return jnp.sum(value.astype(F32), axis=0)


def local(
    residual, heads_out, out_weight, norm_gain, up_weight, down_weight, routes, gates, cotangent
):
    core = lax.axis_index("c").astype(jnp.int32).reshape(1)
    block = lax.axis_index(EXPERT).astype(jnp.int32).reshape(1)
    swap = [(0, 1), (1, 0)]
    heads_t = a2a(jnp.broadcast_to(heads_out.T, (16, 64, 128)), ("yl", "x"))
    wide = jnp.concatenate([out_weight.T, residual.T, cotangent.T], axis=1)
    small = jnp.concatenate(
        [routes.T.astype(F32), gates.T, jnp.pad(norm_gain, (0, 64)).reshape(1, 128)], axis=0
    )
    side, place, gate, pick, drop = call(
        prepare,
        (
            shape((64, SIDE), BF16),
            shape((ROWS, 128), BF16),
            shape((ROWS, 128), F32),
            shape((PACK, ROWS), BF16),
            shape((ROWS, PACK), BF16),
        ),
        "prepare",
        1,
        2,
    )(core, wide, small)
    side = lax.all_gather(side, "c", axis=0, tiled=True)
    turned = call(turn_weight, shape((16, 64, 128), BF16), "turn_weight", 1, 1)(core, side)
    at = jnp.stack([lax.axis_index("x"), lax.axis_index("yl")]).astype(jnp.int32)
    heads_t, turned, at = lax.optimization_barrier((heads_t, turned, at))
    heads_t = lax.all_gather(heads_t, "c", axis=0)
    stream, message = call(
        dispatch, (shape((128, 128), F32), shape((BLOCKS, 4, MSG, 128), BF16)), "dispatch", 1, 4
    )(block, heads_t, side, place, gate)
    message = a2a(message.reshape(64, MSG, 128), ("yh", "z", "yl"))
    packed = call(repack, shape((4, 4, PACK, 128), BF16), "repack", 0, 2)(
        message.reshape(BLOCKS, 4, MSG, 128), pick
    )
    mine = a2a(packed, "x")
    other = lax.ppermute(mine, "c", swap)
    value, pre, weigh, scalars = call(
        only_ahead,
        (
            shape((4, 4, SLOTS, 128), BF16),
            shape((SLOTS, HID), F32),
            shape((8, HID), F32),
            shape((SLOTS, 128), F32),
        ),
        "only_ahead",
        1,
        3,
    )(core, mine, up_weight, down_weight)
    sent = call(both_ways, shape((4, 4, PACK, 128), BF16), "both_ways", 1, 3)(
        1 - core, other, up_weight, down_weight
    )
    sent, pre = lax.optimization_barrier((sent, pre))
    came = lax.ppermute(sent, "c", swap)
    grad = call(only_behind, shape((4, 4, SLOTS + 16, 128), BF16), "only_behind", 1, 6)(
        core, mine, up_weight, down_weight, pre, weigh, scalars
    )
    summed = call(add_pair, shape((4, 4, PACK, 128), BF16), "add_pair", 0, 3)(value, grad, came)
    summed = a2a(summed, "x")
    message = call(add_four, shape((BLOCKS, 4, MSG, 128), BF16), "add_four", 0, 2)(
        summed, drop
    )
    message = a2a(message.reshape(64, MSG, 128), ("yh", "z", "yl"))
    both = call(combine, shape((264, 128), F32), "combine", 0, 3)(
        message.reshape(BLOCKS, 4, MSG, 128), place, gate
    )
    both = lax.all_gather(both, "c", axis=0)
    result, grad_residual, grad_pair, grad_weight = call(
        finish,
        (
            shape((64, 128), BF16),
            shape((64, 128), BF16),
            shape((128, 128), BF16),
            shape((16, 64, 128), BF16),
        ),
        "finish",
        1,
        4,
    )(core, both, stream, side, heads_t)
    grad_weight = total(a2a(grad_weight, EXPERT)).astype(BF16)
    keep, send = call(heads_back, (shape((2, 4, 64, 128), BF16),) * 2, "heads_back", 1, 2)(
        at, grad_pair, turned
    )
    pieces = halve(keep, send, "x")
    grad_weight = jnp.broadcast_to(grad_weight, (16, 64, 128))
    grad_weight = a2a(grad_weight, EXPERT)
    grad_weight = call(lay, shape((64, WIDTH), BF16), "lay", 0, 1)(grad_weight)
    heads_sum = (pieces[0] + pieces[1].astype(F32)).astype(BF16)
    pieces = halve(heads_sum[0:2], heads_sum[2:4], "yl")
    grad_heads = (pieces[0] + pieces[1].astype(F32)).astype(BF16).T
    return (result.T, grad_residual.T, grad_heads, grad_weight.T)


def solution(mesh):
    view = Mesh(mesh.devices.reshape(SPLIT), AXES)
    return jax.shard_map(
        local,
        mesh=view,
        in_specs=(
            P(EXPERT, TENSOR),
            P(EXPERT, TENSOR),
            P(None, TENSOR),
            P(TENSOR),
            P(EXPERT, None, TENSOR),
            P(EXPERT, TENSOR, None),
            P(EXPERT, None),
            P(EXPERT, None),
            P(EXPERT, TENSOR),
        ),
        out_specs=(
            P(EXPERT, TENSOR),
            P(EXPERT, TENSOR),
            P(EXPERT, TENSOR),
            P(None, TENSOR),
        ),
        check_vma=False,
    )
```

```python
import jax
import jax.numpy as jnp
from jax import lax
from jax.experimental import pallas as pl
from jax.experimental.pallas import tpu as pltpu
from jax.sharding import Mesh, PartitionSpec as P

AXES = ("yh", "z", "yl", "x", "c")
EXPERT = ("yh", "z")
TENSOR = ("yl", "x", "c")
SPLIT = (2, 8, 4, 4, 2)
BLOCKS = 16
CAP = 9
MSG = 20
ORDER = (0, 2, 1, 3)
PACK = 304
SLOTS = BLOCKS * CAP
SIDE = 2432
ROWS = BLOCKS * MSG
WIDTH = 2048
HID = 256
F32 = jnp.float32
BF16 = jnp.bfloat16
HIGHEST = lax.Precision.HIGHEST
ROOT = 0.7978845608028654
CUBIC = 0.044715


def iota(shape, axis):
    return lax.broadcasted_iota(jnp.int32, shape, axis)


def div(value, by):
    scale = -(-(1 << 14) // by)
    return lax.shift_right_logical(value * scale, 14)


def dot_nn(a, b, **kw):
    return lax.dot_general(a, b, (((1,), (0,)), ((), ())), preferred_element_type=F32, **kw)


def dot_nt(a, b, **kw):
    return lax.dot_general(a, b, (((1,), (1,)), ((), ())), preferred_element_type=F32, **kw)


def dot_tn(a, b, **kw):
    return lax.dot_general(a, b, (((0,), (0,)), ((), ())), preferred_element_type=F32, **kw)


def eye(n):
    return (iota((n, n), 0) == iota((n, n), 1)).astype(F32).astype(BF16)


def call(kernel, outs, name, n_smem, n_in):
    return pl.pallas_call(
        kernel,
        out_shape=outs,
        in_specs=[pl.BlockSpec(memory_space=pltpu.SMEM)] * n_smem
        + [pl.BlockSpec(memory_space=pltpu.VMEM)] * n_in,
        out_specs=jax.tree.map(lambda _: pl.BlockSpec(memory_space=pltpu.VMEM), outs),
        name=name,
        compiler_params=pltpu.CompilerParams(vmem_limit_bytes=16 * 1024 * 1024),
    )


def shape(dims, dtype):
    return jax.ShapeDtypeStruct(dims, dtype)


def split_three(value):
    high = value.astype(BF16)
    rest = value - high.astype(F32)
    middle = rest.astype(BF16)
    return high, middle, (rest - middle.astype(F32)).astype(BF16)


def split_two(value):
    high = value.astype(BF16)
    low = (value - high.astype(F32)).astype(BF16)
    return high, low


def join(block):
    return block + jnp.concatenate([block[:, 64:], block[:, :64]], axis=1)


def part(value):
    high, low = split_two(value)
    lane = iota(value.shape, 1)
    return jnp.where(lane < 64, high.astype(F32), low.astype(F32)).astype(BF16)


def row_place(row):
    return row & 15, lax.shift_right_logical(row, 4)


def write_messages(out_ref, value, ways):
    for i in range(MSG // 2):
        at = i * 32
        pair = jnp.stack([value[at : at + 16], value[at + 16 : at + 32]], axis=1).astype(BF16)
        for y in ways:
            out_ref[:, y, :, i * 128 : i * 128 + 128] = pair


def read_messages(in_ref, ways):
    rows = []
    for i in range(MSG // 2):
        pair = None
        for y in ways:
            came = in_ref[:, y, :, i * 128 : i * 128 + 128].astype(F32)
            pair = came if pair is None else pair + came
        rows.extend([pair[:, 0], pair[:, 1]])
    return jnp.concatenate(rows, axis=0)


def prepare(
    core_ref, wide_ref, small_ref, side_ref, place_ref, gate_ref, pick_ref, drop_ref
):
    side_ref[:, 0:2304] = wide_ref[...]
    pick = iota((PACK, ROWS), 0) == packed_row(iota((8, ROWS), 1))[0:1]
    pick_ref[...] = jnp.where(pick, 1.0, 0.0).astype(BF16)
    drop = iota((ROWS, PACK), 1) == packed_row(iota((ROWS, 128), 0))[:, 0:1]
    drop_ref[...] = jnp.where(drop, 1.0, 0.0).astype(BF16)
    routes = small_ref[0:2].astype(jnp.int32)
    gates = small_ref[2:4]
    core = core_ref[0]
    row = iota((ROWS, 128), 0)
    group, local = row_place(row)
    slot = jnp.where(local < CAP, local, local - CAP)
    used = local < 2 * CAP
    expert = 2 * group + core
    first = (routes[0:1, :] == expert) & used
    second = (routes[1:2, :] == expert) & used
    named = jnp.where(first | second, 1.0, 0.0)
    before = (iota((128, 128), 0) < iota((128, 128), 1)).astype(F32).astype(BF16)
    earlier = dot_nn(named.astype(BF16), before)
    taken = (earlier == slot.astype(F32)) & (named > 0.5)
    place_ref[...] = jnp.where(taken, 1.0, 0.0).astype(BF16)
    gate = jnp.where(first, gates[0:1, :], gates[1:2, :])
    gate_ref[...] = jnp.where(taken, gate, 0.0)
    own = iota((64, 64), 0) == iota((64, 64), 1)
    gain = jnp.sum(jnp.where(own, small_ref[4:5, 0:64], 0.0), axis=1, keepdims=True)
    high, middle, low = split_three(jnp.broadcast_to(gain, (64, 128)))
    lane = iota((64, 128), 1)
    value = jnp.where(lane == 0, high.astype(F32), middle.astype(F32))
    side_ref[:, 2304:2432] = jnp.where(lane == 2, low.astype(F32), value).astype(BF16)


def turn_weight(core_ref, side_ref, out_ref):
    mirror = eye(128)
    for chip in range(16):
        turned = dot_nt(mirror, side_ref[:, chip * 128 : chip * 128 + 128])
        out_ref[chip] = jnp.where(core_ref[0] == 0, turned[0:64], turned[64:128]).astype(BF16)


def dispatch(block_ref, heads_ref, side_ref, place_ref, gate_ref, stream_ref, out_ref):
    pieces = []
    for chip in range(16):
        pieces.append(heads_ref[0, chip])
        pieces.append(heads_ref[1, chip])
    mixed = dot_nn(side_ref[:, 0:2048], jnp.concatenate(pieces, axis=0))
    stream = side_ref[:, 2048:2176].astype(F32) + mixed
    stream_ref[...] = stream
    shift = jnp.mean(stream, axis=0, keepdims=True)
    centered = (stream - shift).astype(BF16)
    place = place_ref[...]
    placed = place.astype(F32)
    rows_x = dot_nt(place, centered)
    rows_c = dot_nt(place, side_ref[:, 2176:2304])
    gate_col = jnp.sum(gate_ref[...], axis=1, keepdims=True)
    shift_col = jnp.sum(placed * shift, axis=1, keepdims=True)
    row = iota((ROWS, 128), 0)
    lane = iota((ROWS, 128), 1)
    local = row_place(row)[1]
    high, low = split_two(shift_col)
    spread = jnp.where(lane == local, high.astype(F32), 0.0)
    spread = spread + jnp.where(lane == local + 16, low.astype(F32), 0.0)
    spread = jnp.where(local < CAP, spread, 0.0).astype(BF16)
    to_group, to_local = row_place(iota((ROWS, ROWS), 0))
    gather = (to_local == 18) & (to_group == row_place(iota((ROWS, ROWS), 1))[0])
    stats = dot_nn(jnp.where(gather, 1.0, 0.0).astype(BF16), spread)
    feature = iota((128, 128), 0)
    at = iota((128, 128), 1) - 32
    which = lax.shift_right_logical(jnp.maximum(at, 0), 3)
    mine = (at >= 0) & (at < 24) & (feature == 8 * block_ref[0] + (at & 7))
    gains = side_ref[:, 2304:2432].astype(F32)
    gain = jnp.where(which == 0, gains[:, 0:1], jnp.where(which == 1, gains[:, 1:2], gains[:, 2:3]))
    gain = jnp.sum(jnp.where(mine, gain, 0.0), axis=0, keepdims=True)
    value = jnp.where(local < CAP, rows_x, jnp.where(local < 2 * CAP, rows_c * gate_col, stats))
    value = jnp.where(local == 18, value + gain, value)
    write_messages(out_ref, value, range(4))


def packed_row(come):
    group, local = row_place(come)
    to = jnp.where(local < CAP, group * CAP + local, SLOTS + group * CAP + local - CAP)
    return jnp.where(local < 2 * CAP, to, jnp.where(local == 18, 2 * SLOTS + group, -1))


def repack(in_ref, pick_ref, out_ref):
    pick = pick_ref[...]
    for y in range(4):
        rows = read_messages(in_ref, (y,)).astype(BF16)
        packed = dot_nn(pick, rows).astype(BF16)
        for x in range(4):
            out_ref[x, y] = packed


def slot_tables():
    slot = iota((SLOTS, 128), 0)
    return slot - div(slot, CAP) * CAP, iota((SLOTS, 128), 1)


def read_rows(in_ref):
    local, lane = slot_tables()
    expand = (div(iota((SLOTS, 16), 0), CAP) == iota((SLOTS, 16), 1)).astype(F32).astype(BF16)
    shift_lane = (lane == local) | (lane == local + 16)
    at = iota((128, 128), 0) - 32
    collect = (at >= 0) & (at < 24) & ((at & 7) == (iota((128, 128), 1) & 7))
    collect = jnp.where(collect, 1.0, 0.0).astype(BF16)
    ones = jnp.ones((128, 128), BF16)
    own = lax.shift_right_logical(iota((16, 128), 1), 3) == iota((16, 128), 0)
    blocks = [in_ref[i % 4, i // 4, 288:304] for i in range(16)]
    shifts = dot_nn(expand, jnp.concatenate(blocks, axis=1))
    gain_rows = dot_nn(jnp.concatenate(blocks, axis=0), collect)
    chunks = []
    gains = []
    total = jnp.zeros((SLOTS, 128), F32)
    squares = jnp.zeros((SLOTS, 128), F32)
    for i in range(16):
        shift = jnp.where(shift_lane, shifts[:, i * 128 : i * 128 + 128], 0.0).astype(BF16)
        shift = dot_nn(shift, ones)
        base = shift if i == 0 else base
        chunk = in_ref[i % 4, i // 4, 0:144].astype(F32) + (shift - base)
        total = total + chunk
        squares = squares + chunk * chunk
        chunks.append(chunk)
        gain = jnp.where(own, gain_rows[i * 16 : i * 16 + 16], 0.0)
        gains.append(jnp.sum(gain, axis=0, keepdims=True))
    center = jnp.sum(total, axis=1, keepdims=True) / WIDTH
    variance = jnp.sum(squares, axis=1, keepdims=True) / WIDTH - center * center
    inv_scale = lax.rsqrt(variance + 1e-05)
    rows = []
    for i in range(16):
        rows.append(((chunks[i] - center) * inv_scale * gains[i]).astype(BF16))
    center = center + base[:, 0:1]
    return jnp.concatenate(rows, axis=1), jnp.concatenate(gains, axis=1), center, inv_scale


def ahead(in_ref, up, down):
    rows, gain, center, inv_scale = read_rows(in_ref)
    high, middle, low = split_three(jnp.broadcast_to(gain, (16, WIDTH)))
    row = iota((16, WIDTH), 0)
    gain = jnp.where(row == 0, high.astype(F32), middle.astype(F32))
    gain = jnp.where(row == 2, low.astype(F32), gain).astype(BF16)
    product = dot_nn(jnp.concatenate([rows, gain], axis=0), up)
    pre = product[0:SLOTS]
    weigh = product[SLOTS : SLOTS + 1] + product[SLOTS + 1 : SLOTS + 2]
    weigh = weigh + product[SLOTS + 2 : SLOTS + 3]
    bend = jnp.tanh(ROOT * (pre + CUBIC * pre * pre * pre))
    hidden = (0.5 * pre * (1.0 + bend)).astype(BF16)
    return pre, weigh, center, inv_scale, dot_nn(hidden, down).astype(BF16)


def behind(in_ref, up, down, pre, weigh, center, inv_scale):
    cots = [None] * 16
    for x in range(4):
        for y in range(4):
            cots[y * 4 + x] = in_ref[x, y, 144:288]
    grad_hidden = dot_nt(jnp.concatenate(cots, axis=1), down)
    bend = jnp.tanh(ROOT * (pre + CUBIC * pre * pre * pre))
    slope = 0.5 * (1.0 + bend) + 0.5 * pre * (1.0 - bend * bend) * (
        ROOT * (1.0 + 3.0 * CUBIC * pre * pre)
    )
    grad_act = (grad_hidden * slope).astype(BF16)
    wide = grad_act.astype(F32)
    sum_first = jnp.sum(wide * weigh, axis=1, keepdims=True)
    sum_second = jnp.sum(wide * pre, axis=1, keepdims=True)
    local, lane = slot_tables()
    spread = jnp.where(lane == local, sum_first, 0.0)
    spread = spread + jnp.where(lane == local + 16, sum_second, 0.0)
    spread = spread + jnp.where(lane == local + 32, center * (1.0 / 32), 0.0)
    spread = spread + jnp.where(lane == local + 48, inv_scale * (1.0 / 32), 0.0)
    high, low = split_two(spread)
    collect = (iota((16, SLOTS), 0) == div(iota((16, SLOTS), 1), CAP)).astype(F32).astype(BF16)
    high = dot_nn(collect, high)
    low = dot_nn(collect, low)
    stats = high + jnp.concatenate([low[:, 64:], low[:, :64]], axis=1)
    return dot_nt(grad_act, up).astype(BF16), stats.astype(BF16)


def both_ways(which_ref, in_ref, up_ref, down_ref, out_ref):
    up, down = up_ref[which_ref[0]], down_ref[which_ref[0]]
    pre, weigh, center, inv_scale, value = ahead(in_ref, up, down)
    grad_in, stats = behind(in_ref, up, down, pre, weigh, center, inv_scale)
    for x in range(4):
        for y in range(4):
            at = (y * 4 + x) * 128
            out_ref[x, y, 0:144] = value[:, at : at + 128]
            out_ref[x, y, 144:288] = grad_in[:, at : at + 128]
            out_ref[x, y, 288:304] = stats


def only_ahead(which_ref, in_ref, up_ref, down_ref, out_ref, pre_ref, weigh_ref, scalar_ref):
    up, down = up_ref[which_ref[0]], down_ref[which_ref[0]]
    pre, weigh, center, inv_scale, value = ahead(in_ref, up, down)
    pre_ref[...] = pre
    weigh_ref[...] = jnp.broadcast_to(weigh, (8, HID))
    lane = iota((SLOTS, 128), 1)
    scalar_ref[...] = jnp.where(lane == 0, center, inv_scale)
    for x in range(4):
        for y in range(4):
            at = (y * 4 + x) * 128
            out_ref[x, y] = value[:, at : at + 128]


def only_behind(
    which_ref, in_ref, up_ref, down_ref, pre_ref, weigh_ref, scalar_ref, out_ref
):
    up, down = up_ref[which_ref[0]], down_ref[which_ref[0]]
    center, inv_scale = scalar_ref[:, 0:1], scalar_ref[:, 1:2]
    grad_in, stats = behind(
        in_ref, up, down, pre_ref[...], weigh_ref[0:1], center, inv_scale
    )
    for x in range(4):
        for y in range(4):
            at = (y * 4 + x) * 128
            out_ref[x, y, 0:144] = grad_in[:, at : at + 128]
            out_ref[x, y, 144:160] = stats


def add_pair(value_ref, grad_ref, came_ref, out_ref):
    for x in range(4):
        for y in range(4):
            came = came_ref[x, y].astype(F32)
            out_ref[x, y, 0:144] = (value_ref[x, y].astype(F32) + came[0:144]).astype(BF16)
            grad = grad_ref[x, y].astype(F32)
            out_ref[x, y, 144:288] = (grad[0:144] + came[144:288]).astype(BF16)
            out_ref[x, y, 288:304] = part(join(grad[144:160] + came[288:304]))


def add_four(in_ref, drop_ref, out_ref):
    drop = drop_ref[...]
    for y in range(4):
        value = in_ref[0, y].astype(F32)
        for x in range(1, 4):
            value = value + in_ref[x, y].astype(F32)
        rows = jnp.concatenate([value[0:288].astype(BF16), part(join(value[288:304]))], axis=0)
        write_messages(out_ref, dot_nn(drop, rows), (y,))


def combine(in_ref, place_ref, gate_ref, out_ref):
    value = read_messages(in_ref, range(4))
    stats = jnp.concatenate([join(value[288:304])] * MSG, axis=0)
    value = value.astype(BF16)
    row = iota((ROWS, 128), 0)
    lane = iota((ROWS, 128), 1)
    local = row_place(row)[1]
    forward = local < CAP
    place = place_ref[...].astype(F32)
    ahead_place = jnp.where(forward, place, 0.0)
    behind_place = jnp.where(forward, 0.0, place).astype(BF16)
    gate = jnp.where(forward, gate_ref[...], 0.0)
    out_ref[0:128] = dot_tn(value.astype(F32), gate, precision=HIGHEST)
    out_ref[128:256] = dot_tn(value, behind_place)
    for q in range(4):
        column = jnp.sum(jnp.where(lane == local + 16 * q, stats, 0.0), axis=1, keepdims=True)
        out_ref[256 + q : 257 + q] = jnp.sum(ahead_place * column, axis=0, keepdims=True)
    out_ref[260:264] = jnp.zeros((4, 128), F32)


def finish(
    core_ref, in_ref, stream_ref, side_ref, heads_ref, result_ref, grad_ref, pair_ref, gw_ref
):
    got = in_ref[0] + in_ref[1]
    stream = stream_ref[...]
    cot = side_ref[:, 2176:2304].astype(F32)
    gains = side_ref[:, 2304:2432].astype(F32)
    scaled = got[128:256] * (gains[:, 0:1] + gains[:, 1:2] + gains[:, 2:3])
    first = got[256:257] / WIDTH
    second = got[257:258] / WIDTH
    center = got[258:259] * 0.5
    inv_scale = got[259:260] * 0.5
    normal = (stream - center) * inv_scale
    grad = cot + inv_scale * (scaled - first - normal * second)
    result = stream + got[0:128]
    low = core_ref[0] == 0
    result_ref[...] = jnp.where(low, result[0:64], result[64:128]).astype(BF16)
    own = jnp.where(low, grad[0:64], grad[64:128]).astype(BF16)
    grad_ref[...] = own
    pair_ref[...] = grad.astype(BF16)
    for chip in range(16):
        heads = jnp.concatenate([heads_ref[0, chip], heads_ref[1, chip]], axis=0)
        gw_ref[chip] = dot_nt(own, heads).astype(BF16)


def heads_back(at_ref, pair_ref, weight_ref, keep_ref, send_ref):
    for k in range(4):
        for j in range(4):
            chip = (at_ref[1] ^ ORDER[j]) * 4 + (at_ref[0] ^ ORDER[k])
            out_ref = keep_ref if k < 2 else send_ref
            out_ref[k % 2, j] = dot_nn(weight_ref[chip], pair_ref[...]).astype(BF16)


def lay(in_ref, out_ref):
    for chip in range(16):
        out_ref[:, chip * 128 : chip * 128 + 128] = in_ref[chip]


def a2a(value, axes):
    return lax.all_to_all(value, axes, split_axis=0, concat_axis=0, tiled=True)


def halve(keep, send, axis):
    came = lax.ppermute(send, axis, [(i, i ^ 1) for i in range(4)])
    half = keep.astype(F32) + came.astype(F32)
    came = lax.ppermute(half[1].astype(BF16), axis, [(i, i ^ 2) for i in range(4)])
    return half[0], came


def total(value):
    return jnp.sum(value.astype(F32), axis=0)


def local(
    residual, heads_out, out_weight, norm_gain, up_weight, down_weight, routes, gates, cotangent
):
    core = lax.axis_index("c").astype(jnp.int32).reshape(1)
    block = lax.axis_index(EXPERT).astype(jnp.int32).reshape(1)
    swap = [(0, 1), (1, 0)]
    heads_t = a2a(jnp.broadcast_to(heads_out.T, (16, 64, 128)), ("yl", "x"))
    wide = jnp.concatenate([out_weight.T, residual.T, cotangent.T], axis=1)
    small = jnp.concatenate(
        [routes.T.astype(F32), gates.T, jnp.pad(norm_gain, (0, 64)).reshape(1, 128)], axis=0
    )
    side, place, gate, pick, drop = call(
        prepare,
        (
            shape((64, SIDE), BF16),
            shape((ROWS, 128), BF16),
            shape((ROWS, 128), F32),
            shape((PACK, ROWS), BF16),
            shape((ROWS, PACK), BF16),
        ),
        "prepare",
        1,
        2,
    )(core, wide, small)
    side = lax.all_gather(side, "c", axis=0, tiled=True)
    turned = call(turn_weight, shape((16, 64, 128), BF16), "turn_weight", 1, 1)(core, side)
    at = jnp.stack([lax.axis_index("x"), lax.axis_index("yl")]).astype(jnp.int32)
    heads_t, turned, at = lax.optimization_barrier((heads_t, turned, at))
    heads_t = lax.all_gather(heads_t, "c", axis=0)
    stream, message = call(
        dispatch, (shape((128, 128), F32), shape((BLOCKS, 4, 2, MSG * 64), BF16)), "dispatch", 1, 4
    )(block, heads_t, side, place, gate)
    message = a2a(message.reshape(64, 2, MSG * 64), ("yh", "z", "yl"))
    packed = call(repack, shape((4, 4, PACK, 128), BF16), "repack", 0, 2)(
        message.reshape(BLOCKS, 4, 2, MSG * 64), pick
    )
    mine = a2a(packed, "x")
    other = lax.ppermute(mine, "c", swap)
    value, pre, weigh, scalars = call(
        only_ahead,
        (
            shape((4, 4, SLOTS, 128), BF16),
            shape((SLOTS, HID), F32),
            shape((8, HID), F32),
            shape((SLOTS, 128), F32),
        ),
        "only_ahead",
        1,
        3,
    )(core, mine, up_weight, down_weight)
    sent = call(both_ways, shape((4, 4, PACK, 128), BF16), "both_ways", 1, 3)(
        1 - core, other, up_weight, down_weight
    )
    sent, pre = lax.optimization_barrier((sent, pre))
    came = lax.ppermute(sent, "c", swap)
    grad = call(only_behind, shape((4, 4, SLOTS + 16, 128), BF16), "only_behind", 1, 6)(
        core, mine, up_weight, down_weight, pre, weigh, scalars
    )
    summed = call(add_pair, shape((4, 4, PACK, 128), BF16), "add_pair", 0, 3)(value, grad, came)
    summed = a2a(summed, "x")
    message = call(add_four, shape((BLOCKS, 4, 2, MSG * 64), BF16), "add_four", 0, 2)(
        summed, drop
    )
    message = a2a(message.reshape(64, 2, MSG * 64), ("yh", "z", "yl"))
    both = call(combine, shape((264, 128), F32), "combine", 0, 3)(
        message.reshape(BLOCKS, 4, 2, MSG * 64), place, gate
    )
    both = lax.all_gather(both, "c", axis=0)
    result, grad_residual, grad_pair, grad_weight = call(
        finish,
        (
            shape((64, 128), BF16),
            shape((64, 128), BF16),
            shape((128, 128), BF16),
            shape((16, 64, 128), BF16),
        ),
        "finish",
        1,
        4,
    )(core, both, stream, side, heads_t)
    grad_weight = total(a2a(grad_weight, EXPERT)).astype(BF16)
    keep, send = call(heads_back, (shape((2, 4, 64, 128), BF16),) * 2, "heads_back", 1, 2)(
        at, grad_pair, turned
    )
    pieces = halve(keep, send, "x")
    grad_weight = jnp.broadcast_to(grad_weight, (16, 64, 128))
    grad_weight = a2a(grad_weight, EXPERT)
    grad_weight = call(lay, shape((64, WIDTH), BF16), "lay", 0, 1)(grad_weight)
    heads_sum = (pieces[0] + pieces[1].astype(F32)).astype(BF16)
    pieces = halve(heads_sum[0:2], heads_sum[2:4], "yl")
    grad_heads = (pieces[0] + pieces[1].astype(F32)).astype(BF16).T
    return (result.T, grad_residual.T, grad_heads, grad_weight.T)


def solution(mesh):
    view = Mesh(mesh.devices.reshape(SPLIT), AXES)
    return jax.shard_map(
        local,
        mesh=view,
        in_specs=(
            P(EXPERT, TENSOR),
            P(EXPERT, TENSOR),
            P(None, TENSOR),
            P(TENSOR),
            P(EXPERT, None, TENSOR),
            P(EXPERT, TENSOR, None),
            P(EXPERT, None),
            P(EXPERT, None),
            P(EXPERT, TENSOR),
        ),
        out_specs=(
            P(EXPERT, TENSOR),
            P(EXPERT, TENSOR),
            P(EXPERT, TENSOR),
            P(None, TENSOR),
        ),
        check_vma=False,
    )
```

```python
import jax
import jax.numpy as jnp
from jax import lax
from jax.experimental import pallas as pl
from jax.experimental.pallas import tpu as pltpu
from jax.sharding import Mesh, PartitionSpec as P

AXES = ("yh", "z", "yl", "x", "c")
EXPERT = ("yh", "z")
TENSOR = ("yl", "x", "c")
SPLIT = (2, 8, 4, 4, 2)
BLOCKS = 16
CAP = 9
MSG = 20
ORDER_X = (0, 3, 1, 2)
ORDER_Y = (0, 2, 1, 3)
PACK = 304
SLOTS = BLOCKS * CAP
SIDE = 2432
ROWS = BLOCKS * MSG
WIDTH = 2048
HID = 256
F32 = jnp.float32
BF16 = jnp.bfloat16
HIGHEST = lax.Precision.HIGHEST
ROOT = 0.7978845608028654
CUBIC = 0.044715


def iota(shape, axis):
    return lax.broadcasted_iota(jnp.int32, shape, axis)


def div(value, by):
    scale = -(-(1 << 14) // by)
    return lax.shift_right_logical(value * scale, 14)


def dot_nn(a, b, **kw):
    return lax.dot_general(a, b, (((1,), (0,)), ((), ())), preferred_element_type=F32, **kw)


def dot_nt(a, b, **kw):
    return lax.dot_general(a, b, (((1,), (1,)), ((), ())), preferred_element_type=F32, **kw)


def dot_tn(a, b, **kw):
    return lax.dot_general(a, b, (((0,), (0,)), ((), ())), preferred_element_type=F32, **kw)


def eye(n):
    return (iota((n, n), 0) == iota((n, n), 1)).astype(F32).astype(BF16)


def call(kernel, outs, name, n_smem, n_in):
    return pl.pallas_call(
        kernel,
        out_shape=outs,
        in_specs=[pl.BlockSpec(memory_space=pltpu.SMEM)] * n_smem
        + [pl.BlockSpec(memory_space=pltpu.VMEM)] * n_in,
        out_specs=jax.tree.map(lambda _: pl.BlockSpec(memory_space=pltpu.VMEM), outs),
        name=name,
        compiler_params=pltpu.CompilerParams(vmem_limit_bytes=16 * 1024 * 1024),
    )


def shape(dims, dtype):
    return jax.ShapeDtypeStruct(dims, dtype)


def split_three(value):
    high = value.astype(BF16)
    rest = value - high.astype(F32)
    middle = rest.astype(BF16)
    return high, middle, (rest - middle.astype(F32)).astype(BF16)


def split_two(value):
    high = value.astype(BF16)
    low = (value - high.astype(F32)).astype(BF16)
    return high, low


def join(block):
    return block + jnp.concatenate([block[:, 64:], block[:, :64]], axis=1)


def part(value):
    high, low = split_two(value)
    lane = iota(value.shape, 1)
    return jnp.where(lane < 64, high.astype(F32), low.astype(F32)).astype(BF16)


def row_place(row):
    return row & 15, lax.shift_right_logical(row, 4)


def write_messages(out_ref, value, ways):
    for i in range(MSG // 2):
        at = i * 32
        pair = jnp.stack([value[at : at + 16], value[at + 16 : at + 32]], axis=1).astype(BF16)
        for y in ways:
            out_ref[:, y, :, i * 128 : i * 128 + 128] = pair


def read_messages(in_ref, ways):
    rows = []
    for i in range(MSG // 2):
        pair = None
        for y in ways:
            came = in_ref[:, y, :, i * 128 : i * 128 + 128].astype(F32)
            pair = came if pair is None else pair + came
        rows.extend([pair[:, 0], pair[:, 1]])
    return jnp.concatenate(rows, axis=0)


def prepare(
    core_ref, wide_ref, small_ref, side_ref, place_ref, gate_ref, pick_ref, drop_ref
):
    side_ref[:, 0:2304] = wide_ref[...]
    pick = iota((PACK, ROWS), 0) == packed_row(iota((8, ROWS), 1))[0:1]
    pick_ref[...] = jnp.where(pick, 1.0, 0.0).astype(BF16)
    drop = iota((ROWS, PACK), 1) == packed_row(iota((ROWS, 128), 0))[:, 0:1]
    drop_ref[...] = jnp.where(drop, 1.0, 0.0).astype(BF16)
    routes = small_ref[0:2].astype(jnp.int32)
    gates = small_ref[2:4]
    core = core_ref[0]
    row = iota((ROWS, 128), 0)
    group, local = row_place(row)
    slot = jnp.where(local < CAP, local, local - CAP)
    used = local < 2 * CAP
    expert = 2 * group + core
    first = (routes[0:1, :] == expert) & used
    second = (routes[1:2, :] == expert) & used
    named = jnp.where(first | second, 1.0, 0.0)
    before = (iota((128, 128), 0) < iota((128, 128), 1)).astype(F32).astype(BF16)
    earlier = dot_nn(named.astype(BF16), before)
    taken = (earlier == slot.astype(F32)) & (named > 0.5)
    place_ref[...] = jnp.where(taken, 1.0, 0.0).astype(BF16)
    gate = jnp.where(first, gates[0:1, :], gates[1:2, :])
    gate_ref[...] = jnp.where(taken, gate, 0.0)
    own = iota((64, 64), 0) == iota((64, 64), 1)
    gain = jnp.sum(jnp.where(own, small_ref[4:5, 0:64], 0.0), axis=1, keepdims=True)
    high, middle, low = split_three(jnp.broadcast_to(gain, (64, 128)))
    lane = iota((64, 128), 1)
    value = jnp.where(lane == 0, high.astype(F32), middle.astype(F32))
    side_ref[:, 2304:2432] = jnp.where(lane == 2, low.astype(F32), value).astype(BF16)


def turn_weight(core_ref, side_ref, out_ref):
    mirror = eye(128)
    for chip in range(16):
        turned = dot_nt(mirror, side_ref[:, chip * 128 : chip * 128 + 128])
        out_ref[chip] = jnp.where(core_ref[0] == 0, turned[0:64], turned[64:128]).astype(BF16)


def dispatch(block_ref, heads_ref, side_ref, place_ref, gate_ref, stream_ref, whole_ref, out_ref):
    pieces = []
    for chip in range(16):
        pieces.append(heads_ref[0, chip])
        pieces.append(heads_ref[1, chip])
    heads = jnp.concatenate(pieces, axis=0)
    whole_ref[...] = heads
    mixed = dot_nn(side_ref[:, 0:2048], heads)
    stream = side_ref[:, 2048:2176].astype(F32) + mixed
    stream_ref[...] = stream
    shift = jnp.mean(stream, axis=0, keepdims=True)
    centered = (stream - shift).astype(BF16)
    place = place_ref[...]
    placed = place.astype(F32)
    rows_x = dot_nt(place, centered)
    rows_c = dot_nt(place, side_ref[:, 2176:2304])
    gate_col = jnp.sum(gate_ref[...], axis=1, keepdims=True)
    shift_col = jnp.sum(placed * shift, axis=1, keepdims=True)
    row = iota((ROWS, 128), 0)
    lane = iota((ROWS, 128), 1)
    local = row_place(row)[1]
    high, low = split_two(shift_col)
    spread = jnp.where(lane == local, high.astype(F32), 0.0)
    spread = spread + jnp.where(lane == local + 16, low.astype(F32), 0.0)
    spread = jnp.where(local < CAP, spread, 0.0).astype(BF16)
    to_group, to_local = row_place(iota((ROWS, ROWS), 0))
    gather = (to_local == 18) & (to_group == row_place(iota((ROWS, ROWS), 1))[0])
    stats = dot_nn(jnp.where(gather, 1.0, 0.0).astype(BF16), spread)
    feature = iota((128, 128), 0)
    at = iota((128, 128), 1) - 32
    which = lax.shift_right_logical(jnp.maximum(at, 0), 3)
    mine = (at >= 0) & (at < 24) & (feature == 8 * block_ref[0] + (at & 7))
    gains = side_ref[:, 2304:2432].astype(F32)
    gain = jnp.where(which == 0, gains[:, 0:1], jnp.where(which == 1, gains[:, 1:2], gains[:, 2:3]))
    gain = jnp.sum(jnp.where(mine, gain, 0.0), axis=0, keepdims=True)
    value = jnp.where(local < CAP, rows_x, jnp.where(local < 2 * CAP, rows_c * gate_col, stats))
    value = jnp.where(local == 18, value + gain, value)
    write_messages(out_ref, value, range(4))


def packed_row(come):
    group, local = row_place(come)
    to = jnp.where(local < CAP, group * CAP + local, SLOTS + group * CAP + local - CAP)
    return jnp.where(local < 2 * CAP, to, jnp.where(local == 18, 2 * SLOTS + group, -1))


def repack(in_ref, pick_ref, out_ref):
    pick = pick_ref[...]
    for y in range(4):
        rows = read_messages(in_ref, (y,)).astype(BF16)
        packed = dot_nn(pick, rows).astype(BF16)
        for x in range(4):
            out_ref[x, y] = packed


def slot_tables():
    slot = iota((SLOTS, 128), 0)
    return slot - div(slot, CAP) * CAP, iota((SLOTS, 128), 1)


def read_rows(in_ref):
    local, lane = slot_tables()
    expand = (div(iota((SLOTS, 16), 0), CAP) == iota((SLOTS, 16), 1)).astype(F32).astype(BF16)
    shift_lane = (lane == local) | (lane == local + 16)
    at = iota((128, 128), 0) - 32
    collect = (at >= 0) & (at < 24) & ((at & 7) == (iota((128, 128), 1) & 7))
    collect = jnp.where(collect, 1.0, 0.0).astype(BF16)
    ones = jnp.ones((128, 128), BF16)
    own = lax.shift_right_logical(iota((16, 128), 1), 3) == iota((16, 128), 0)
    blocks = [in_ref[i % 4, i // 4, 288:304] for i in range(16)]
    shifts = dot_nn(expand, jnp.concatenate(blocks, axis=1))
    gain_rows = dot_nn(jnp.concatenate(blocks, axis=0), collect)
    chunks = []
    gains = []
    total = jnp.zeros((SLOTS, 128), F32)
    squares = jnp.zeros((SLOTS, 128), F32)
    for i in range(16):
        shift = jnp.where(shift_lane, shifts[:, i * 128 : i * 128 + 128], 0.0).astype(BF16)
        shift = dot_nn(shift, ones)
        base = shift if i == 0 else base
        chunk = in_ref[i % 4, i // 4, 0:144].astype(F32) + (shift - base)
        total = total + chunk
        squares = squares + chunk * chunk
        chunks.append(chunk)
        gain = jnp.where(own, gain_rows[i * 16 : i * 16 + 16], 0.0)
        gains.append(jnp.sum(gain, axis=0, keepdims=True))
    center = jnp.sum(total, axis=1, keepdims=True) / WIDTH
    variance = jnp.sum(squares, axis=1, keepdims=True) / WIDTH - center * center
    inv_scale = lax.rsqrt(variance + 1e-05)
    rows = []
    for i in range(16):
        rows.append(((chunks[i] - center) * inv_scale * gains[i]).astype(BF16))
    center = center + base[:, 0:1]
    return jnp.concatenate(rows, axis=1), jnp.concatenate(gains, axis=1), center, inv_scale


def ahead(in_ref, up, down):
    rows, gain, center, inv_scale = read_rows(in_ref)
    high, middle, low = split_three(jnp.broadcast_to(gain, (16, WIDTH)))
    row = iota((16, WIDTH), 0)
    gain = jnp.where(row == 0, high.astype(F32), middle.astype(F32))
    gain = jnp.where(row == 2, low.astype(F32), gain).astype(BF16)
    product = dot_nn(jnp.concatenate([rows, gain], axis=0), up)
    pre = product[0:SLOTS]
    weigh = product[SLOTS : SLOTS + 1] + product[SLOTS + 1 : SLOTS + 2]
    weigh = weigh + product[SLOTS + 2 : SLOTS + 3]
    bend = jnp.tanh(ROOT * (pre + CUBIC * pre * pre * pre))
    hidden = (0.5 * pre * (1.0 + bend)).astype(BF16)
    return pre, weigh, center, inv_scale, dot_nn(hidden, down).astype(BF16)


def behind(in_ref, up, down, pre, weigh, center, inv_scale):
    cots = [None] * 16
    for x in range(4):
        for y in range(4):
            cots[y * 4 + x] = in_ref[x, y, 144:288]
    grad_hidden = dot_nt(jnp.concatenate(cots, axis=1), down)
    bend = jnp.tanh(ROOT * (pre + CUBIC * pre * pre * pre))
    slope = 0.5 * (1.0 + bend) + 0.5 * pre * (1.0 - bend * bend) * (
        ROOT * (1.0 + 3.0 * CUBIC * pre * pre)
    )
    grad_act = (grad_hidden * slope).astype(BF16)
    wide = grad_act.astype(F32)
    sum_first = jnp.sum(wide * weigh, axis=1, keepdims=True)
    sum_second = jnp.sum(wide * pre, axis=1, keepdims=True)
    local, lane = slot_tables()
    spread = jnp.where(lane == local, sum_first, 0.0)
    spread = spread + jnp.where(lane == local + 16, sum_second, 0.0)
    spread = spread + jnp.where(lane == local + 32, center * (1.0 / 32), 0.0)
    spread = spread + jnp.where(lane == local + 48, inv_scale * (1.0 / 32), 0.0)
    high, low = split_two(spread)
    collect = (iota((16, SLOTS), 0) == div(iota((16, SLOTS), 1), CAP)).astype(F32).astype(BF16)
    high = dot_nn(collect, high)
    low = dot_nn(collect, low)
    stats = high + jnp.concatenate([low[:, 64:], low[:, :64]], axis=1)
    return dot_nt(grad_act, up).astype(BF16), stats.astype(BF16)


def both_ways(which_ref, in_ref, up_ref, down_ref, out_ref):
    up, down = up_ref[which_ref[0]], down_ref[which_ref[0]]
    pre, weigh, center, inv_scale, value = ahead(in_ref, up, down)
    grad_in, stats = behind(in_ref, up, down, pre, weigh, center, inv_scale)
    for x in range(4):
        for y in range(4):
            at = (y * 4 + x) * 128
            out_ref[x, y, 0:144] = value[:, at : at + 128]
            out_ref[x, y, 144:288] = grad_in[:, at : at + 128]
            out_ref[x, y, 288:304] = stats


def only_ahead(which_ref, in_ref, up_ref, down_ref, out_ref, pre_ref, weigh_ref, scalar_ref):
    up, down = up_ref[which_ref[0]], down_ref[which_ref[0]]
    pre, weigh, center, inv_scale, value = ahead(in_ref, up, down)
    pre_ref[...] = pre
    weigh_ref[...] = jnp.broadcast_to(weigh, (8, HID))
    lane = iota((SLOTS, 128), 1)
    scalar_ref[...] = jnp.where(lane == 0, center, inv_scale)
    for x in range(4):
        for y in range(4):
            at = (y * 4 + x) * 128
            out_ref[x, y] = value[:, at : at + 128]


def only_behind(
    which_ref, in_ref, up_ref, down_ref, pre_ref, weigh_ref, scalar_ref, out_ref
):
    up, down = up_ref[which_ref[0]], down_ref[which_ref[0]]
    center, inv_scale = scalar_ref[:, 0:1], scalar_ref[:, 1:2]
    grad_in, stats = behind(
        in_ref, up, down, pre_ref[...], weigh_ref[0:1], center, inv_scale
    )
    for x in range(4):
        for y in range(4):
            at = (y * 4 + x) * 128
            out_ref[x, y, 0:144] = grad_in[:, at : at + 128]
            out_ref[x, y, 144:160] = stats


def add_pair(value_ref, grad_ref, came_ref, out_ref):
    for x in range(4):
        for y in range(4):
            came = came_ref[x, y].astype(F32)
            out_ref[x, y, 0:144] = (value_ref[x, y].astype(F32) + came[0:144]).astype(BF16)
            grad = grad_ref[x, y].astype(F32)
            out_ref[x, y, 144:288] = (grad[0:144] + came[144:288]).astype(BF16)
            out_ref[x, y, 288:304] = part(join(grad[144:160] + came[288:304]))


def add_four(in_ref, drop_ref, out_ref):
    drop = drop_ref[...]
    for y in range(4):
        value = in_ref[0, y].astype(F32)
        for x in range(1, 4):
            value = value + in_ref[x, y].astype(F32)
        rows = jnp.concatenate([value[0:288].astype(BF16), part(join(value[288:304]))], axis=0)
        write_messages(out_ref, dot_nn(drop, rows), (y,))


def combine(in_ref, place_ref, gate_ref, out_ref):
    value = read_messages(in_ref, range(4))
    stats = jnp.concatenate([join(value[288:304])] * MSG, axis=0)
    value = value.astype(BF16)
    row = iota((ROWS, 128), 0)
    lane = iota((ROWS, 128), 1)
    local = row_place(row)[1]
    forward = local < CAP
    place = place_ref[...].astype(F32)
    ahead_place = jnp.where(forward, place, 0.0)
    behind_place = jnp.where(forward, 0.0, place).astype(BF16)
    gate = jnp.where(forward, gate_ref[...], 0.0)
    out_ref[0:128] = dot_tn(value.astype(F32), gate, precision=HIGHEST)
    out_ref[128:256] = dot_tn(value, behind_place)
    for q in range(4):
        column = jnp.sum(jnp.where(lane == local + 16 * q, stats, 0.0), axis=1, keepdims=True)
        out_ref[256 + q : 257 + q] = jnp.sum(ahead_place * column, axis=0, keepdims=True)
    out_ref[260:264] = jnp.zeros((4, 128), F32)


def finish(
    core_ref, in_ref, stream_ref, side_ref, heads_ref, result_ref, grad_ref, pair_ref, gw_ref
):
    got = in_ref[0] + in_ref[1]
    stream = stream_ref[...]
    cot = side_ref[:, 2176:2304].astype(F32)
    gains = side_ref[:, 2304:2432].astype(F32)
    scaled = got[128:256] * (gains[:, 0:1] + gains[:, 1:2] + gains[:, 2:3])
    first = got[256:257] / WIDTH
    second = got[257:258] / WIDTH
    center = got[258:259] * 0.5
    inv_scale = got[259:260] * 0.5
    normal = (stream - center) * inv_scale
    grad = cot + inv_scale * (scaled - first - normal * second)
    result = stream + got[0:128]
    low = core_ref[0] == 0
    result_ref[...] = jnp.where(low, result[0:64], result[64:128]).astype(BF16)
    own = jnp.where(low, grad[0:64], grad[64:128]).astype(BF16)
    grad_ref[...] = own
    pair_ref[...] = grad.astype(BF16)
    product = dot_nt(own, heads_ref[...]).astype(BF16)
    for chip in range(16):
        gw_ref[chip] = product[:, chip * 128 : chip * 128 + 128]


def heads_back(at_ref, pair_ref, weight_ref, keep_ref, send_ref):
    for k in range(4):
        for j in range(4):
            chip = (at_ref[1] ^ ORDER_Y[j]) * 4 + (at_ref[0] ^ ORDER_X[k])
            out_ref = keep_ref if k < 2 else send_ref
            out_ref[k % 2, j] = dot_nn(weight_ref[chip], pair_ref[...]).astype(BF16)


def lay(in_ref, out_ref):
    for chip in range(16):
        out_ref[:, chip * 128 : chip * 128 + 128] = in_ref[chip]


def a2a(value, axes):
    return lax.all_to_all(value, axes, split_axis=0, concat_axis=0, tiled=True)


def halve(keep, send, axis, far):
    came = lax.ppermute(send, axis, [(i, i ^ 1) for i in range(4)])
    half = keep.astype(F32) + came.astype(F32)
    came = lax.ppermute(half[1].astype(BF16), axis, [(i, i ^ far) for i in range(4)])
    return half[0], came


def total(value):
    return jnp.sum(value.astype(F32), axis=0)


def local(
    residual, heads_out, out_weight, norm_gain, up_weight, down_weight, routes, gates, cotangent
):
    core = lax.axis_index("c").astype(jnp.int32).reshape(1)
    block = lax.axis_index(EXPERT).astype(jnp.int32).reshape(1)
    swap = [(0, 1), (1, 0)]
    heads_t = a2a(jnp.broadcast_to(heads_out.T, (16, 64, 128)), ("yl", "x"))
    wide = jnp.concatenate([out_weight.T, residual.T, cotangent.T], axis=1)
    small = jnp.concatenate(
        [routes.T.astype(F32), gates.T, jnp.pad(norm_gain, (0, 64)).reshape(1, 128)], axis=0
    )
    side, place, gate, pick, drop = call(
        prepare,
        (
            shape((64, SIDE), BF16),
            shape((ROWS, 128), BF16),
            shape((ROWS, 128), F32),
            shape((PACK, ROWS), BF16),
            shape((ROWS, PACK), BF16),
        ),
        "prepare",
        1,
        2,
    )(core, wide, small)
    side = lax.all_gather(side, "c", axis=0, tiled=True)
    turned = call(turn_weight, shape((16, 64, 128), BF16), "turn_weight", 1, 1)(core, side)
    at = jnp.stack([lax.axis_index("x"), lax.axis_index("yl")]).astype(jnp.int32)
    heads_t, turned, at = lax.optimization_barrier((heads_t, turned, at))
    heads_t = lax.all_gather(heads_t, "c", axis=0)
    stream, heads_t, message = call(
        dispatch,
        (
            shape((128, 128), F32),
            shape((WIDTH, 128), BF16),
            shape((BLOCKS, 4, 2, MSG * 64), BF16),
        ),
        "dispatch",
        1,
        4,
    )(block, heads_t, side, place, gate)
    message = a2a(message.reshape(64, 2, MSG * 64), ("yh", "z", "yl"))
    packed = call(repack, shape((4, 4, PACK, 128), BF16), "repack", 0, 2)(
        message.reshape(BLOCKS, 4, 2, MSG * 64), pick
    )
    mine = a2a(packed, "x")
    other = lax.ppermute(mine, "c", swap)
    value, pre, weigh, scalars = call(
        only_ahead,
        (
            shape((4, 4, SLOTS, 128), BF16),
            shape((SLOTS, HID), F32),
            shape((8, HID), F32),
            shape((SLOTS, 128), F32),
        ),
        "only_ahead",
        1,
        3,
    )(core, mine, up_weight, down_weight)
    sent = call(both_ways, shape((4, 4, PACK, 128), BF16), "both_ways", 1, 3)(
        1 - core, other, up_weight, down_weight
    )
    sent, pre = lax.optimization_barrier((sent, pre))
    came = lax.ppermute(sent, "c", swap)
    grad = call(only_behind, shape((4, 4, SLOTS + 16, 128), BF16), "only_behind", 1, 6)(
        core, mine, up_weight, down_weight, pre, weigh, scalars
    )
    summed = call(add_pair, shape((4, 4, PACK, 128), BF16), "add_pair", 0, 3)(value, grad, came)
    summed = a2a(summed, "x")
    message = call(add_four, shape((BLOCKS, 4, 2, MSG * 64), BF16), "add_four", 0, 2)(
        summed, drop
    )
    message = a2a(message.reshape(64, 2, MSG * 64), ("yh", "z", "yl"))
    both = call(combine, shape((264, 128), F32), "combine", 0, 3)(
        message.reshape(BLOCKS, 4, 2, MSG * 64), place, gate
    )
    both = lax.all_gather(both, "c", axis=0)
    result, grad_residual, grad_pair, grad_weight = call(
        finish,
        (
            shape((64, 128), BF16),
            shape((64, 128), BF16),
            shape((128, 128), BF16),
            shape((16, 64, 128), BF16),
        ),
        "finish",
        1,
        4,
    )(core, both, stream, side, heads_t)
    grad_weight = total(a2a(grad_weight, EXPERT)).astype(BF16)
    keep, send = call(heads_back, (shape((2, 4, 64, 128), BF16),) * 2, "heads_back", 1, 2)(
        at, grad_pair, turned
    )
    pieces = halve(keep, send, "x", 3)
    grad_weight = jnp.broadcast_to(grad_weight, (16, 64, 128))
    grad_weight = a2a(grad_weight, EXPERT)
    grad_weight = call(lay, shape((64, WIDTH), BF16), "lay", 0, 1)(grad_weight)
    heads_sum = (pieces[0] + pieces[1].astype(F32)).astype(BF16)
    pieces = halve(heads_sum[0:2], heads_sum[2:4], "yl", 2)
    grad_heads = (pieces[0] + pieces[1].astype(F32)).astype(BF16).T
    return (result.T, grad_residual.T, grad_heads, grad_weight.T)


def solution(mesh):
    view = Mesh(mesh.devices.reshape(SPLIT), AXES)
    return jax.shard_map(
        local,
        mesh=view,
        in_specs=(
            P(EXPERT, TENSOR),
            P(EXPERT, TENSOR),
            P(None, TENSOR),
            P(TENSOR),
            P(EXPERT, None, TENSOR),
            P(EXPERT, TENSOR, None),
            P(EXPERT, None),
            P(EXPERT, None),
            P(EXPERT, TENSOR),
        ),
        out_specs=(
            P(EXPERT, TENSOR),
            P(EXPERT, TENSOR),
            P(EXPERT, TENSOR),
            P(None, TENSOR),
        ),
        check_vma=False,
    )
```

```python
import jax
import jax.numpy as jnp
from jax import lax
from jax.experimental import pallas as pl
from jax.experimental.pallas import tpu as pltpu
from jax.sharding import Mesh, PartitionSpec as P

AXES = ("yh", "z", "yl", "x", "c")
EXPERT = ("yh", "z")
TENSOR = ("yl", "x", "c")
SPLIT = (2, 8, 4, 4, 2)
BLOCKS = 16
CAP = 9
MSG = 20
ORDER_X = (0, 3, 1, 2)
ORDER_Y = (0, 2, 1, 3)
PACK = 304
SLOTS = BLOCKS * CAP
SIDE = 2432
ROWS = BLOCKS * MSG
WIDTH = 2048
HID = 256
F32 = jnp.float32
BF16 = jnp.bfloat16
HIGHEST = lax.Precision.HIGHEST
ROOT = 0.7978845608028654
CUBIC = 0.044715


def iota(shape, axis):
    return lax.broadcasted_iota(jnp.int32, shape, axis)


def div(value, by):
    scale = -(-(1 << 14) // by)
    return lax.shift_right_logical(value * scale, 14)


def dot_nn(a, b, **kw):
    return lax.dot_general(a, b, (((1,), (0,)), ((), ())), preferred_element_type=F32, **kw)


def dot_nt(a, b, **kw):
    return lax.dot_general(a, b, (((1,), (1,)), ((), ())), preferred_element_type=F32, **kw)


def dot_tn(a, b, **kw):
    return lax.dot_general(a, b, (((0,), (0,)), ((), ())), preferred_element_type=F32, **kw)


def eye(n):
    return (iota((n, n), 0) == iota((n, n), 1)).astype(F32).astype(BF16)


def call(kernel, outs, name, n_smem, n_in):
    return pl.pallas_call(
        kernel,
        out_shape=outs,
        in_specs=[pl.BlockSpec(memory_space=pltpu.SMEM)] * n_smem
        + [pl.BlockSpec(memory_space=pltpu.VMEM)] * n_in,
        out_specs=jax.tree.map(lambda _: pl.BlockSpec(memory_space=pltpu.VMEM), outs),
        name=name,
        compiler_params=pltpu.CompilerParams(vmem_limit_bytes=16 * 1024 * 1024),
    )


def shape(dims, dtype):
    return jax.ShapeDtypeStruct(dims, dtype)


def split_three(value):
    high = value.astype(BF16)
    rest = value - high.astype(F32)
    middle = rest.astype(BF16)
    return high, middle, (rest - middle.astype(F32)).astype(BF16)


def split_two(value):
    high = value.astype(BF16)
    low = (value - high.astype(F32)).astype(BF16)
    return high, low


def join(block):
    return block + jnp.concatenate([block[:, 64:], block[:, :64]], axis=1)


def part(value):
    high, low = split_two(value)
    lane = iota(value.shape, 1)
    return jnp.where(lane < 64, high.astype(F32), low.astype(F32)).astype(BF16)


def row_place(row):
    pair = lax.shift_right_logical(row, 5)
    return lax.shift_right_logical(row & 31, 1), 2 * pair + (row & 1)


def write_messages(out_ref, value, ways):
    for i in range(MSG // 2):
        at = i * 32
        pair = value[at : at + 32].reshape(BLOCKS, 2, 128).astype(BF16)
        for y in ways:
            out_ref[:, y, :, i * 128 : i * 128 + 128] = pair


def read_messages(in_ref, ways):
    rows = []
    for i in range(MSG // 2):
        pair = None
        for y in ways:
            came = in_ref[:, y, :, i * 128 : i * 128 + 128].astype(F32)
            pair = came if pair is None else pair + came
        rows.append(pair.reshape(32, 128))
    return jnp.concatenate(rows, axis=0)


def prepare(
    core_ref, wide_ref, small_ref, side_ref, place_ref, gate_ref, pick_ref, drop_ref
):
    side_ref[:, 0:2304] = wide_ref[...]
    pick = iota((PACK, ROWS), 0) == packed_row(iota((8, ROWS), 1))[0:1]
    pick_ref[...] = jnp.where(pick, 1.0, 0.0).astype(BF16)
    drop = iota((ROWS, PACK), 1) == packed_row(iota((ROWS, 128), 0))[:, 0:1]
    drop_ref[...] = jnp.where(drop, 1.0, 0.0).astype(BF16)
    routes = small_ref[0:2].astype(jnp.int32)
    gates = small_ref[2:4]
    core = core_ref[0]
    row = iota((ROWS, 128), 0)
    group, local = row_place(row)
    slot = jnp.where(local < CAP, local, local - CAP)
    used = local < 2 * CAP
    expert = 2 * group + core
    first = (routes[0:1, :] == expert) & used
    second = (routes[1:2, :] == expert) & used
    named = jnp.where(first | second, 1.0, 0.0)
    before = (iota((128, 128), 0) < iota((128, 128), 1)).astype(F32).astype(BF16)
    earlier = dot_nn(named.astype(BF16), before)
    taken = (earlier == slot.astype(F32)) & (named > 0.5)
    place_ref[...] = jnp.where(taken, 1.0, 0.0).astype(BF16)
    gate = jnp.where(first, gates[0:1, :], gates[1:2, :])
    gate_ref[...] = jnp.where(taken, gate, 0.0)
    own = iota((64, 64), 0) == iota((64, 64), 1)
    gain = jnp.sum(jnp.where(own, small_ref[4:5, 0:64], 0.0), axis=1, keepdims=True)
    high, middle, low = split_three(jnp.broadcast_to(gain, (64, 128)))
    lane = iota((64, 128), 1)
    value = jnp.where(lane == 0, high.astype(F32), middle.astype(F32))
    side_ref[:, 2304:2432] = jnp.where(lane == 2, low.astype(F32), value).astype(BF16)


def turn_weight(core_ref, side_ref, out_ref):
    mirror = eye(128)
    for chip in range(16):
        turned = dot_nt(mirror, side_ref[:, chip * 128 : chip * 128 + 128])
        out_ref[chip] = jnp.where(core_ref[0] == 0, turned[0:64], turned[64:128]).astype(BF16)


def dispatch(block_ref, heads_ref, side_ref, place_ref, gate_ref, stream_ref, whole_ref, out_ref):
    pieces = []
    for chip in range(16):
        pieces.append(heads_ref[0, chip])
        pieces.append(heads_ref[1, chip])
    heads = jnp.concatenate(pieces, axis=0)
    whole_ref[...] = heads
    mixed = dot_nn(side_ref[:, 0:2048], heads)
    stream = side_ref[:, 2048:2176].astype(F32) + mixed
    stream_ref[...] = stream
    shift = jnp.mean(stream, axis=0, keepdims=True)
    centered = (stream - shift).astype(BF16)
    place = place_ref[...]
    placed = place.astype(F32)
    rows_x = dot_nt(place, centered)
    rows_c = dot_nt(place, side_ref[:, 2176:2304])
    gate_col = jnp.sum(gate_ref[...], axis=1, keepdims=True)
    shift_col = jnp.sum(placed * shift, axis=1, keepdims=True)
    row = iota((ROWS, 128), 0)
    lane = iota((ROWS, 128), 1)
    local = row_place(row)[1]
    high, low = split_two(shift_col)
    spread = jnp.where(lane == local, high.astype(F32), 0.0)
    spread = spread + jnp.where(lane == local + 16, low.astype(F32), 0.0)
    spread = jnp.where(local < CAP, spread, 0.0).astype(BF16)
    to_group, to_local = row_place(iota((ROWS, ROWS), 0))
    gather = (to_local == 18) & (to_group == row_place(iota((ROWS, ROWS), 1))[0])
    stats = dot_nn(jnp.where(gather, 1.0, 0.0).astype(BF16), spread)
    feature = iota((128, 128), 0)
    at = iota((128, 128), 1) - 32
    which = lax.shift_right_logical(jnp.maximum(at, 0), 3)
    mine = (at >= 0) & (at < 24) & (feature == 8 * block_ref[0] + (at & 7))
    gains = side_ref[:, 2304:2432].astype(F32)
    gain = jnp.where(which == 0, gains[:, 0:1], jnp.where(which == 1, gains[:, 1:2], gains[:, 2:3]))
    gain = jnp.sum(jnp.where(mine, gain, 0.0), axis=0, keepdims=True)
    value = jnp.where(local < CAP, rows_x, jnp.where(local < 2 * CAP, rows_c * gate_col, stats))
    value = jnp.where(local == 18, value + gain, value)
    write_messages(out_ref, value, range(4))


def packed_row(come):
    group, local = row_place(come)
    to = jnp.where(local < CAP, group * CAP + local, SLOTS + group * CAP + local - CAP)
    return jnp.where(local < 2 * CAP, to, jnp.where(local == 18, 2 * SLOTS + group, -1))


def repack(in_ref, pick_ref, out_ref):
    pick = pick_ref[...]
    for y in range(4):
        rows = read_messages(in_ref, (y,)).astype(BF16)
        packed = dot_nn(pick, rows).astype(BF16)
        for x in range(4):
            out_ref[x, y] = packed


def slot_tables():
    slot = iota((SLOTS, 128), 0)
    return slot - div(slot, CAP) * CAP, iota((SLOTS, 128), 1)


def read_rows(in_ref):
    local, lane = slot_tables()
    expand = (div(iota((SLOTS, 16), 0), CAP) == iota((SLOTS, 16), 1)).astype(F32).astype(BF16)
    shift_lane = (lane == local) | (lane == local + 16)
    at = iota((128, 128), 0) - 32
    collect = (at >= 0) & (at < 24) & ((at & 7) == (iota((128, 128), 1) & 7))
    collect = jnp.where(collect, 1.0, 0.0).astype(BF16)
    ones = jnp.ones((128, 128), BF16)
    own = lax.shift_right_logical(iota((16, 128), 1), 3) == iota((16, 128), 0)
    blocks = [in_ref[i % 4, i // 4, 288:304] for i in range(16)]
    shifts = dot_nn(expand, jnp.concatenate(blocks, axis=1))
    gain_rows = dot_nn(jnp.concatenate(blocks, axis=0), collect)
    chunks = []
    gains = []
    total = jnp.zeros((SLOTS, 128), F32)
    squares = jnp.zeros((SLOTS, 128), F32)
    for i in range(16):
        shift = jnp.where(shift_lane, shifts[:, i * 128 : i * 128 + 128], 0.0).astype(BF16)
        shift = dot_nn(shift, ones)
        base = shift if i == 0 else base
        chunk = in_ref[i % 4, i // 4, 0:144].astype(F32) + (shift - base)
        total = total + chunk
        squares = squares + chunk * chunk
        chunks.append(chunk)
        gain = jnp.where(own, gain_rows[i * 16 : i * 16 + 16], 0.0)
        gains.append(jnp.sum(gain, axis=0, keepdims=True))
    center = jnp.sum(total, axis=1, keepdims=True) / WIDTH
    variance = jnp.sum(squares, axis=1, keepdims=True) / WIDTH - center * center
    inv_scale = lax.rsqrt(variance + 1e-05)
    rows = []
    for i in range(16):
        rows.append(((chunks[i] - center) * inv_scale * gains[i]).astype(BF16))
    center = center + base[:, 0:1]
    return jnp.concatenate(rows, axis=1), jnp.concatenate(gains, axis=1), center, inv_scale


def ahead(in_ref, up, down):
    rows, gain, center, inv_scale = read_rows(in_ref)
    high, middle, low = split_three(jnp.broadcast_to(gain, (16, WIDTH)))
    row = iota((16, WIDTH), 0)
    gain = jnp.where(row == 0, high.astype(F32), middle.astype(F32))
    gain = jnp.where(row == 2, low.astype(F32), gain).astype(BF16)
    product = dot_nn(jnp.concatenate([rows, gain], axis=0), up)
    pre = product[0:SLOTS]
    weigh = product[SLOTS : SLOTS + 1] + product[SLOTS + 1 : SLOTS + 2]
    weigh = weigh + product[SLOTS + 2 : SLOTS + 3]
    bend = jnp.tanh(ROOT * (pre + CUBIC * pre * pre * pre))
    hidden = (0.5 * pre * (1.0 + bend)).astype(BF16)
    return pre, weigh, center, inv_scale, dot_nn(hidden, down).astype(BF16)


def behind(in_ref, up, down, pre, weigh, center, inv_scale):
    cots = [None] * 16
    for x in range(4):
        for y in range(4):
            cots[y * 4 + x] = in_ref[x, y, 144:288]
    grad_hidden = dot_nt(jnp.concatenate(cots, axis=1), down)
    bend = jnp.tanh(ROOT * (pre + CUBIC * pre * pre * pre))
    slope = 0.5 * (1.0 + bend) + 0.5 * pre * (1.0 - bend * bend) * (
        ROOT * (1.0 + 3.0 * CUBIC * pre * pre)
    )
    grad_act = (grad_hidden * slope).astype(BF16)
    wide = grad_act.astype(F32)
    sum_first = jnp.sum(wide * weigh, axis=1, keepdims=True)
    sum_second = jnp.sum(wide * pre, axis=1, keepdims=True)
    local, lane = slot_tables()
    spread = jnp.where(lane == local, sum_first, 0.0)
    spread = spread + jnp.where(lane == local + 16, sum_second, 0.0)
    spread = spread + jnp.where(lane == local + 32, center * (1.0 / 32), 0.0)
    spread = spread + jnp.where(lane == local + 48, inv_scale * (1.0 / 32), 0.0)
    high, low = split_two(spread)
    collect = (iota((16, SLOTS), 0) == div(iota((16, SLOTS), 1), CAP)).astype(F32).astype(BF16)
    high = dot_nn(collect, high)
    low = dot_nn(collect, low)
    stats = high + jnp.concatenate([low[:, 64:], low[:, :64]], axis=1)
    return dot_nt(grad_act, up).astype(BF16), stats.astype(BF16)


def both_ways(which_ref, in_ref, up_ref, down_ref, out_ref):
    up, down = up_ref[which_ref[0]], down_ref[which_ref[0]]
    pre, weigh, center, inv_scale, value = ahead(in_ref, up, down)
    grad_in, stats = behind(in_ref, up, down, pre, weigh, center, inv_scale)
    for x in range(4):
        for y in range(4):
            at = (y * 4 + x) * 128
            out_ref[x, y, 0:144] = value[:, at : at + 128]
            out_ref[x, y, 144:288] = grad_in[:, at : at + 128]
            out_ref[x, y, 288:304] = stats


def only_ahead(which_ref, in_ref, up_ref, down_ref, out_ref, pre_ref, weigh_ref, scalar_ref):
    up, down = up_ref[which_ref[0]], down_ref[which_ref[0]]
    pre, weigh, center, inv_scale, value = ahead(in_ref, up, down)
    pre_ref[...] = pre
    weigh_ref[...] = jnp.broadcast_to(weigh, (8, HID))
    lane = iota((SLOTS, 128), 1)
    scalar_ref[...] = jnp.where(lane == 0, center, inv_scale)
    for x in range(4):
        for y in range(4):
            at = (y * 4 + x) * 128
            out_ref[x, y] = value[:, at : at + 128]


def only_behind(
    which_ref, in_ref, up_ref, down_ref, pre_ref, weigh_ref, scalar_ref, out_ref
):
    up, down = up_ref[which_ref[0]], down_ref[which_ref[0]]
    center, inv_scale = scalar_ref[:, 0:1], scalar_ref[:, 1:2]
    grad_in, stats = behind(
        in_ref, up, down, pre_ref[...], weigh_ref[0:1], center, inv_scale
    )
    for x in range(4):
        for y in range(4):
            at = (y * 4 + x) * 128
            out_ref[x, y, 0:144] = grad_in[:, at : at + 128]
            out_ref[x, y, 144:160] = stats


def add_pair(value_ref, grad_ref, came_ref, out_ref):
    for x in range(4):
        for y in range(4):
            came = came_ref[x, y].astype(F32)
            out_ref[x, y, 0:144] = (value_ref[x, y].astype(F32) + came[0:144]).astype(BF16)
            grad = grad_ref[x, y].astype(F32)
            out_ref[x, y, 144:288] = (grad[0:144] + came[144:288]).astype(BF16)
            out_ref[x, y, 288:304] = part(join(grad[144:160] + came[288:304]))


def add_four(in_ref, drop_ref, out_ref):
    drop = drop_ref[...]
    for y in range(4):
        value = in_ref[0, y].astype(F32)
        for x in range(1, 4):
            value = value + in_ref[x, y].astype(F32)
        rows = jnp.concatenate([value[0:288].astype(BF16), part(join(value[288:304]))], axis=0)
        write_messages(out_ref, dot_nn(drop, rows), (y,))


def combine(in_ref, place_ref, gate_ref, out_ref):
    value = read_messages(in_ref, range(4))
    stats = join(value[288:320])
    odd = (iota((32, 128), 0) & 1) == 1
    above = jnp.concatenate([stats[31:32], stats[0:31]], axis=0)
    stats = jnp.concatenate([jnp.where(odd, above, stats)] * (MSG // 2), axis=0)
    value = value.astype(BF16)
    row = iota((ROWS, 128), 0)
    lane = iota((ROWS, 128), 1)
    local = row_place(row)[1]
    forward = local < CAP
    place = place_ref[...].astype(F32)
    ahead_place = jnp.where(forward, place, 0.0)
    behind_place = jnp.where(forward, 0.0, place).astype(BF16)
    gate = jnp.where(forward, gate_ref[...], 0.0)
    out_ref[0:128] = dot_tn(value.astype(F32), gate, precision=HIGHEST)
    out_ref[128:256] = dot_tn(value, behind_place)
    for q in range(4):
        column = jnp.sum(jnp.where(lane == local + 16 * q, stats, 0.0), axis=1, keepdims=True)
        out_ref[256 + q : 257 + q] = jnp.sum(ahead_place * column, axis=0, keepdims=True)
    out_ref[260:264] = jnp.zeros((4, 128), F32)


def finish(
    core_ref, in_ref, stream_ref, side_ref, heads_ref, result_ref, grad_ref, pair_ref, gw_ref
):
    got = in_ref[0] + in_ref[1]
    stream = stream_ref[...]
    cot = side_ref[:, 2176:2304].astype(F32)
    gains = side_ref[:, 2304:2432].astype(F32)
    scaled = got[128:256] * (gains[:, 0:1] + gains[:, 1:2] + gains[:, 2:3])
    first = got[256:257] / WIDTH
    second = got[257:258] / WIDTH
    center = got[258:259] * 0.5
    inv_scale = got[259:260] * 0.5
    normal = (stream - center) * inv_scale
    grad = cot + inv_scale * (scaled - first - normal * second)
    result = stream + got[0:128]
    low = core_ref[0] == 0
    result_ref[...] = jnp.where(low, result[0:64], result[64:128]).astype(BF16)
    own = jnp.where(low, grad[0:64], grad[64:128]).astype(BF16)
    grad_ref[...] = own
    pair_ref[...] = grad.astype(BF16)
    product = dot_nt(own, heads_ref[...]).astype(BF16)
    for chip in range(16):
        gw_ref[chip] = product[:, chip * 128 : chip * 128 + 128]


def heads_back(at_ref, pair_ref, weight_ref, keep_ref, send_ref):
    for k in range(4):
        for j in range(4):
            chip = (at_ref[1] ^ ORDER_Y[j]) * 4 + (at_ref[0] ^ ORDER_X[k])
            out_ref = keep_ref if k < 2 else send_ref
            out_ref[k % 2, j] = dot_nn(weight_ref[chip], pair_ref[...]).astype(BF16)


def lay(in_ref, out_ref):
    for chip in range(16):
        out_ref[:, chip * 128 : chip * 128 + 128] = in_ref[chip]


def a2a(value, axes):
    return lax.all_to_all(value, axes, split_axis=0, concat_axis=0, tiled=True)


def halve(keep, send, axis, far):
    came = lax.ppermute(send, axis, [(i, i ^ 1) for i in range(4)])
    half = keep.astype(F32) + came.astype(F32)
    came = lax.ppermute(half[1].astype(BF16), axis, [(i, i ^ far) for i in range(4)])
    return half[0], came


def total(value):
    return jnp.sum(value.astype(F32), axis=0)


def local(
    residual, heads_out, out_weight, norm_gain, up_weight, down_weight, routes, gates, cotangent
):
    core = lax.axis_index("c").astype(jnp.int32).reshape(1)
    block = lax.axis_index(EXPERT).astype(jnp.int32).reshape(1)
    swap = [(0, 1), (1, 0)]
    heads_t = a2a(jnp.broadcast_to(heads_out.T, (16, 64, 128)), ("yl", "x"))
    wide = jnp.concatenate([out_weight.T, residual.T, cotangent.T], axis=1)
    small = jnp.concatenate(
        [routes.T.astype(F32), gates.T, jnp.pad(norm_gain, (0, 64)).reshape(1, 128)], axis=0
    )
    side, place, gate, pick, drop = call(
        prepare,
        (
            shape((64, SIDE), BF16),
            shape((ROWS, 128), BF16),
            shape((ROWS, 128), F32),
            shape((PACK, ROWS), BF16),
            shape((ROWS, PACK), BF16),
        ),
        "prepare",
        1,
        2,
    )(core, wide, small)
    side = lax.all_gather(side, "c", axis=0, tiled=True)
    turned = call(turn_weight, shape((16, 64, 128), BF16), "turn_weight", 1, 1)(core, side)
    at = jnp.stack([lax.axis_index("x"), lax.axis_index("yl")]).astype(jnp.int32)
    heads_t, turned, at = lax.optimization_barrier((heads_t, turned, at))
    heads_t = lax.all_gather(heads_t, "c", axis=0)
    stream, heads_t, message = call(
        dispatch,
        (
            shape((128, 128), F32),
            shape((WIDTH, 128), BF16),
            shape((BLOCKS, 4, 2, MSG * 64), BF16),
        ),
        "dispatch",
        1,
        4,
    )(block, heads_t, side, place, gate)
    message = a2a(message.reshape(64, 2, MSG * 64), ("yh", "z", "yl"))
    packed = call(repack, shape((4, 4, PACK, 128), BF16), "repack", 0, 2)(
        message.reshape(BLOCKS, 4, 2, MSG * 64), pick
    )
    mine = a2a(packed, "x")
    other = lax.ppermute(mine, "c", swap)
    value, pre, weigh, scalars = call(
        only_ahead,
        (
            shape((4, 4, SLOTS, 128), BF16),
            shape((SLOTS, HID), F32),
            shape((8, HID), F32),
            shape((SLOTS, 128), F32),
        ),
        "only_ahead",
        1,
        3,
    )(core, mine, up_weight, down_weight)
    sent = call(both_ways, shape((4, 4, PACK, 128), BF16), "both_ways", 1, 3)(
        1 - core, other, up_weight, down_weight
    )
    sent, pre = lax.optimization_barrier((sent, pre))
    came = lax.ppermute(sent, "c", swap)
    grad = call(only_behind, shape((4, 4, SLOTS + 16, 128), BF16), "only_behind", 1, 6)(
        core, mine, up_weight, down_weight, pre, weigh, scalars
    )
    summed = call(add_pair, shape((4, 4, PACK, 128), BF16), "add_pair", 0, 3)(value, grad, came)
    summed = a2a(summed, "x")
    message = call(add_four, shape((BLOCKS, 4, 2, MSG * 64), BF16), "add_four", 0, 2)(
        summed, drop
    )
    message = a2a(message.reshape(64, 2, MSG * 64), ("yh", "z", "yl"))
    both = call(combine, shape((264, 128), F32), "combine", 0, 3)(
        message.reshape(BLOCKS, 4, 2, MSG * 64), place, gate
    )
    both = lax.all_gather(both, "c", axis=0)
    result, grad_residual, grad_pair, grad_weight = call(
        finish,
        (
            shape((64, 128), BF16),
            shape((64, 128), BF16),
            shape((128, 128), BF16),
            shape((16, 64, 128), BF16),
        ),
        "finish",
        1,
        4,
    )(core, both, stream, side, heads_t)
    grad_weight = total(a2a(grad_weight, EXPERT)).astype(BF16)
    keep, send = call(heads_back, (shape((2, 4, 64, 128), BF16),) * 2, "heads_back", 1, 2)(
        at, grad_pair, turned
    )
    pieces = halve(keep, send, "x", 3)
    grad_weight = jnp.broadcast_to(grad_weight, (16, 64, 128))
    grad_weight = a2a(grad_weight, EXPERT)
    grad_weight = call(lay, shape((64, WIDTH), BF16), "lay", 0, 1)(grad_weight)
    heads_sum = (pieces[0] + pieces[1].astype(F32)).astype(BF16)
    pieces = halve(heads_sum[0:2], heads_sum[2:4], "yl", 2)
    grad_heads = (pieces[0] + pieces[1].astype(F32)).astype(BF16).T
    return (result.T, grad_residual.T, grad_heads, grad_weight.T)


def solution(mesh):
    view = Mesh(mesh.devices.reshape(SPLIT), AXES)
    return jax.shard_map(
        local,
        mesh=view,
        in_specs=(
            P(EXPERT, TENSOR),
            P(EXPERT, TENSOR),
            P(None, TENSOR),
            P(TENSOR),
            P(EXPERT, None, TENSOR),
            P(EXPERT, TENSOR, None),
            P(EXPERT, None),
            P(EXPERT, None),
            P(EXPERT, TENSOR),
        ),
        out_specs=(
            P(EXPERT, TENSOR),
            P(EXPERT, TENSOR),
            P(EXPERT, TENSOR),
            P(None, TENSOR),
        ),
        check_vma=False,
    )
```

```python
import jax
import jax.numpy as jnp
from jax import lax
from jax.experimental import pallas as pl
from jax.experimental.pallas import tpu as pltpu
from jax.sharding import Mesh, PartitionSpec as P

AXES = ("yh", "z", "yl", "x", "c")
EXPERT = ("yh", "z")
TENSOR = ("yl", "x", "c")
SPLIT = (2, 8, 4, 4, 2)
BLOCKS = 16
CAP = 9
MSG = 20
ORDER_X = (0, 3, 1, 2)
ORDER_Y = (0, 2, 1, 3)
PACK = 304
SLOTS = BLOCKS * CAP
SIDE = 2432
ROWS = BLOCKS * MSG
WIDTH = 2048
HID = 256
F32 = jnp.float32
BF16 = jnp.bfloat16
HIGHEST = lax.Precision.HIGHEST
ROOT = 0.7978845608028654
CUBIC = 0.044715


def iota(shape, axis):
    return lax.broadcasted_iota(jnp.int32, shape, axis)


def div(value, by):
    scale = -(-(1 << 14) // by)
    return lax.shift_right_logical(value * scale, 14)


def dot_nn(a, b, **kw):
    return lax.dot_general(a, b, (((1,), (0,)), ((), ())), preferred_element_type=F32, **kw)


def dot_nt(a, b, **kw):
    return lax.dot_general(a, b, (((1,), (1,)), ((), ())), preferred_element_type=F32, **kw)


def dot_tn(a, b, **kw):
    return lax.dot_general(a, b, (((0,), (0,)), ((), ())), preferred_element_type=F32, **kw)


def eye(n):
    return (iota((n, n), 0) == iota((n, n), 1)).astype(F32).astype(BF16)


def call(kernel, outs, name, n_smem, n_in):
    return pl.pallas_call(
        kernel,
        out_shape=outs,
        in_specs=[pl.BlockSpec(memory_space=pltpu.SMEM)] * n_smem
        + [pl.BlockSpec(memory_space=pltpu.VMEM)] * n_in,
        out_specs=jax.tree.map(lambda _: pl.BlockSpec(memory_space=pltpu.VMEM), outs),
        name=name,
        compiler_params=pltpu.CompilerParams(vmem_limit_bytes=16 * 1024 * 1024),
    )


def shape(dims, dtype):
    return jax.ShapeDtypeStruct(dims, dtype)


def split_three(value):
    high = value.astype(BF16)
    rest = value - high.astype(F32)
    middle = rest.astype(BF16)
    return high, middle, (rest - middle.astype(F32)).astype(BF16)


def split_two(value):
    high = value.astype(BF16)
    low = (value - high.astype(F32)).astype(BF16)
    return high, low


def join(block):
    return block + jnp.concatenate([block[:, 64:], block[:, :64]], axis=1)


def part(value):
    high, low = split_two(value)
    lane = iota(value.shape, 1)
    return jnp.where(lane < 64, high.astype(F32), low.astype(F32)).astype(BF16)


def row_place(row):
    pair = lax.shift_right_logical(row, 5)
    return lax.shift_right_logical(row & 31, 1), 2 * pair + (row & 1)


def write_messages(out_ref, value, ways):
    for i in range(MSG // 2):
        at = i * 32
        pair = value[at : at + 32].reshape(BLOCKS, 2, 128).astype(BF16)
        for y in ways:
            out_ref[:, y, :, i * 128 : i * 128 + 128] = pair


def read_messages(in_ref, ways):
    rows = []
    for i in range(MSG // 2):
        pair = None
        for y in ways:
            came = in_ref[:, y, :, i * 128 : i * 128 + 128].astype(F32)
            pair = came if pair is None else pair + came
        rows.append(pair.reshape(32, 128))
    return jnp.concatenate(rows, axis=0)


def prepare(
    core_ref, wide_ref, small_ref, side_ref, place_ref, gate_ref, pick_ref, drop_ref
):
    side_ref[:, 0:2304] = wide_ref[...]
    pick = iota((PACK, ROWS), 0) == packed_row(iota((8, ROWS), 1))[0:1]
    pick_ref[...] = jnp.where(pick, 1.0, 0.0).astype(BF16)
    drop = iota((ROWS, PACK), 1) == packed_row(iota((ROWS, 128), 0))[:, 0:1]
    drop_ref[...] = jnp.where(drop, 1.0, 0.0).astype(BF16)
    routes = small_ref[0:2].astype(jnp.int32)
    gates = small_ref[2:4]
    core = core_ref[0]
    row = iota((ROWS, 128), 0)
    group, local = row_place(row)
    slot = jnp.where(local < CAP, local, local - CAP)
    used = local < 2 * CAP
    expert = 2 * group + core
    first = (routes[0:1, :] == expert) & used
    second = (routes[1:2, :] == expert) & used
    named = jnp.where(first | second, 1.0, 0.0)
    before = (iota((128, 128), 0) < iota((128, 128), 1)).astype(F32).astype(BF16)
    earlier = dot_nn(named.astype(BF16), before)
    taken = (earlier == slot.astype(F32)) & (named > 0.5)
    place_ref[...] = jnp.where(taken, 1.0, 0.0).astype(BF16)
    gate = jnp.where(first, gates[0:1, :], gates[1:2, :])
    gate_ref[...] = jnp.where(taken, gate, 0.0)
    own = iota((64, 64), 0) == iota((64, 64), 1)
    gain = jnp.sum(jnp.where(own, small_ref[4:5, 0:64], 0.0), axis=1, keepdims=True)
    high, middle, low = split_three(jnp.broadcast_to(gain, (64, 128)))
    lane = iota((64, 128), 1)
    value = jnp.where(lane == 0, high.astype(F32), middle.astype(F32))
    side_ref[:, 2304:2432] = jnp.where(lane == 2, low.astype(F32), value).astype(BF16)


def turn_weight(core_ref, side_ref, out_ref):
    mirror = eye(128)
    for chip in range(16):
        turned = dot_nt(mirror, side_ref[:, chip * 128 : chip * 128 + 128])
        out_ref[chip] = jnp.where(core_ref[0] == 0, turned[0:64], turned[64:128]).astype(BF16)


def dispatch(block_ref, heads_ref, side_ref, place_ref, gate_ref, stream_ref, whole_ref, out_ref):
    pieces = []
    for chip in range(16):
        pieces.append(heads_ref[0, chip])
        pieces.append(heads_ref[1, chip])
    heads = jnp.concatenate(pieces, axis=0)
    whole_ref[...] = heads
    mixed = dot_nn(side_ref[:, 0:2048], heads)
    stream = side_ref[:, 2048:2176].astype(F32) + mixed
    stream_ref[...] = stream
    shift = jnp.mean(stream, axis=0, keepdims=True)
    centered = (stream - shift).astype(BF16)
    place = place_ref[...]
    placed = place.astype(F32)
    rows_x = dot_nt(place, centered)
    rows_c = dot_nt(place, side_ref[:, 2176:2304])
    gate_col = jnp.sum(gate_ref[...], axis=1, keepdims=True)
    shift_col = jnp.sum(placed * shift, axis=1, keepdims=True)
    row = iota((ROWS, 128), 0)
    lane = iota((ROWS, 128), 1)
    local = row_place(row)[1]
    high, low = split_two(shift_col)
    spread = jnp.where(lane == local, high.astype(F32), 0.0)
    spread = spread + jnp.where(lane == local + 16, low.astype(F32), 0.0)
    spread = jnp.where(local < CAP, spread, 0.0).astype(BF16)
    to_group, to_local = row_place(iota((ROWS, ROWS), 0))
    gather = (to_local == 18) & (to_group == row_place(iota((ROWS, ROWS), 1))[0])
    stats = dot_nn(jnp.where(gather, 1.0, 0.0).astype(BF16), spread)
    feature = iota((128, 128), 0)
    at = iota((128, 128), 1) - 32
    which = lax.shift_right_logical(jnp.maximum(at, 0), 3)
    mine = (at >= 0) & (at < 24) & (feature == 8 * block_ref[0] + (at & 7))
    gains = side_ref[:, 2304:2432].astype(F32)
    gain = jnp.where(which == 0, gains[:, 0:1], jnp.where(which == 1, gains[:, 1:2], gains[:, 2:3]))
    gain = jnp.sum(jnp.where(mine, gain, 0.0), axis=0, keepdims=True)
    value = jnp.where(local < CAP, rows_x, jnp.where(local < 2 * CAP, rows_c * gate_col, stats))
    value = jnp.where(local == 18, value + gain, value)
    write_messages(out_ref, value, range(4))


def packed_row(come):
    group, local = row_place(come)
    to = jnp.where(local < CAP, group * CAP + local, SLOTS + group * CAP + local - CAP)
    return jnp.where(local < 2 * CAP, to, jnp.where(local == 18, 2 * SLOTS + group, -1))


def repack(in_ref, pick_ref, out_ref):
    pick = pick_ref[...]
    for y in range(4):
        rows = [in_ref[:, y, :, i * 128 : i * 128 + 128] for i in range(MSG // 2)]
        rows = jnp.concatenate([pair.reshape(32, 128) for pair in rows], axis=0)
        packed = dot_nn(pick, rows).astype(BF16)
        for x in range(4):
            out_ref[x, y] = packed


def slot_tables():
    slot = iota((SLOTS, 128), 0)
    return slot - div(slot, CAP) * CAP, iota((SLOTS, 128), 1)


def read_rows(in_ref):
    local, lane = slot_tables()
    expand = (div(iota((SLOTS, 16), 0), CAP) == iota((SLOTS, 16), 1)).astype(F32).astype(BF16)
    shift_lane = (lane == local) | (lane == local + 16)
    at = iota((128, 128), 0) - 32
    collect = (at >= 0) & (at < 24) & ((at & 7) == (iota((128, 128), 1) & 7))
    collect = jnp.where(collect, 1.0, 0.0).astype(BF16)
    ones = jnp.ones((128, 128), BF16)
    own = lax.shift_right_logical(iota((16, 128), 1), 3) == iota((16, 128), 0)
    blocks = [in_ref[i % 4, i // 4, 288:304] for i in range(16)]
    shifts = dot_nn(expand, jnp.concatenate(blocks, axis=1))
    gain_rows = dot_nn(jnp.concatenate(blocks, axis=0), collect)
    chunks = []
    gains = []
    total = jnp.zeros((SLOTS, 128), F32)
    squares = jnp.zeros((SLOTS, 128), F32)
    for i in range(16):
        shift = jnp.where(shift_lane, shifts[:, i * 128 : i * 128 + 128], 0.0).astype(BF16)
        shift = dot_nn(shift, ones)
        base = shift if i == 0 else base
        chunk = in_ref[i % 4, i // 4, 0:144].astype(F32) + (shift - base)
        total = total + chunk
        squares = squares + chunk * chunk
        chunks.append(chunk)
        gain = jnp.where(own, gain_rows[i * 16 : i * 16 + 16], 0.0)
        gains.append(jnp.sum(gain, axis=0, keepdims=True))
    center = jnp.sum(total, axis=1, keepdims=True) / WIDTH
    variance = jnp.sum(squares, axis=1, keepdims=True) / WIDTH - center * center
    inv_scale = lax.rsqrt(variance + 1e-05)
    rows = []
    for i in range(16):
        rows.append(((chunks[i] - center) * inv_scale * gains[i]).astype(BF16))
    center = center + base[:, 0:1]
    return jnp.concatenate(rows, axis=1), jnp.concatenate(gains, axis=1), center, inv_scale


def ahead(in_ref, up, down):
    rows, gain, center, inv_scale = read_rows(in_ref)
    high, middle, low = split_three(jnp.broadcast_to(gain, (16, WIDTH)))
    row = iota((16, WIDTH), 0)
    gain = jnp.where(row == 0, high.astype(F32), middle.astype(F32))
    gain = jnp.where(row == 2, low.astype(F32), gain).astype(BF16)
    product = dot_nn(jnp.concatenate([rows, gain], axis=0), up)
    pre = product[0:SLOTS]
    weigh = product[SLOTS : SLOTS + 1] + product[SLOTS + 1 : SLOTS + 2]
    weigh = weigh + product[SLOTS + 2 : SLOTS + 3]
    bend = jnp.tanh(ROOT * (pre + CUBIC * pre * pre * pre))
    hidden = (0.5 * pre * (1.0 + bend)).astype(BF16)
    return pre, weigh, center, inv_scale, dot_nn(hidden, down).astype(BF16)


def behind(in_ref, up, down, pre, weigh, center, inv_scale):
    cots = [None] * 16
    for x in range(4):
        for y in range(4):
            cots[y * 4 + x] = in_ref[x, y, 144:288]
    grad_hidden = dot_nt(jnp.concatenate(cots, axis=1), down)
    bend = jnp.tanh(ROOT * (pre + CUBIC * pre * pre * pre))
    slope = 0.5 * (1.0 + bend) + 0.5 * pre * (1.0 - bend * bend) * (
        ROOT * (1.0 + 3.0 * CUBIC * pre * pre)
    )
    grad_act = (grad_hidden * slope).astype(BF16)
    wide = grad_act.astype(F32)
    sum_first = jnp.sum(wide * weigh, axis=1, keepdims=True)
    sum_second = jnp.sum(wide * pre, axis=1, keepdims=True)
    local, lane = slot_tables()
    spread = jnp.where(lane == local, sum_first, 0.0)
    spread = spread + jnp.where(lane == local + 16, sum_second, 0.0)
    spread = spread + jnp.where(lane == local + 32, center * (1.0 / 32), 0.0)
    spread = spread + jnp.where(lane == local + 48, inv_scale * (1.0 / 32), 0.0)
    high, low = split_two(spread)
    collect = (iota((16, SLOTS), 0) == div(iota((16, SLOTS), 1), CAP)).astype(F32).astype(BF16)
    high = dot_nn(collect, high)
    low = dot_nn(collect, low)
    stats = high + jnp.concatenate([low[:, 64:], low[:, :64]], axis=1)
    return dot_nt(grad_act, up).astype(BF16), stats.astype(BF16)


def both_ways(which_ref, in_ref, up_ref, down_ref, out_ref):
    up, down = up_ref[which_ref[0]], down_ref[which_ref[0]]
    pre, weigh, center, inv_scale, value = ahead(in_ref, up, down)
    grad_in, stats = behind(in_ref, up, down, pre, weigh, center, inv_scale)
    for x in range(4):
        for y in range(4):
            at = (y * 4 + x) * 128
            out_ref[x, y, 0:144] = value[:, at : at + 128]
            out_ref[x, y, 144:288] = grad_in[:, at : at + 128]
            out_ref[x, y, 288:304] = stats


def only_ahead(which_ref, in_ref, up_ref, down_ref, out_ref, pre_ref, weigh_ref, scalar_ref):
    up, down = up_ref[which_ref[0]], down_ref[which_ref[0]]
    pre, weigh, center, inv_scale, value = ahead(in_ref, up, down)
    pre_ref[...] = pre
    weigh_ref[...] = jnp.broadcast_to(weigh, (8, HID))
    lane = iota((SLOTS, 128), 1)
    scalar_ref[...] = jnp.where(lane == 0, center, inv_scale)
    for x in range(4):
        for y in range(4):
            at = (y * 4 + x) * 128
            out_ref[x, y] = value[:, at : at + 128]


def only_behind(
    which_ref, in_ref, up_ref, down_ref, pre_ref, weigh_ref, scalar_ref, out_ref
):
    up, down = up_ref[which_ref[0]], down_ref[which_ref[0]]
    center, inv_scale = scalar_ref[:, 0:1], scalar_ref[:, 1:2]
    grad_in, stats = behind(
        in_ref, up, down, pre_ref[...], weigh_ref[0:1], center, inv_scale
    )
    for x in range(4):
        for y in range(4):
            at = (y * 4 + x) * 128
            out_ref[x, y, 0:144] = grad_in[:, at : at + 128]
            out_ref[x, y, 144:160] = stats


def add_pair(value_ref, grad_ref, came_ref, out_ref):
    for x in range(4):
        for y in range(4):
            came = came_ref[x, y].astype(F32)
            out_ref[x, y, 0:144] = (value_ref[x, y].astype(F32) + came[0:144]).astype(BF16)
            grad = grad_ref[x, y].astype(F32)
            out_ref[x, y, 144:288] = (grad[0:144] + came[144:288]).astype(BF16)
            out_ref[x, y, 288:304] = part(join(grad[144:160] + came[288:304]))


def add_four(in_ref, drop_ref, out_ref):
    drop = drop_ref[...]
    for y in range(4):
        value = in_ref[0, y].astype(F32)
        for x in range(1, 4):
            value = value + in_ref[x, y].astype(F32)
        rows = jnp.concatenate([value[0:288].astype(BF16), part(join(value[288:304]))], axis=0)
        write_messages(out_ref, dot_nn(drop, rows), (y,))


def combine(in_ref, place_ref, gate_ref, out_ref):
    value = read_messages(in_ref, range(4))
    stats = join(value[288:320])
    odd = (iota((32, 128), 0) & 1) == 1
    above = jnp.concatenate([stats[31:32], stats[0:31]], axis=0)
    stats = jnp.concatenate([jnp.where(odd, above, stats)] * (MSG // 2), axis=0)
    value = value.astype(BF16)
    row = iota((ROWS, 128), 0)
    lane = iota((ROWS, 128), 1)
    local = row_place(row)[1]
    forward = local < CAP
    place = place_ref[...].astype(F32)
    ahead_place = jnp.where(forward, place, 0.0)
    behind_place = jnp.where(forward, 0.0, place).astype(BF16)
    gate = jnp.where(forward, gate_ref[...], 0.0)
    out_ref[0:128] = dot_tn(value.astype(F32), gate, precision=HIGHEST)
    out_ref[128:256] = dot_tn(value, behind_place)
    for q in range(4):
        column = jnp.sum(jnp.where(lane == local + 16 * q, stats, 0.0), axis=1, keepdims=True)
        out_ref[256 + q : 257 + q] = jnp.sum(ahead_place * column, axis=0, keepdims=True)
    out_ref[260:264] = jnp.zeros((4, 128), F32)


def finish(
    core_ref, in_ref, stream_ref, side_ref, heads_ref, result_ref, grad_ref, pair_ref, gw_ref
):
    got = in_ref[0] + in_ref[1]
    stream = stream_ref[...]
    cot = side_ref[:, 2176:2304].astype(F32)
    gains = side_ref[:, 2304:2432].astype(F32)
    scaled = got[128:256] * (gains[:, 0:1] + gains[:, 1:2] + gains[:, 2:3])
    first = got[256:257] / WIDTH
    second = got[257:258] / WIDTH
    center = got[258:259] * 0.5
    inv_scale = got[259:260] * 0.5
    normal = (stream - center) * inv_scale
    grad = cot + inv_scale * (scaled - first - normal * second)
    result = stream + got[0:128]
    low = core_ref[0] == 0
    result_ref[...] = jnp.where(low, result[0:64], result[64:128]).astype(BF16)
    own = jnp.where(low, grad[0:64], grad[64:128]).astype(BF16)
    grad_ref[...] = own
    pair_ref[...] = grad.astype(BF16)
    product = dot_nt(own, heads_ref[...]).astype(BF16)
    for chip in range(16):
        gw_ref[chip] = product[:, chip * 128 : chip * 128 + 128]


def heads_back(at_ref, pair_ref, weight_ref, keep_ref, send_ref):
    for k in range(4):
        for j in range(4):
            chip = (at_ref[1] ^ ORDER_Y[j]) * 4 + (at_ref[0] ^ ORDER_X[k])
            out_ref = keep_ref if k < 2 else send_ref
            out_ref[k % 2, j] = dot_nn(weight_ref[chip], pair_ref[...]).astype(BF16)


def lay(in_ref, out_ref):
    for chip in range(16):
        out_ref[:, chip * 128 : chip * 128 + 128] = in_ref[chip]


def a2a(value, axes):
    return lax.all_to_all(value, axes, split_axis=0, concat_axis=0, tiled=True)


def halve(keep, send, axis, far):
    came = lax.ppermute(send, axis, [(i, i ^ 1) for i in range(4)])
    half = keep.astype(F32) + came.astype(F32)
    came = lax.ppermute(half[1].astype(BF16), axis, [(i, i ^ far) for i in range(4)])
    return half[0], came


def total(value):
    return jnp.sum(value.astype(F32), axis=0)


def local(
    residual, heads_out, out_weight, norm_gain, up_weight, down_weight, routes, gates, cotangent
):
    core = lax.axis_index("c").astype(jnp.int32).reshape(1)
    block = lax.axis_index(EXPERT).astype(jnp.int32).reshape(1)
    swap = [(0, 1), (1, 0)]
    heads_t = a2a(jnp.broadcast_to(heads_out.T, (16, 64, 128)), ("yl", "x"))
    wide = jnp.concatenate([out_weight.T, residual.T, cotangent.T], axis=1)
    small = jnp.concatenate(
        [routes.T.astype(F32), gates.T, jnp.pad(norm_gain, (0, 64)).reshape(1, 128)], axis=0
    )
    side, place, gate, pick, drop = call(
        prepare,
        (
            shape((64, SIDE), BF16),
            shape((ROWS, 128), BF16),
            shape((ROWS, 128), F32),
            shape((PACK, ROWS), BF16),
            shape((ROWS, PACK), BF16),
        ),
        "prepare",
        1,
        2,
    )(core, wide, small)
    side = lax.all_gather(side, "c", axis=0, tiled=True)
    turned = call(turn_weight, shape((16, 64, 128), BF16), "turn_weight", 1, 1)(core, side)
    at = jnp.stack([lax.axis_index("x"), lax.axis_index("yl")]).astype(jnp.int32)
    heads_t, turned, at = lax.optimization_barrier((heads_t, turned, at))
    heads_t = lax.all_gather(heads_t, "c", axis=0)
    stream, heads_t, message = call(
        dispatch,
        (
            shape((128, 128), F32),
            shape((WIDTH, 128), BF16),
            shape((BLOCKS, 4, 2, MSG * 64), BF16),
        ),
        "dispatch",
        1,
        4,
    )(block, heads_t, side, place, gate)
    message = a2a(message.reshape(64, 2, MSG * 64), ("yh", "z", "yl"))
    packed = call(repack, shape((4, 4, PACK, 128), BF16), "repack", 0, 2)(
        message.reshape(BLOCKS, 4, 2, MSG * 64), pick
    )
    mine = a2a(packed, "x")
    other = lax.ppermute(mine, "c", swap)
    value, pre, weigh, scalars = call(
        only_ahead,
        (
            shape((4, 4, SLOTS, 128), BF16),
            shape((SLOTS, HID), F32),
            shape((8, HID), F32),
            shape((SLOTS, 128), F32),
        ),
        "only_ahead",
        1,
        3,
    )(core, mine, up_weight, down_weight)
    sent = call(both_ways, shape((4, 4, PACK, 128), BF16), "both_ways", 1, 3)(
        1 - core, other, up_weight, down_weight
    )
    sent, pre = lax.optimization_barrier((sent, pre))
    came = lax.ppermute(sent, "c", swap)
    grad = call(only_behind, shape((4, 4, SLOTS + 16, 128), BF16), "only_behind", 1, 6)(
        core, mine, up_weight, down_weight, pre, weigh, scalars
    )
    summed = call(add_pair, shape((4, 4, PACK, 128), BF16), "add_pair", 0, 3)(value, grad, came)
    summed = a2a(summed, "x")
    message = call(add_four, shape((BLOCKS, 4, 2, MSG * 64), BF16), "add_four", 0, 2)(
        summed, drop
    )
    message = a2a(message.reshape(64, 2, MSG * 64), ("yh", "z", "yl"))
    both = call(combine, shape((264, 128), F32), "combine", 0, 3)(
        message.reshape(BLOCKS, 4, 2, MSG * 64), place, gate
    )
    both = lax.all_gather(both, "c", axis=0)
    result, grad_residual, grad_pair, grad_weight = call(
        finish,
        (
            shape((64, 128), BF16),
            shape((64, 128), BF16),
            shape((128, 128), BF16),
            shape((16, 64, 128), BF16),
        ),
        "finish",
        1,
        4,
    )(core, both, stream, side, heads_t)
    grad_weight = total(a2a(grad_weight, EXPERT)).astype(BF16)
    keep, send = call(heads_back, (shape((2, 4, 64, 128), BF16),) * 2, "heads_back", 1, 2)(
        at, grad_pair, turned
    )
    pieces = halve(keep, send, "x", 3)
    grad_weight = jnp.broadcast_to(grad_weight, (16, 64, 128))
    grad_weight = a2a(grad_weight, EXPERT)
    grad_weight = call(lay, shape((64, WIDTH), BF16), "lay", 0, 1)(grad_weight)
    heads_sum = (pieces[0] + pieces[1].astype(F32)).astype(BF16)
    pieces = halve(heads_sum[0:2], heads_sum[2:4], "yl", 2)
    grad_heads = (pieces[0] + pieces[1].astype(F32)).astype(BF16).T
    return (result.T, grad_residual.T, grad_heads, grad_weight.T)


def solution(mesh):
    view = Mesh(mesh.devices.reshape(SPLIT), AXES)
    return jax.shard_map(
        local,
        mesh=view,
        in_specs=(
            P(EXPERT, TENSOR),
            P(EXPERT, TENSOR),
            P(None, TENSOR),
            P(TENSOR),
            P(EXPERT, None, TENSOR),
            P(EXPERT, TENSOR, None),
            P(EXPERT, None),
            P(EXPERT, None),
            P(EXPERT, TENSOR),
        ),
        out_specs=(
            P(EXPERT, TENSOR),
            P(EXPERT, TENSOR),
            P(EXPERT, TENSOR),
            P(None, TENSOR),
        ),
        check_vma=False,
    )
```
